32 devices in a mesh: dp: 16 (over z, x, core), fsdp: 2 (over y).
Axes of the slice: x: 2, y: 2, z: 4, core: 2. Of those that a mesh axis runs over, the one named last changes fastest.
Arguments:
- block_input: float32 [32768, 1024], P(('dp', 'fsdp')), may hold values from -6 to 6
- cotangent: float32 [32768, 1024], P(('dp', 'fsdp')), may hold values from -6 to 6
- scene_lengths: int32 [32, 3], P(('dp', 'fsdp')), may hold values from 1 to 480, 960 in all within a row
- norm_gain: float32 [1024], P(('dp', 'fsdp')), may hold values from 0.5 to 1.5
- in_weight: float32 [1024, 4384], P(('dp', 'fsdp')), may hold values from -0.1875 to 0.1875
- conv_weight: float32 [2304, 4], P(('dp', 'fsdp')), may hold values from -3 to 3
- conv_bias: float32 [2304], P(('dp', 'fsdp')), may hold values from -3 to 3
- dt_bias: float32 [32], replicated, may hold values from -7 to -2.3
- a_log: float32 [32], replicated, may hold values from 0 to 2.77
- skip_gain: float32 [32], replicated, may hold values from 0.5 to 1.5
- gated_gain: float32 [2048], P(('dp', 'fsdp')), may hold values from 0.5 to 1.5
- out_weight: float32 [2048, 1024], P(('dp', 'fsdp')), may hold values from -0.125 to 0.125
Outputs:
- block_output: float32 [32768, 1024], P(('dp', 'fsdp'))
- input_grad: float32 [32768, 1024], P(('dp', 'fsdp'))
- norm_gain_grad: float32 [1024], P(('dp', 'fsdp'))
- in_weight_grad: float32 [1024, 4384], P(('dp', 'fsdp'))
- conv_weight_grad: float32 [2304, 4], P(('dp', 'fsdp'))
- conv_bias_grad: float32 [2304], P(('dp', 'fsdp'))
- dt_bias_grad: float32 [32], replicated
- a_log_grad: float32 [32], replicated
- skip_gain_grad: float32 [32], replicated
- gated_gain_grad: float32 [2048], P(('dp', 'fsdp'))
- out_weight_grad: float32 [2048, 1024], P(('dp', 'fsdp'))
The draws below stay inside these ranges and needn't reach their ends.
Inputs may be any that keep to these rules, and one draw needn't show every extreme that they name: `scene_lengths`: each group's 3 lengths sum to 960 and the longest is exactly 480; the last 64 tokens of every group are padding.
All inputs are finite; a program needn't handle non-finite values.
Results may differ from the reference program's by a relative error of at most 0.012.
Values may be sent and summed in bfloat16 or wider, within the bound.
No kernel may reach another device: no remote copies, remote signals or barrier semaphores. Data moves between devices by JAX's collectives and lax.ppermute only.
A program may use at most 256 MiB of HBM per device.

```python
import math
import jax
import jax.numpy as jnp
import numpy as np
from jax import lax

D = 1024
HEADS = 32
KW = 4
SPAN = 256
SCENES = 3
TOK_DEV = 1024
INNER = 2048
XBC = 2304
PROJ = 4384
LIVE = 960
SCENE_MAX = 480
GROUPS = 32
TOKENS = 32768


def block_scale(key, shape, cuts, least, top_value):
    level, own = 1.0, jax.random.fold_in(key, 6)
    for position, shards_of in cuts:
        heights = jnp.exp(jax.random.uniform(jax.random.fold_in(own, position), (shards_of,), jnp.float32, least / len(cuts), top_value / len(cuts)))
        level = level * jnp.repeat(heights, shape[position] // shards_of).reshape([-1 if axis == position else 1 for axis in range(len(shape))])
    return level


def profile(count, total, most, slope):
    portions = [(1 << 20) // math.isqrt(standing ** slope) + 1 for standing in range(2, count + 1)]
    rest, counts = total - most - (count - 1), [1] * (count - 1)
    while rest > 0:
        free = [i for i in range(count - 1) if counts[i] < most]
        pool, left = sum([portions[i] for i in free]), rest
        for i in free:
            addition = min(most - counts[i], max(1, left * portions[i] // pool), rest)
            counts[i] = counts[i] + addition
            rest = rest - addition
    return np.array([most] + counts)


def ragged(own_key, amount, total, most, skew):
    if amount == 2:
        one = jax.random.randint(own_key, (), max(1, total - most), min(most, total - 1) + 1)
        return jnp.stack([one, total - one])
    tallies = jnp.asarray(profile(amount, total, most, skew), jnp.int32)
    twos = (amount - 1) // 2
    giver, receiver = tallies[1:1 + 2 * twos:2], tallies[2:2 + 2 * twos:2]
    slack = jnp.minimum(giver - 1, most - receiver)
    passed = jax.random.randint(jax.random.fold_in(own_key, 1), (twos,), 0, 1 << 20) % (slack + 1)
    tallies = tallies.at[1:1 + 2 * twos:2].set(giver - passed).at[2:2 + 2 * twos:2].set(receiver + passed)
    return tallies[jax.random.permutation(jax.random.fold_in(own_key, 2), amount)]


def centred(rng, dims, scale, limit, cuts=(), dtype=jnp.bfloat16):
    loudness = block_scale(rng, dims, cuts, -0.22, 0.18) if cuts else 1.0
    drawn = jax.random.normal(rng, dims, jnp.float32) * scale * loudness
    return jnp.minimum(jnp.maximum(drawn, -limit), limit).astype(dtype)


def setup_inputs(seed: int = 0) -> dict:
    splits = jax.random.split(jax.random.key(seed), 13)
    return {
        "block_input": centred(splits[0], (TOKENS, D), 1.0, 6.0, ((0, 32),), jnp.float32),
        "cotangent": centred(splits[1], (TOKENS, D), 1.0, 6.0, ((0, 32),), jnp.float32),
        "scene_lengths": jax.vmap(lambda own: ragged(own, SCENES, LIVE, SCENE_MAX, 2))(jax.random.split(splits[2], GROUPS)).reshape((GROUPS, SCENES)).astype(jnp.int32),
        "norm_gain": jnp.clip(1.0 + 0.1 * jax.random.normal(splits[3], (D,), jnp.float32), 0.5, 1.5),
        "in_weight": centred(splits[4], (D, PROJ), D ** -0.5, 0.1875, ((0, 32),), jnp.float32),
        "conv_weight": centred(splits[5], (XBC, KW), KW ** -0.5, 3.0, ((0, 32),), jnp.float32),
        "conv_bias": centred(splits[6], (XBC,), 0.5, 3.0, ((0, 32),), jnp.float32),
        "dt_bias": jnp.clip(jax.random.uniform(splits[7], (HEADS,), jnp.float32, -7.0, -2.3), -7.0, -2.3),
        "a_log": jnp.clip(jax.random.uniform(splits[8], (HEADS,), jnp.float32, 0.0, 2.77), 0.0, 2.77),
        "skip_gain": jnp.clip(jax.random.uniform(splits[9], (HEADS,), jnp.float32, 0.5, 1.5), 0.5, 1.5),
        "gated_gain": jnp.clip(1.0 + 0.1 * jax.random.normal(splits[10], (INNER,), jnp.float32), 0.5, 1.5),
        "out_weight": centred(splits[11], (INNER, D), INNER ** -0.5, 0.125, ((0, 32),), jnp.float32),
    }


epsilon = 1e-05
highest = lax.Precision.HIGHEST

@jax.custom_vjp
def low(v):
    return lax.optimization_barrier(v.astype(jnp.bfloat16)).astype(jnp.float32)

@jax.custom_vjp
def low_back(v):
    return v

def low_keep(v):
    return (low(v), None)

def low_pass(kept, grad):
    return (grad,)

def back_keep(v):
    return (v, None)

def back_low(kept, grad):
    return (low(grad),)
low.defvjp(low_keep, low_pass)
low_back.defvjp(back_keep, back_low)

def rms_scale(matrix, gain):
    return matrix * lax.rsqrt(lax.optimization_barrier(jnp.mean(matrix * matrix, axis=-1, keepdims=True)) + epsilon) * gain

def scene_ids(lengths_row, token_count):
    bounds = jnp.cumsum(lengths_row).astype(jnp.int32)
    places = lax.iota(jnp.int32, token_count)
    scene = lax.optimization_barrier(jnp.sum((places[:, None] >= bounds[None, :]).astype(jnp.int32), axis=1)).astype(jnp.int32)
    alive = (places < bounds[-1]).astype(jnp.float32)
    return (scene, alive)

def mixer(projected, conv_weight, conv_bias, dt_bias, a_log, skip_gain, gated_gain, scene, alive):
    token_count = projected.shape[0]
    inner_width = gated_gain.shape[0]
    channels = conv_bias.shape[0]
    head_count = a_log.shape[0]
    state_width = (channels - inner_width) // 2
    head_dim = inner_width // head_count
    kernel = conv_weight.shape[1]
    gate_part = projected[:, :inner_width]
    conv_in = projected[:, inner_width:inner_width + channels]
    step_raw = projected[:, inner_width + channels:]
    conv_sum = conv_bias + conv_in * conv_weight[:, kernel - 1]
    for offset in range(1, kernel):
        shifted = jnp.pad(conv_in, ((offset, 0), (0, 0)))[:token_count]
        shifted_scene = jnp.pad(scene, (offset, 0), constant_values=-1)[:token_count]
        same_scene = (shifted_scene == scene).astype(jnp.float32)
        conv_sum = conv_sum + shifted * same_scene[:, None] * conv_weight[:, kernel - 1 - offset]
    activated = jax.nn.silu(conv_sum)
    values = activated[:, :inner_width].reshape(token_count, head_count, head_dim)
    b_in = activated[:, inner_width:inner_width + state_width]
    c_out = activated[:, inner_width + state_width:]
    dt_step = jax.nn.softplus(step_raw + dt_bias)
    log_decay = -dt_step * jnp.exp(a_log)
    block_count = token_count // SPAN
    blocked = (values.reshape(block_count, SPAN, head_count, head_dim), b_in.reshape(block_count, SPAN, state_width), c_out.reshape(block_count, SPAN, state_width), dt_step.reshape(block_count, SPAN, head_count), log_decay.reshape(block_count, SPAN, head_count), scene.reshape(block_count, SPAN))

    def one_block(carry, block):
        held_state, prior_scene = carry
        block_values, block_b, block_c, block_step, block_decay, block_scene = block
        cum_decay = jnp.cumsum(block_decay, axis=0)
        within = lax.iota(jnp.int32, SPAN)
        causal = ((within[:, None] >= within[None, :]) & (block_scene[:, None] == block_scene[None, :])).astype(jnp.float32)
        spread = cum_decay[:, None, :] - cum_decay[None, :, :]
        weights = jnp.exp(jnp.minimum(spread, 0.0)) * causal[:, :, None]
        intersection = jnp.dot(block_c, block_b.T, precision=highest, preferred_element_type=jnp.float32)
        scores = weights * intersection[:, :, None] * block_step[None, :, :]
        inside = jnp.einsum('tsh,shp->thp', scores, block_values, precision=highest)
        entering = (block_scene == prior_scene).astype(jnp.float32)
        carried = jnp.einsum('tn,hpn->thp', block_c, held_state, precision=highest) * (jnp.exp(cum_decay) * entering[:, None])[:, :, None]
        final_scene = block_scene[SPAN - 1]
        end_weight = jnp.exp(cum_decay[SPAN - 1][None, :] - cum_decay) * (block_scene == final_scene).astype(jnp.float32)[:, None] * block_step
        fresh_state = jnp.einsum('shp,sn->hpn', end_weight[:, :, None] * block_values, block_b, precision=highest)
        through = jnp.exp(cum_decay[SPAN - 1]) * (final_scene == prior_scene).astype(jnp.float32)
        held_state = held_state * through[:, None, None] + fresh_state
        return ((held_state, final_scene), inside + carried)
    initial = (jnp.zeros((head_count, head_dim, state_width), jnp.float32), jnp.array(-1, jnp.int32))
    _, outputs = lax.scan(one_block, initial, blocked)
    scan_out = outputs.reshape(token_count, head_count, head_dim) + skip_gain[None, :, None] * values
    gated = scan_out.reshape(token_count, inner_width) * jax.nn.silu(gate_part) * alive[:, None]
    return rms_scale(gated, gated_gain)

def reference(block_input, cotangent, scene_lengths, norm_gain, in_weight, conv_weight, conv_bias, dt_bias, a_log, skip_gain, gated_gain, out_weight):
    grouped = block_input.reshape(GROUPS, TOK_DEV, D)

    def forward(group_input, gain_arg, inproj_arg, conv_arg, convbias_arg, dtbias_arg, alog_arg, skip_arg, gated_arg, outproj_arg):
        gain_low = low(gain_arg)
        inproj_low = low(inproj_arg)
        conv_low = low(conv_arg)
        convbias_low = low(convbias_arg)
        gated_low = low(gated_arg)
        outproj_low = low(outproj_arg)

        def group_block(pieces):
            group_rows, lengths_row = pieces
            scene, alive = scene_ids(lengths_row, TOK_DEV)
            normed = low(rms_scale(group_rows, gain_low))
            projected = low_back(jnp.dot(normed, inproj_low, precision=highest, preferred_element_type=jnp.float32))
            mixed = low(mixer(projected, conv_low, convbias_low, dtbias_arg, alog_arg, skip_arg, gated_low, scene, alive))
            branch = low_back(jnp.dot(mixed, outproj_low, precision=highest, preferred_element_type=jnp.float32))
            return group_rows + branch
        return lax.map(jax.checkpoint(group_block), (group_input, scene_lengths))
    outputs, pullback = jax.vjp(forward, grouped, norm_gain, in_weight, conv_weight, conv_bias, dt_bias, a_log, skip_gain, gated_gain, out_weight)
    grads = pullback(cotangent.reshape(GROUPS, TOK_DEV, D))
    return (outputs.reshape(TOKENS, D), grads[0].reshape(TOKENS, D), grads[1], grads[2], grads[3], grads[4], grads[5], grads[6], grads[7], grads[8], grads[9])
```

```python
import functools

import jax
import jax.numpy as jnp
from jax import lax
from jax.experimental import pallas as pl
from jax.experimental.pallas import tpu as pltpu
from jax.sharding import PartitionSpec as P

AXES = ("chip", "core", "fsdp")
CHIPS = ("chip", "fsdp")
SHARDS = 32
PIECES = tuple(c | y | x for c in (0, 2) for y in (0, 1) for x in (0, 4))
BLOCK = 128
GROUP = 256
EPS = 1e-05
LOG2E = 1.4426950408889634
VMEM_LIMIT = 60 * 1024 * 1024
f32 = jnp.float32
bf16 = jnp.bfloat16
highest = lax.Precision.HIGHEST


def dot(a, b):
    return jnp.dot(a, b, preferred_element_type=f32)


def dot_nt(a, b):
    return lax.dot_general(a, b, (((1,), (1,)), ((), ())), preferred_element_type=f32)


def dot_tn(a, b):
    return lax.dot_general(a, b, (((0,), (0,)), ((), ())), preferred_element_type=f32)


def sigmoid(v):
    return 0.5 * jnp.tanh(0.5 * v) + 0.5


def iota(shape, axis):
    return lax.broadcasted_iota(jnp.int32, shape, axis)


def rows8(v):
    return jnp.sum(v.reshape(v.shape[0] // 8, 8, v.shape[1]), axis=0)


def scene_of(place, sm):
    scene = jnp.zeros(place.shape, jnp.int32)
    for i in range(3):
        scene = scene + jnp.where(place >= sm[i], 1, 0)
    return scene


def call(kernel, out, grid=None, in_specs=None, out_specs=None, scratch=(), name=None, flops=0, size=0):
    return pl.pallas_call(
        kernel,
        out_shape=out,
        grid=grid or (1,),
        in_specs=in_specs,
        out_specs=out_specs,
        scratch_shapes=scratch,
        name=name,
        compiler_params=pltpu.CompilerParams(
            vmem_limit_bytes=VMEM_LIMIT, dimension_semantics=("arbitrary",)
        ),
        cost_estimate=pl.CostEstimate(flops=int(flops), bytes_accessed=int(size), transcendentals=0),
    )


def whole(shape):
    return pl.BlockSpec(shape, lambda g: (0,) * len(shape))


SMEM = pl.BlockSpec(memory_space=pltpu.SMEM)


def struct(shape, dtype=f32):
    return jax.ShapeDtypeStruct(shape, dtype)


def conv_block(window, masks, taps, width):
    current = window[8:]
    total = taps[4:5] + current * taps[3:4]
    shifted = [current]
    for off in range(1, width):
        moved = window[8 - off : 8 - off + BLOCK] * masks[:, off - 1 : off]
        shifted.append(moved)
        total = total + moved * taps[width - 1 - off : width - off]
    return total, shifted


def conv_back(window, masks, taps, width):
    total = window[:BLOCK] * taps[width - 1 : width]
    for off in range(1, width):
        moved = pltpu.roll(window * masks[:, off - 1 : off], window.shape[0] - off, 0)[:BLOCK]
        total = total + moved * taps[width - 1 - off : width - off]
    return total


def unpack_kernel(sm, *refs):
    pieces, (skip_ref, w_ref, taps_ref, gain_ref) = refs[: len(PIECES)], refs[len(PIECES) :]
    assemble(sm, pieces, w_ref, 32)
    row, col = iota((8 * SHARDS, 32 * SHARDS), 0), iota((8 * SHARDS, 32 * SHARDS), 1)
    pick = jnp.where(col == (row & (SHARDS - 1)) * 32 + row // SHARDS, 1.0, 0.0).astype(bf16)
    packed = dot(pick, w_ref[:, 256:384]).astype(bf16)

    def spread(kind, lane, size):
        total = size * SHARDS
        place = iota((1, total), 1)
        owner, within = place // size, place % size
        copy = jnp.where(iota((128, total), 0) == within + lane, 1.0, 0.0).astype(bf16)
        values = dot(packed[kind * SHARDS : (kind + 1) * SHARDS, :], copy)
        return jnp.sum(jnp.where(iota((SHARDS, total), 0) == owner, values, 0.0), axis=0, keepdims=True)

    taps_ref[...] = jnp.zeros(taps_ref.shape, f32)
    gain_ref[...] = jnp.broadcast_to(spread(0, 32, 32), gain_ref.shape)
    inner = skip_ref.shape[1]
    taps_ref[6:7, :inner] = spread(0, 64, inner // SHARDS)
    channels = taps_ref.shape[1]
    for k in range(5):
        taps_ref[k : k + 1, :] = spread(k + 1, 32, channels // SHARDS)
    taps_ref[5:6, :inner] = skip_ref[0:1, :]


def unpack(sm, pieces, skip, channels, width):
    outs = [struct((width, 384), bf16), struct((8, channels)), struct((8, width))]
    return call(
        unpack_kernel,
        outs,
        in_specs=[SMEM] + [whole(a.shape) for a in (*pieces, skip)],
        out_specs=[whole(o.shape) for o in outs],
        name="unpack",
        size=2e6,
    )(sm, *pieces, skip)


def core_first(shard):
    return (shard >> 1 & 1) * 16 + (shard >> 2) * 2 + (shard & 1)


def prep_kernel(
    ring, sm, x_ref, gain_ref, w_ref, taps_ref, head_ref,
    normed_ref, normt_ref, cin_ref, b_ref, c_ref, bt_ref, ct_ref, s_ref, st_ref,
    cum_ref, cumt_ref, ea_ref, eb_ref, step_ref, mask_ref, cs_scr,
):
    tokens = x_ref.shape[0]
    x = x_ref[...]
    scale = lax.rsqrt(jnp.mean(x * x, axis=-1, keepdims=True) + EPS)
    normed_low = (x * scale * gain_ref[0:1, :]).astype(bf16)
    normed_ref[...] = normed_low
    flipped = normed_low.astype(f32).T.astype(bf16)
    if ring:
        for shard in range(SHARDS):
            at = core_first(shard) * 32
            normt_ref[at : at + 32, :] = flipped[shard * 32 : shard * 32 + 32, :]
    else:
        normt_ref[...] = flipped
    proj = dot(normed_low, w_ref[...])
    lanes = iota((1, 128), 1)
    heads = cumt_ref.shape[0]
    is_head = lanes < heads
    cin_low = proj[:, :256].astype(bf16)
    cin_ref[...] = cin_low
    cs_scr[0:8, :] = jnp.zeros((8, 256), f32)
    cs_scr[pl.ds(8, tokens), :] = cin_low.astype(f32)
    step_ref[...] = jnp.where(is_head, proj[:, 256:384] + head_ref[0:1, :], 0.0)
    taps = taps_ref[...]

    def block(k, _):
        t0 = pl.multiple_of(k * BLOCK, BLOCK)
        rows = pl.ds(t0, BLOCK)
        place = iota((BLOCK, 128), 0) + t0
        lane = iota((BLOCK, 128), 1)
        scene = scene_of(place, sm)
        before = place - lane - 1
        same = (before >= 0) & (scene_of(before, sm) == scene)
        mask = jnp.where(lane < 3, jnp.where(same, 1.0, 0.0), jnp.where(place < sm[2], 1.0, 0.0))
        mask_ref[rows, :] = mask
        conv, _ = conv_block(cs_scr[pl.ds(t0, BLOCK + 8), :], mask, taps, 4)
        act = conv * sigmoid(conv)
        b_low = act[:, :128].astype(bf16)
        c_low = act[:, 128:].astype(bf16)
        b_ref[rows, :] = b_low
        c_ref[rows, :] = c_low
        bt_ref[:, rows] = act[:, :128].T.astype(bf16)
        ct_ref[:, rows] = act[:, 128:].T.astype(bf16)
        other = scene_of(lane + t0, sm)
        low = (lane + t0 <= place) & (other == scene)
        s_ref[rows, :] = jnp.where(low, dot_nt(c_low, b_low), 0.0)
        high = (lane + t0 >= place) & (other == scene)
        st_ref[rows, :] = jnp.where(high, dot_nt(b_low, c_low), 0.0)
        step = step_ref[rows, :]
        dt = jnp.maximum(step, 0.0) + jnp.log1p(jnp.exp(-jnp.abs(step)))
        dt = jnp.where(is_head, dt, 0.0)
        log_decay = dt * (head_ref[1:2, :] * -LOG2E)
        lower = jnp.where(lane <= iota((BLOCK, 128), 0), 1.0, 0.0)
        cum = jnp.dot(lower, log_decay, precision=highest, preferred_element_type=f32)
        cum_ref[rows, :] = cum
        cumt_ref[:, rows] = cum.T[:heads, :]
        first = jnp.full((1, 128), t0 - 1, jnp.int32)
        last = jnp.full((1, 128), t0 + BLOCK - 1, jnp.int32)
        entering = (scene_of(first, sm) == scene) & (first >= 0) & is_head
        final = (scene_of(last, sm) == scene) & is_head
        grow = jnp.where(entering, jnp.exp2(cum), 0.0)
        end = jnp.where(final, jnp.exp2(cum[BLOCK - 1 :] - cum), 0.0)

        def packed(v):
            hi = v.astype(bf16).astype(f32)
            return hi + pltpu.roll((v - hi).astype(bf16).astype(f32), 32, 1)

        ea_ref[rows, :] = (packed(dt) + pltpu.roll(packed(grow), 64, 1)).astype(bf16)
        eb_ref[rows, :] = packed(end).astype(bf16)
        return 0

    mask_ref[pl.ds(tokens, 8), :] = jnp.zeros((8, 128), f32)
    lax.fori_loop(0, tokens // BLOCK, block, 0)


def prep(ring, sm, x, gain, w_bc, taps, head, heads):
    tokens, width = x.shape
    wide = (tokens, 128)
    outs = [
        struct(x.shape, bf16), struct((width, tokens), bf16), struct((tokens, 256), bf16),
        struct(wide, bf16), struct(wide, bf16), struct((128, tokens), bf16), struct((128, tokens), bf16),
        struct(wide), struct(wide), struct(wide), struct((heads, tokens)), struct(wide, bf16), struct(wide, bf16),
        struct(wide), struct((tokens + 8, 128)),
    ]
    args = (x, gain, w_bc, taps, head)
    return call(
        functools.partial(prep_kernel, ring),
        outs,
        in_specs=[SMEM] + [whole(a.shape) for a in args],
        out_specs=[whole(o.shape) for o in outs],
        scratch=[pltpu.VMEM((tokens + 8, 256), f32)],
        name="prep",
        flops=2 * tokens * width * 384,
        size=12e6,
    )(sm, *args)


def fill_spread(e_scr, group):
    row = iota((128, 768), 0)
    col = iota((128, 768), 1)
    head = 4 * group + (col % GROUP) // 64
    part = jnp.where(col < GROUP, 0, jnp.where(col < 2 * GROUP, 64, 0))
    hit = (row == head + part) | (row == head + part + 32)
    e_scr[...] = jnp.where(hit, 1.0, 0.0).astype(bf16)


def pair_masks():
    low = jnp.where(iota((1, 128), 1) < 64, 1.0, 0.0).astype(bf16)
    high = jnp.where(iota((1, 128), 1) < 64, 0.0, 1.0).astype(bf16)
    return low, high


def assemble(sm, pieces, out_ref, block):
    for i, piece in enumerate(pieces):
        for j in range(4):
            shard = sm[3] ^ (PIECES[i] | j << 3)
            out_ref[pl.ds(pl.multiple_of(shard * block, block), block), :] = piece[j * block : (j + 1) * block, :]


def fwd_kernel(*refs):
    base, ring, sm = refs[:3]
    if ring:
        n = len(PIECES)
        gates, values = refs[3 : 3 + n], refs[3 + n : 3 + 2 * n]
        rest = list(refs[3 + 2 * n :])
        wv_ref, wg_ref = rest.pop(15), rest.pop(14)
        assemble(sm, gates, wg_ref, 32)
        assemble(sm, values, wv_ref, 32)
        rest[1:1] = [wg_ref, wv_ref]
    else:
        rest = list(refs[5:])
        rest[1:1] = refs[3:5]
    fwd_body(base, *rest)


def fwd_body(
    base, normed_ref, wg_ref, wv_ref, taps_ref, ea_ref, eb_ref, cum_ref, cumt_ref, c_ref, bt_ref, s_ref, mask_ref,
    z_ref, cin_ref, y_ref, h_ref, cs_scr, e_scr, h_scr,
):
    group = pl.program_id(0) + base
    tokens = normed_ref.shape[0]
    normed = normed_ref[...]
    z_ref[...] = dot(normed, wg_ref[...]).astype(bf16)
    cin_low = dot(normed, wv_ref[...]).astype(bf16)
    cin_ref[...] = cin_low
    cs_scr[0:8, :] = jnp.zeros((8, GROUP), f32)
    cs_scr[pl.ds(8, tokens), :] = cin_low.astype(f32)
    fill_spread(e_scr, group)
    h_scr[...] = jnp.zeros(h_scr.shape, f32)
    taps = taps_ref[...]
    m_low, m_high = pair_masks()

    def block(k, _):
        t0 = pl.multiple_of(k * BLOCK, BLOCK)
        rows = pl.ds(t0, BLOCK)
        mask = mask_ref[rows, :]
        conv, _ = conv_block(cs_scr[pl.ds(t0, BLOCK + 8), :], mask, taps, 4)
        v = conv * sigmoid(conv)
        ea = dot(ea_ref[rows, :], e_scr[:, : 2 * GROUP])
        wx = dot(eb_ref[rows, :], e_scr[:, 2 * GROUP :])
        dtx, ex = ea[:, :GROUP], ea[:, GROUP:]
        vd_low = (v * dtx).astype(bf16)
        h_old = h_scr[...]
        h_low = h_old.astype(bf16)
        h_ref[rows, :] = h_low
        carried = dot(c_ref[rows, :], h_low) * ex
        cums = pltpu.roll(cum_ref[rows, :], 128 - 4 * group, 1)
        s = s_ref[rows, :]
        inside = []
        for pair in range(2):
            weights = []
            for j in (2 * pair, 2 * pair + 1):
                spread = cums[:, j : j + 1] - cumt_ref[0, j : j + 1, rows]
                weights.append((jnp.exp2(jnp.minimum(spread, 0.0)) * s).astype(bf16))
            vp = vd_low[:, pair * 128 : pair * 128 + 128]
            stack = jnp.concatenate([vp * m_low, vp * m_high], axis=0)
            inside.append(dot(jnp.concatenate(weights, axis=1), stack))
        y_ref[rows, :] = jnp.concatenate(inside, axis=1) + carried + taps[5:6] * v
        fresh = dot(bt_ref[:, rows], (vd_low.astype(f32) * wx).astype(bf16))
        h_scr[...] = h_old * ex[BLOCK - 1 :] + fresh
        return 0

    lax.fori_loop(0, tokens // BLOCK, block, 0)


def fwd(base, count, ring, sm, normed, gates, values, inner, taps, pre):
    tokens, width = normed.shape
    full = lambda a: whole(a.shape)
    ea, eb, cum, cumt, c, bt, s, mask = pre
    first = inner // GROUP
    col = lambda rows, dtype: struct((rows, count * GROUP), dtype)
    block = lambda rows: pl.BlockSpec((rows, GROUP), lambda g: (0, g))
    outs = [col(tokens, bf16), col(tokens, bf16), col(tokens, f32), col(tokens, bf16)]
    if ring:
        w_specs = [block(a.shape[0]) for a in (*gates, *values)]
        outs += [col(width, bf16)] * 2
    else:
        w_specs = [
            pl.BlockSpec((width, GROUP), lambda g: (0, base + g)),
            pl.BlockSpec((width, GROUP), lambda g: (0, first + base + g)),
        ]
    return call(
        functools.partial(fwd_kernel, base, ring),
        outs,
        grid=(count,),
        in_specs=[SMEM] + w_specs + [
            full(normed),
            pl.BlockSpec((8, GROUP), lambda g: (0, base + g)),
            full(ea), full(eb), full(cum),
            pl.BlockSpec((1, 4, tokens), lambda g: (base + g, 0, 0)),
            full(c), full(bt), full(s), full(mask),
        ],
        out_specs=[block(o.shape[0]) for o in outs],
        scratch=[pltpu.VMEM((tokens + 8, GROUP), f32), pltpu.VMEM((128, 3 * GROUP), bf16), pltpu.VMEM((128, GROUP), f32)],
        name=f"fwd{base}",
        flops=count * 2 * tokens * width * 2 * GROUP * 3,
        size=count * 4e6,
    )(sm, *gates, *values, normed, taps, ea, eb, cum, cumt, c, bt, s, mask)


MID = 256
MID_C = 512


def mid_kernel(ring, chunks, sm, cot_ref, w_ref, taps_ref, mask_ref, *refs):
    zs, ys = refs[:chunks], refs[chunks : 2 * chunks]
    mixed_ref, dz_ref, dy_ref, gg_ref, *terms = refs[2 * chunks : -3]
    g_scr, u_scr, acc_scr = refs[-3:]
    step = pl.program_id(0)
    inner = dz_ref.shape[1]
    wide = inner // chunks
    alive = mask_ref[:, 3:4]
    cot_low = cot_ref[...].astype(bf16)
    square = jnp.zeros((MID, 128), f32)
    parts = [slice(i, i + MID_C) for i in range(0, inner, MID_C)]
    here = [(zs[p.start // wide], ys[p.start // wide], slice(p.start % wide, p.start % wide + MID_C)) for p in parts]
    for part, (z_ref, y_ref, cut) in zip(parts, here):
        z = z_ref[:, cut].astype(f32)
        g = y_ref[:, cut] * (z * sigmoid(z)) * alive
        g_scr[:, part] = g
        sq = g * g
        for i in range(0, MID_C, 128):
            square = square + sq[:, i : i + 128]
    r = lax.rsqrt(jnp.sum(square, axis=-1, keepdims=True) * (1.0 / inner) + EPS)
    cross = jnp.zeros((MID, 128), f32)
    for part in parts:
        gain = taps_ref[6:7, part]
        dm = dot_nt(cot_low, w_ref[part, :])
        g = g_scr[:, part]
        u = dm * gain
        u_scr[:, part] = u
        ug = u * g
        for i in range(0, MID_C, 128):
            cross = cross + ug[:, i : i + 128]
        gr = g * r
        mixed_ref[:, part] = (gr * gain).astype(bf16)
        gg = rows8(dm * gr)

        @pl.when(step == 0)
        def _():
            gg_ref[:, part] = gg

        @pl.when(step > 0)
        def _():
            gg_ref[:, part] += gg

    r3 = r * r * r * (jnp.sum(cross, axis=-1, keepdims=True) * (1.0 / inner))
    for part in parts:
        term = dot_tn(mixed_ref[:, part], cot_low)

        @pl.when(step == 0)
        def _():
            acc_scr[part, :] = term

        @pl.when(step > 0)
        def _():
            acc_scr[part, :] += term

    for part, (z_ref, y_ref, cut) in zip(parts, here):
        z = z_ref[:, cut].astype(f32)
        sig = sigmoid(z)
        dg = (u_scr[:, part] * r - g_scr[:, part] * r3) * alive
        dy_ref[:, part] = (dg * (z * sig)).astype(bf16)
        dz_ref[:, part] = (dg * y_ref[:, cut] * (sig * (1.0 + z * (1.0 - sig)))).astype(bf16)

    @pl.when(step == pl.num_programs(0) - 1)
    def _():
        if not ring:
            terms[0][...] = acc_scr[...].astype(bf16)
            return
        width = acc_scr.shape[1]
        for shard in range(SHARDS):
            at = core_first(shard) % 16 * 32
            for half in range(2):
                value = acc_scr[shard * 64 + half * 32 : shard * 64 + half * 32 + 32, :].astype(bf16)

                def put(ref):
                    ref[at : at + 32, half * width : (half + 1) * width] = value

                mine = (sm[3] >> 1 & 1) == (shard >> 1 & 1)
                pl.when(mine)(functools.partial(put, terms[0]))
                pl.when(jnp.logical_not(mine))(functools.partial(put, terms[1]))


def mid(ring, sm, cot, w_out, taps, mask, zs, ys):
    tokens, width = cot.shape
    inner = w_out.shape[0]
    row = lambda n: pl.BlockSpec((MID, n), lambda g: (g, 0))
    wide = struct((tokens, inner), bf16)
    outs = [wide, wide, wide, struct((8, inner))]
    outs += [struct((inner // 4, 2 * width), bf16)] * 2 if ring else [struct(w_out.shape, bf16)]
    return call(
        functools.partial(mid_kernel, ring, len(zs)),
        outs,
        grid=(tokens // MID,),
        in_specs=[SMEM, row(width), whole(w_out.shape), whole(taps.shape), row(128)] + [row(a.shape[1]) for a in (*zs, *ys)],
        out_specs=[row(inner)] * 3 + [whole(o.shape) for o in outs[3:]],
        scratch=[pltpu.VMEM((MID, inner), f32), pltpu.VMEM((MID, inner), f32), pltpu.VMEM(w_out.shape, f32)],
        name="mid",
        flops=4 * tokens * width * inner,
        size=30e6,
    )(sm, cot, w_out, taps, mask, *zs, *ys)


def branch_kernel(x_ref, m_ref, w_ref, out_ref):
    out_ref[...] = x_ref[...] + dot(m_ref[...], w_ref[...])


def branch(x, mixed, w_out):
    tokens, width = x.shape
    row = lambda n: pl.BlockSpec((MID, n), lambda g: (g, 0))
    return call(
        branch_kernel,
        struct(x.shape),
        grid=(tokens // MID,),
        in_specs=[row(width), row(mixed.shape[1]), whole(w_out.shape)],
        out_specs=row(width),
        name="branch",
        flops=2 * tokens * width * mixed.shape[1],
        size=16e6,
    )(x, mixed, w_out)


def bwd_kernel(
    base, cin_ref, y_ref, dy_ref, taps_ref, ea_ref, eb_ref, cum_ref, cumt_ref, b_ref, c_ref, ct_ref, st_ref, mask_ref, h_ref,
    dcin_ref, grad_ref, dst_ref, db_ref, dc_ref, dcum_ref, ddt_ref, cs_scr, ds_scr, e_scr, et_scr, h_scr,
):
    group = pl.program_id(0) + base
    tokens = cin_ref.shape[0]
    cs_scr[0:8, :] = jnp.zeros((8, GROUP), f32)
    cs_scr[pl.ds(8, tokens), :] = cin_ref[...].astype(f32)
    ds_scr[...] = jnp.zeros(ds_scr.shape, f32)
    fill_spread(e_scr, group)
    row, col = iota((GROUP, 128), 0), iota((GROUP, 128), 1)
    et_scr[...] = jnp.where(col == 4 * group + row // 64, 1.0, 0.0).astype(bf16)
    h_scr[...] = jnp.zeros(h_scr.shape, f32)
    taps = taps_ref[...]
    m_low, m_high = pair_masks()
    grad_ref[...] = jnp.zeros(grad_ref.shape, f32)

    @pl.when(pl.program_id(0) == 0)
    def _():
        for ref in (dst_ref, db_ref, dc_ref, dcum_ref, ddt_ref):
            ref[...] = jnp.zeros(ref.shape, f32)

    def to_heads(v):
        hi = v.astype(bf16)
        lo = (v - hi.astype(f32)).astype(bf16)
        return dot(hi, et_scr[...]) + dot(lo, et_scr[...])

    blocks = tokens // BLOCK

    def block(step, _):
        k = blocks - 1 - step
        t0 = pl.multiple_of(k * BLOCK, BLOCK)
        rows = pl.ds(t0, BLOCK)
        mask = mask_ref[rows, :]
        conv, shifted = conv_block(cs_scr[pl.ds(t0, BLOCK + 8), :], mask, taps, 4)
        sig = sigmoid(conv)
        v = conv * sig
        ea = dot(ea_ref[rows, :], e_scr[:, : 2 * GROUP])
        wx = dot(eb_ref[rows, :], e_scr[:, 2 * GROUP :])
        dtx, ex = ea[:, :GROUP], ea[:, GROUP:]
        vd_low = (v * dtx).astype(bf16)
        vd = vd_low.astype(f32)
        dy_low = dy_ref[rows, :]
        dy = dy_low.astype(f32)
        skip = taps[5:6]
        dh_old = h_scr[...]
        dh_low = dh_old.astype(bf16)
        h_low = h_ref[rows, :]
        dye = (dy * ex).astype(bf16)
        dc_ref[rows, :] += dot_nt(dye, h_low)
        db_ref[rows, :] += dot_nt((vd * wx).astype(bf16), dh_low)
        dvd_end = dot(b_ref[rows, :], dh_low) * wx
        cums = pltpu.roll(cum_ref[rows, :], 128 - 4 * group, 1)
        st = st_ref[rows, :]
        inside = []
        dst = jnp.zeros((BLOCK, BLOCK), f32)
        for pair in range(2):
            cols = slice(pair * 128, pair * 128 + 128)
            decays, weights = [], []
            for j in (2 * pair, 2 * pair + 1):
                spread = cumt_ref[0, j : j + 1, rows] - cums[:, j : j + 1]
                decay = jnp.exp2(jnp.minimum(spread, 0.0))
                decays.append(decay)
                weights.append((decay * st).astype(bf16))
            dyp = dy_low[:, cols]
            stack = jnp.concatenate([dyp * m_low, dyp * m_high], axis=0)
            inside.append(dot(jnp.concatenate(weights, axis=1), stack))
            cross = dot_nt(vd_low[:, cols], stack)
            dst = dst + cross[:, :128] * decays[0] + cross[:, 128:] * decays[1]
        dst_ref[rows, :] += dst
        dvd = jnp.concatenate(inside, axis=1) + dvd_end
        through = ex[BLOCK - 1 :]
        last = jnp.sum(vd * dvd_end, axis=0, keepdims=True) + through * jnp.sum(
            dh_old * h_low.astype(f32), axis=0, keepdims=True
        )
        p = dy * (y_ref[rows, :] - skip * v) - vd * dvd
        p = p + jnp.where(iota((BLOCK, 1), 0) == BLOCK - 1, last, 0.0)
        dcum_ref[rows, :] += to_heads(p)
        ddt_ref[rows, :] += to_heads(dvd * v)
        h_scr[...] = dh_old * through + dot(ct_ref[:, rows], dye)
        dconv = (dvd * dtx + skip * dy) * (sig * (1.0 + conv * (1.0 - sig)))
        window = jnp.concatenate([dconv, ds_scr[...]], axis=0)
        ds_scr[...] = dconv[:8]
        grads = [jnp.sum(rows8(dconv * shifted[3 - i]), axis=0, keepdims=True) for i in range(4)]
        grads.append(jnp.sum(rows8(dconv), axis=0, keepdims=True))
        grads.append(jnp.sum(rows8(dy * v), axis=0, keepdims=True))
        grads.append(jnp.zeros((2, GROUP), f32))
        grad_ref[...] += jnp.concatenate(grads, axis=0)
        dcin_ref[rows, :] = conv_back(
            window, mask_ref[pl.ds(t0, BLOCK + 8), :], taps, 4
        ).astype(bf16)
        return 0

    lax.fori_loop(0, blocks, block, 0)


def bwd(base, count, cin, y, dy, taps, pre, h):
    tokens = cin.shape[0]
    full = lambda a: whole(a.shape)
    ea, eb, cum, cumt, b, c, ct, st, mask = pre
    local = lambda rows: pl.BlockSpec((rows, GROUP), lambda g: (0, g))
    global_ = lambda rows: pl.BlockSpec((rows, GROUP), lambda g: (0, base + g))
    wide = struct((tokens, 128))
    return call(
        functools.partial(bwd_kernel, base),
        [struct((tokens, count * GROUP), bf16), struct((8, count * GROUP))] + [wide] * 5,
        grid=(count,),
        in_specs=[
            local(tokens), local(tokens), global_(tokens), global_(8),
            full(ea), full(eb), full(cum),
            pl.BlockSpec((1, 4, tokens), lambda g: (base + g, 0, 0)),
            full(b), full(c), full(ct), full(st), full(mask), local(tokens),
        ],
        out_specs=[local(tokens), local(8)] + [whole(wide.shape)] * 5,
        scratch=[
            pltpu.VMEM((tokens + 8, GROUP), f32), pltpu.VMEM((8, GROUP), f32),
            pltpu.VMEM((128, 3 * GROUP), bf16), pltpu.VMEM((GROUP, 128), bf16), pltpu.VMEM((128, GROUP), f32),
        ],
        name=f"bwd{base}",
        flops=count * 2 * tokens * 128 * GROUP * 8,
        size=count * 4e6,
    )(cin, y, dy, taps, ea, eb, cum, cumt, b, c, ct, st, mask, h)


def tail_kernel(sm, cin_ref, taps_ref, head_ref, b_ref, c_ref, step_ref, mask_ref, *refs):
    dp_ref, grad_ref, stat_ref, cs_scr, ds_scr = refs[-5:]
    sums = refs[:-5]
    tokens = cin_ref.shape[0]
    cs_scr[0:8, :] = jnp.zeros((8, 256), f32)
    cs_scr[pl.ds(8, tokens), :] = cin_ref[...].astype(f32)
    ds_scr[...] = jnp.zeros(ds_scr.shape, f32)
    taps = taps_ref[...]
    grad_ref[...] = jnp.zeros(grad_ref.shape, f32)
    stat_ref[...] = jnp.zeros(stat_ref.shape, f32)
    blocks = tokens // BLOCK

    def block(step, _):
        k = blocks - 1 - step
        t0 = pl.multiple_of(k * BLOCK, BLOCK)
        rows = pl.ds(t0, BLOCK)
        row, lane = iota((BLOCK, 128), 0), iota((BLOCK, 128), 1)
        dst_sum, db_sum, dc_sum, dcum_sum, ddt_sum = [
            functools.reduce(jnp.add, [ref[rows, :] for ref in sums[i::5]]) for i in range(5)
        ]
        keep = (lane >= row) & (scene_of(lane + t0, sm) == scene_of(row + t0, sm))
        dst = jnp.where(keep, dst_sum, 0.0).astype(bf16)
        db = db_sum + dot(dst, c_ref[rows, :])
        dc = dc_sum + dot_tn(dst, b_ref[rows, :])
        conv, shifted = conv_block(cs_scr[pl.ds(t0, BLOCK + 8), :], mask_ref[rows, :], taps, 4)
        sig = sigmoid(conv)
        dconv = jnp.concatenate([db, dc], axis=1) * (sig * (1.0 + conv * (1.0 - sig)))
        window = jnp.concatenate([dconv, ds_scr[...]], axis=0)
        ds_scr[...] = dconv[:8]
        grads = [jnp.sum(rows8(dconv * shifted[3 - i]), axis=0, keepdims=True) for i in range(4)]
        grads.append(jnp.sum(rows8(dconv), axis=0, keepdims=True))
        grads.append(jnp.zeros((3, 256), f32))
        grad_ref[...] += jnp.concatenate(grads, axis=0)
        dcin = conv_back(window, mask_ref[pl.ds(t0, BLOCK + 8), :], taps, 4)
        upper = jnp.where(lane >= row, 1.0, 0.0)
        dlog = jnp.dot(upper, dcum_sum, precision=highest, preferred_element_type=f32)
        step_in = step_ref[rows, :]
        dt = jnp.maximum(step_in, 0.0) + jnp.log1p(jnp.exp(-jnp.abs(step_in)))
        rate = head_ref[1:2, :]
        dstep = (ddt_sum - dlog * rate) * sigmoid(step_in)
        dalog = -dlog * dt * rate
        stat_ref[...] += jnp.concatenate(
            [
                jnp.sum(rows8(dstep), axis=0, keepdims=True),
                jnp.sum(rows8(dalog), axis=0, keepdims=True),
                jnp.zeros((6, 128), f32),
            ],
            axis=0,
        )
        dp_ref[rows, :] = jnp.concatenate([dcin, dstep], axis=1).astype(bf16)
        return 0

    lax.fori_loop(0, blocks, block, 0)


def tail(sm, cin, taps, head, b, c, step, mask, sums):
    tokens = cin.shape[0]
    args = (cin, taps, head, b, c, step, mask, *sums)
    outs = [struct((tokens, 384), bf16), struct((8, 256)), struct((8, 128))]
    return call(
        tail_kernel,
        outs,
        in_specs=[SMEM] + [whole(a.shape) for a in args],
        out_specs=[whole(o.shape) for o in outs],
        scratch=[pltpu.VMEM((tokens + 8, 256), f32), pltpu.VMEM((8, 256), f32)],
        name="tail",
        flops=2 * tokens * 128 * 128 * 4,
        size=8e6,
    )(sm, *args)


def term_kernel(sm, nt_ref, *refs):
    *parts, out_ref = refs
    at = 0
    for part in parts:
        out_ref[:, at : at + part.shape[1]] = dot(nt_ref[...], part[...]).astype(bf16)
        at += part.shape[1]


def in_term(half, normt, parts, name):
    halves, width, tokens = normt.shape
    n = sum(p.shape[1] for p in parts)
    spec = pltpu.PrefetchScalarGridSpec(
        num_scalar_prefetch=1,
        grid=(1,),
        in_specs=[pl.BlockSpec((None, width, tokens), lambda g, sm: (sm[0], 0, 0))]
        + [pl.BlockSpec(p.shape, lambda g, sm: (0, 0)) for p in parts],
        out_specs=pl.BlockSpec((width, n), lambda g, sm: (0, 0)),
    )
    return pl.pallas_call(
        term_kernel,
        out_shape=struct((width, n), bf16),
        grid_spec=spec,
        name=name,
        compiler_params=pltpu.CompilerParams(vmem_limit_bytes=VMEM_LIMIT, dimension_semantics=("arbitrary",)),
        cost_estimate=pl.CostEstimate(
            flops=2 * tokens * width * n, bytes_accessed=2 * (width * tokens + tokens * n + width * n), transcendentals=0
        ),
    )(half, normt, *parts)


def last_kernel(count, x_ref, cot_ref, gain_ref, *refs):
    ds, ws, (dx_ref, gg_ref) = refs[:count], refs[count : 2 * count], refs[2 * count :]
    x = x_ref[...]
    width = x.shape[1]
    dn = functools.reduce(jnp.add, [dot_nt(d[...], w[...]) for d, w in zip(ds, ws)])
    r = lax.rsqrt(jnp.mean(x * x, axis=-1, keepdims=True) + EPS)
    u = dn * gain_ref[0:1, :]
    xr = x * r
    mu = jnp.sum(u * xr, axis=-1, keepdims=True) * (1.0 / width)
    dx_ref[...] = cot_ref[...] + r * (u - xr * mu)
    gg = rows8(dn * xr)

    @pl.when(pl.program_id(0) == 0)
    def _():
        gg_ref[...] = gg

    @pl.when(pl.program_id(0) > 0)
    def _():
        gg_ref[...] += gg


def last(x, cot, gain, pairs):
    tokens, width = x.shape
    row = lambda n: pl.BlockSpec((MID, n), lambda g: (g, 0))
    ds, ws = zip(*pairs)
    n = sum(k for _, k, _ in ds)
    return call(
        functools.partial(last_kernel, len(pairs)),
        [struct(x.shape), struct((8, width))],
        grid=(tokens // MID,),
        in_specs=[row(width), row(width), whole(gain.shape)]
        + [pl.BlockSpec((MID, k), functools.partial(lambda i, g: (g, i), i)) for _, k, i in ds]
        + [pl.BlockSpec((width, k), functools.partial(lambda i, g: (0, i), i)) for _, k, i in ws],
        out_specs=[row(width), whole((8, width))],
        name="last",
        flops=2 * tokens * width * n,
        size=40e6,
    )(x, cot, gain, *[d[0] for d in ds], *[w[0] for w in ws])


Y, CORE, X, Z1, Z2 = 1, 2, 4, 8, 16


def exchange(a, bit):
    return lax.ppermute(a, AXES, [(i, i ^ bit) for i in range(SHARDS)])


def gather_z(own):
    two = jnp.concatenate([own, exchange(own, Z1)], axis=0)
    return jnp.concatenate([two, exchange(two, Z2)], axis=0)


def gather_rest(four, x_first):
    first, second = (X, Y) if x_first else (Y, X)
    found = {0: four, first: exchange(four, first)}
    for key in (0, first):
        found[key | second] = exchange(found[key], second)
    for key in (0, X, Y, X | Y):
        found[key | CORE] = exchange(found[key], CORE)
    return [found[key] for key in PIECES]


def take(a, bit, axis):
    return lax.dynamic_index_in_dim(a, bit, axis, keepdims=False)


def scatter_chips(place, keep, order):
    names = [Z2, Z1, X, Y]
    left = keep.reshape(2, 2, 2, 2, keep.shape[0] // 16, keep.shape[1])
    for bit in order:
        axis = names.index(bit)
        names.pop(axis)
        mine = jnp.where((place & bit) > 0, 1, 0)
        got = exchange(take(left, 1 - mine, axis), bit)
        left = take(left, mine, axis).astype(f32) + got.astype(f32)
        if names:
            left = left.astype(bf16)
    return left


def both(a, b):
    return (a.astype(f32) + b.astype(f32)).astype(bf16)


def pad_to(a, rows, columns):
    return jnp.pad(a, ((0, rows - a.shape[0]), (0, columns - a.shape[1])))


def local(
    ring, block_input, cotangent, scene_lengths, norm_gain, in_weight, conv_weight, conv_bias, dt_bias, a_log, skip_gain,
    gated_gain, out_weight,
):
    tokens, width = block_input.shape
    heads = a_log.shape[0]
    inner = out_weight.shape[0] * lax.axis_size(AXES)
    channels = conv_bias.shape[0] * lax.axis_size(AXES)
    proj = in_weight.shape[1]
    bc = proj - 2 * inner
    place = lax.axis_index(AXES).astype(jnp.int32)
    bounds = jnp.cumsum(scene_lengths[0]).astype(jnp.int32)
    sm = jnp.concatenate([bounds, place[None], jnp.zeros((4,), jnp.int32)])
    groups = inner // GROUP
    gather = lambda a: lax.all_gather(a.astype(bf16), AXES, axis=0, tiled=True)
    skip_row = jnp.repeat(skip_gain, inner // heads)[None]
    w_low = in_weight.astype(bf16)
    if ring:
        out_full = gather(out_weight)
        small = jnp.concatenate(
            [
                jnp.concatenate([norm_gain, gated_gain])[None],
                pad_to(conv_weight.T, 4, 96),
                pad_to(conv_bias[None], 27, 96),
            ],
            axis=0,
        )
        first = jnp.concatenate([w_low[:, 2 * inner :], small.astype(bf16)], axis=1)
        pieces = gather_rest(gather_z(first), True)
        w_bc, taps, gain = unpack(sm, pieces, skip_row, channels, width)
        bases = (0, groups // 2)
        weights = []
        wide = inner // 2
        for base in bases:
            at = base * GROUP
            four = gather_z(jnp.concatenate([w_low[:, at : at + wide], w_low[:, inner + at : inner + at + wide]], axis=1))
            weights.append((gather_rest(four[:, :wide], True), gather_rest(four[:, wide:], False)))
    else:
        in_full, out_full = gather(in_weight), gather(out_weight)
        norm_full, conv_full, bias_full, gated_full = map(gather, (norm_gain, conv_weight, conv_bias, gated_gain))
        gain = jnp.broadcast_to(norm_full.astype(f32)[None], (8, width))
        w_bc = pad_to(in_full[:, 2 * inner :], width, 384)
        taps = jnp.concatenate(
            [
                conv_full.astype(f32).T,
                bias_full.astype(f32)[None],
                pad_to(jnp.concatenate([skip_row, gated_full.astype(f32)[None]], axis=0), 3, channels),
            ],
            axis=0,
        )
        bases = (0,)
        weights = [([in_full], [in_full])]
    taps_bc = taps[:, inner:]
    head = jnp.pad(jnp.stack([dt_bias, jnp.exp(a_log)]), ((0, 6), (0, 128 - heads)))
    (normed, normt, cin_bc, b, c, bt, ct, s, st, cum, cumt, ea, eb, step, mask) = prep(
        ring, sm, block_input, gain, w_bc, taps_bc, head, heads
    )
    cumt = cumt.reshape(heads // 4, 4, tokens)
    count = groups // len(bases)
    pre = (ea, eb, cum, cumt, c, bt, s, mask)
    runs = [fwd(base, count, ring, sm, normed, *w, inner, taps, pre) for base, w in zip(bases, weights)]
    mixed, dz, dy, gg, *terms = mid(
        ring, sm, cotangent, out_full, taps, mask, [r[0] for r in runs], [r[2] for r in runs]
    )
    normt = normt.reshape(2 if ring else 1, -1, tokens)
    core = sm[3:4] >> 1 & 1
    if ring:
        gate_away = exchange(in_term(1 - core, normt, [dz], "gate_away"), CORE)
        out_away = exchange(terms[1], CORE)
        gate_here = in_term(core, normt, [dz], "gate_here")
        early = jnp.concatenate([both(gate_here, gate_away), both(terms[0], out_away)], axis=1)
        early = lax.psum_scatter(early, CHIPS, scatter_dimension=0, tiled=True).astype(f32)
        gate_grad, out_grad = early[:, :inner], early[:, inner:]
        out_grad = jnp.concatenate([out_grad[:, :width], out_grad[:, width:]], axis=0)
    dvs, grads, sums = [], [], []
    pre = (ea, eb, cum, cumt, b, c, ct, st, mask)
    for base, run in zip(bases, runs):
        dv, grad, *part = bwd(base, count, run[1], run[2], dy, taps, pre, run[3])
        dvs.append(dv)
        grads.append(grad)
        sums += part
    dbc, grad_bc, stat = tail(sm, cin_bc, taps_bc, head, b, c, step, mask, sums)
    grads = jnp.concatenate([*grads, grad_bc], axis=1)
    if ring:
        late = []
        for parts, order, name in (([dvs[0]], (X, Y, Z2, Z1), "late0"), ([dvs[1], dbc], (Y, X, Z2, Z1), "late1")):
            away = exchange(in_term(1 - core, normt, parts, name + "_away"), CORE)
            here = in_term(core, normt, parts, name + "_here")
            late.append(scatter_chips(place, both(here, away), order))
        in_grad = jnp.concatenate([gate_grad, *late], axis=1)[:, :proj]
        pairs = []
        for i, run in enumerate(runs):
            pairs.append(((dz, wide, i), (run[4], wide, 0)))
            pairs.append(((dvs[i], wide, 0), (run[5], wide, 0)))
    else:
        scatter = lambda a: lax.psum_scatter(a.astype(f32), AXES, scatter_dimension=0, tiled=True)
        in_grad = scatter(in_term(core * 0, normt, [dz, *dvs, dbc], "all")[:, :proj])
        out_grad = scatter(terms[0])
        pairs = [((dz, inner, 0), (in_full, inner, 0)), ((dvs[0], inner, 0), (in_full, inner, 1))]
    pairs.append(((dbc, 384, 0), (w_bc, 384, 0)))
    input_grad, d_gain = last(block_input, cotangent, gain, pairs)
    block_output = branch(block_input, mixed, out_full)
    d_skip = jnp.sum(grads[5, :inner].reshape(heads, -1), axis=1)
    side = jnp.concatenate([jnp.sum(d_gain, axis=0), stat[0, :heads], stat[1, :heads], d_skip])
    small = jnp.concatenate(
        [grads[:5], pad_to(jnp.sum(gg, axis=0)[None], 1, channels), pad_to(side[None], 2, channels)], axis=0
    )
    if ring:
        for bit in (CORE, X, Y, Z1, Z2):
            small = small + exchange(small, bit)
    else:
        small = lax.psum(small, AXES)
    part = lambda row, n: lax.dynamic_slice_in_dim(row, place * n, n, axis=-1)
    side = small[6, width:]
    return (
        block_output,
        input_grad,
        part(small[6], norm_gain.shape[0]),
        in_grad,
        part(small[:4], conv_bias.shape[0]).T,
        part(small[4], conv_bias.shape[0]),
        side[:heads],
        side[heads : 2 * heads],
        side[2 * heads : 3 * heads],
        part(small[5], gated_gain.shape[0]),
        out_grad,
    )


def solution(mesh):
    dp, fsdp = mesh.devices.shape
    split = jax.sharding.Mesh(mesh.devices.reshape(dp // 2, 2, fsdp), AXES)
    row = P(AXES, None)
    flat = P(AXES)
    return jax.shard_map(
        functools.partial(local, (dp, fsdp) == (16, 2)),
        mesh=split,
        in_specs=(row, row, row, flat, row, row, flat, P(), P(), P(), flat, row),
        out_specs=(row, row, flat, row, row, flat, P(), P(), P(), flat, row),
        check_vma=False,
    )
```

```python
import functools

import jax
import jax.numpy as jnp
from jax import lax
from jax.experimental import pallas as pl
from jax.experimental.pallas import tpu as pltpu
from jax.sharding import PartitionSpec as P

AXES = ("chip", "core", "fsdp")
CHIPS = ("chip", "fsdp")
SHARDS = 32
PIECES = tuple(c | y | x for c in (0, 2) for y in (0, 1) for x in (0, 4))
BLOCK = 128
GROUP = 256
EPS = 1e-05
LOG2E = 1.4426950408889634
VMEM_LIMIT = 60 * 1024 * 1024
f32 = jnp.float32
bf16 = jnp.bfloat16
highest = lax.Precision.HIGHEST


def dot(a, b):
    return jnp.dot(a, b, preferred_element_type=f32)


def dot_nt(a, b):
    return lax.dot_general(a, b, (((1,), (1,)), ((), ())), preferred_element_type=f32)


def dot_tn(a, b):
    return lax.dot_general(a, b, (((0,), (0,)), ((), ())), preferred_element_type=f32)


def sigmoid(v):
    return 0.5 * jnp.tanh(0.5 * v) + 0.5


def iota(shape, axis):
    return lax.broadcasted_iota(jnp.int32, shape, axis)


def rows8(v):
    return jnp.sum(v.reshape(v.shape[0] // 8, 8, v.shape[1]), axis=0)


def scene_of(place, sm):
    scene = jnp.zeros(place.shape, jnp.int32)
    for i in range(3):
        scene = scene + jnp.where(place >= sm[i], 1, 0)
    return scene


def cost(us):
    return pl.CostEstimate(flops=0, bytes_accessed=int(us * 3.69e6), transcendentals=0)


def call(kernel, out, grid=None, in_specs=None, out_specs=None, scratch=(), name=None, us=1.0):
    return pl.pallas_call(
        kernel,
        out_shape=out,
        grid=grid or (1,),
        in_specs=in_specs,
        out_specs=out_specs,
        scratch_shapes=scratch,
        name=name,
        compiler_params=pltpu.CompilerParams(
            vmem_limit_bytes=VMEM_LIMIT, dimension_semantics=("arbitrary",)
        ),
        cost_estimate=cost(us),
    )


def whole(shape):
    return pl.BlockSpec(shape, lambda g: (0,) * len(shape))


def bc_taps(inner):
    return pl.BlockSpec((8, 256), lambda g: (0, inner // 256))


SMEM = pl.BlockSpec(memory_space=pltpu.SMEM)


def struct(shape, dtype=f32):
    return jax.ShapeDtypeStruct(shape, dtype)


def conv_block(window, masks, taps, width):
    current = window[8:]
    total = taps[4:5] + current * taps[3:4]
    shifted = [current]
    for off in range(1, width):
        moved = window[8 - off : 8 - off + BLOCK] * masks[:, off - 1 : off]
        shifted.append(moved)
        total = total + moved * taps[width - 1 - off : width - off]
    return total, shifted


def conv_back(window, masks, taps, width):
    total = window[:BLOCK] * taps[width - 1 : width]
    for off in range(1, width):
        moved = pltpu.roll(window * masks[:, off - 1 : off], window.shape[0] - off, 0)[:BLOCK]
        total = total + moved * taps[width - 1 - off : width - off]
    return total


def unpack_kernel(sm, *refs):
    pieces, (skip_ref, w_ref, taps_ref, gain_ref) = refs[: len(PIECES)], refs[len(PIECES) :]
    assemble(sm, pieces, w_ref, 32)
    row, col = iota((8 * SHARDS, 32 * SHARDS), 0), iota((8 * SHARDS, 32 * SHARDS), 1)
    pick = jnp.where(col == (row & (SHARDS - 1)) * 32 + row // SHARDS, 1.0, 0.0).astype(bf16)
    packed = dot(pick, w_ref[:, 256:384]).astype(bf16)

    def spread(kind, lane, size):
        total = size * SHARDS
        place = iota((1, total), 1)
        owner, within = place // size, place % size
        copy = jnp.where(iota((128, total), 0) == within + lane, 1.0, 0.0).astype(bf16)
        values = dot(packed[kind * SHARDS : (kind + 1) * SHARDS, :], copy)
        return jnp.sum(jnp.where(iota((SHARDS, total), 0) == owner, values, 0.0), axis=0, keepdims=True)

    taps_ref[...] = jnp.zeros(taps_ref.shape, f32)
    gain_ref[...] = jnp.broadcast_to(spread(0, 32, 32), gain_ref.shape)
    inner = skip_ref.shape[1]
    taps_ref[6:7, :inner] = spread(0, 64, inner // SHARDS)
    channels = taps_ref.shape[1]
    for k in range(5):
        taps_ref[k : k + 1, :] = spread(k + 1, 32, channels // SHARDS)
    taps_ref[5:6, :inner] = skip_ref[0:1, :]


def unpack(sm, pieces, skip, channels, width):
    outs = [struct((width, 384), bf16), struct((8, channels)), struct((8, width))]
    return call(
        unpack_kernel,
        outs,
        in_specs=[SMEM] + [whole(a.shape) for a in (*pieces, skip)],
        out_specs=[whole(o.shape) for o in outs],
        name="unpack",
        us=3.0,
    )(sm, *pieces, skip)


def core_first(shard):
    return (shard >> 1 & 1) * 16 + (shard >> 2) * 2 + (shard & 1)


def prep_kernel(
    ring, sm, x_ref, gain_ref, w_ref, taps_ref, head_ref,
    normed_ref, normt_ref, cin_ref, b_ref, c_ref, bt_ref, ct_ref, s_ref, st_ref,
    cum_ref, cumt_ref, ea_ref, eb_ref, step_ref, mask_ref, cs_scr,
):
    tokens = x_ref.shape[0]
    x = x_ref[...]
    scale = lax.rsqrt(jnp.mean(x * x, axis=-1, keepdims=True) + EPS)
    normed_low = (x * scale * gain_ref[0:1, :]).astype(bf16)
    normed_ref[...] = normed_low
    flipped = normed_low.astype(f32).T.astype(bf16)
    if ring:
        for shard in range(SHARDS):
            at = core_first(shard) * 32
            normt_ref[at : at + 32, :] = flipped[shard * 32 : shard * 32 + 32, :]
    else:
        normt_ref[...] = flipped
    proj = dot(normed_low, w_ref[...])
    lanes = iota((1, 128), 1)
    heads = 4 * cumt_ref.shape[0]
    is_head = lanes < heads
    cin_low = proj[:, :256].astype(bf16)
    cin_ref[...] = cin_low
    cs_scr[0:8, :] = jnp.zeros((8, 256), f32)
    cs_scr[pl.ds(8, tokens), :] = cin_low.astype(f32)
    step_ref[...] = jnp.where(is_head, proj[:, 256:384] + head_ref[0:1, :], 0.0)
    taps = taps_ref[...]

    for k in range(tokens // BLOCK):
        t0 = k * BLOCK
        rows = pl.ds(t0, BLOCK)
        place = iota((BLOCK, 128), 0) + t0
        lane = iota((BLOCK, 128), 1)
        scene = scene_of(place, sm)
        before = place - lane - 1
        same = (before >= 0) & (scene_of(before, sm) == scene)
        mask = jnp.where(lane < 3, jnp.where(same, 1.0, 0.0), jnp.where(place < sm[2], 1.0, 0.0))
        mask_ref[rows, :] = mask
        conv, _ = conv_block(cs_scr[pl.ds(t0, BLOCK + 8), :], mask, taps, 4)
        act = conv * sigmoid(conv)
        b_low = act[:, :128].astype(bf16)
        c_low = act[:, 128:].astype(bf16)
        b_ref[rows, :] = b_low
        c_ref[rows, :] = c_low
        bt_ref[:, rows] = act[:, :128].T.astype(bf16)
        ct_ref[:, rows] = act[:, 128:].T.astype(bf16)
        other = scene_of(lane + t0, sm)
        low = (lane + t0 <= place) & (other == scene)
        s_ref[rows, :] = jnp.where(low, dot_nt(c_low, b_low), 0.0)
        high = (lane + t0 >= place) & (other == scene)
        st_ref[rows, :] = jnp.where(high, dot_nt(b_low, c_low), 0.0)
        step = step_ref[rows, :]
        dt = jnp.maximum(step, 0.0) + jnp.log1p(jnp.exp(-jnp.abs(step)))
        dt = jnp.where(is_head, dt, 0.0)
        log_decay = dt * (head_ref[1:2, :] * -LOG2E)
        lower = jnp.where(lane <= iota((BLOCK, 128), 0), 1.0, 0.0)
        cum = jnp.dot(lower, log_decay, precision=highest, preferred_element_type=f32)
        cum_ref[rows, :] = cum
        flat = cum.T
        for i in range(heads // 4):
            cumt_ref[i, :, rows] = flat[4 * i : 4 * i + 4, :]
        first = jnp.full((1, 128), t0 - 1, jnp.int32)
        last = jnp.full((1, 128), t0 + BLOCK - 1, jnp.int32)
        entering = (scene_of(first, sm) == scene) & (first >= 0) & is_head
        final = (scene_of(last, sm) == scene) & is_head
        grow = jnp.where(entering, jnp.exp2(cum), 0.0)
        end = jnp.where(final, jnp.exp2(cum[BLOCK - 1 :] - cum), 0.0)

        def packed(v):
            hi = v.astype(bf16).astype(f32)
            return hi + pltpu.roll((v - hi).astype(bf16).astype(f32), 32, 1)

        ea_ref[rows, :] = (packed(dt) + pltpu.roll(packed(grow), 64, 1)).astype(bf16)
        eb_ref[rows, :] = packed(end).astype(bf16)
    mask_ref[pl.ds(tokens, 8), :] = jnp.zeros((8, 128), f32)


def prep(ring, sm, x, gain, w_bc, taps, inner, head, heads):
    tokens, width = x.shape
    wide = (tokens, 128)
    outs = [
        struct(x.shape, bf16), struct((width, tokens), bf16), struct((tokens, 256), bf16),
        struct(wide, bf16), struct(wide, bf16), struct((128, tokens), bf16), struct((128, tokens), bf16),
        struct(wide), struct(wide), struct(wide), struct((heads // 4, 4, tokens)), struct(wide, bf16), struct(wide, bf16),
        struct(wide), struct((tokens + 8, 128)),
    ]
    args = (x, gain, w_bc, taps, head)
    return call(
        functools.partial(prep_kernel, ring),
        outs,
        in_specs=[SMEM] + [whole(a.shape) if a is not taps else bc_taps(inner) for a in args],
        out_specs=[whole(o.shape) for o in outs],
        scratch=[pltpu.VMEM((tokens + 8, 256), f32)],
        name="prep",
        us=13.0,
    )(sm, *args)


def fill_spread(e_scr, group):
    row = iota((128, 768), 0)
    col = iota((128, 768), 1)
    head = 4 * group + (col % GROUP) // 64
    part = jnp.where(col < GROUP, 0, jnp.where(col < 2 * GROUP, 64, 0))
    hit = (row == head + part) | (row == head + part + 32)
    e_scr[...] = jnp.where(hit, 1.0, 0.0).astype(bf16)


def pair_masks():
    low = jnp.where(iota((1, 128), 1) < 64, 1.0, 0.0).astype(bf16)
    high = jnp.where(iota((1, 128), 1) < 64, 0.0, 1.0).astype(bf16)
    return low, high


def assemble(sm, pieces, out_ref, block):
    for i, piece in enumerate(pieces):
        for j in range(4):
            shard = sm[3] ^ (PIECES[i] | j << 3)
            out_ref[pl.ds(pl.multiple_of(shard * block, block), block), :] = piece[j * block : (j + 1) * block, :]


def fwd_kernel(*refs):
    base, ring, sm = refs[:3]
    if ring:
        n = len(PIECES)
        gates, values = refs[3 : 3 + n], refs[3 + n : 3 + 2 * n]
        rest = list(refs[3 + 2 * n :])
        wv_ref, wg_ref = rest.pop(15), rest.pop(14)
        assemble(sm, gates, wg_ref, 32)
        assemble(sm, values, wv_ref, 32)
        rest[1:1] = [wg_ref, wv_ref]
    else:
        rest = list(refs[5:])
        rest[1:1] = refs[3:5]
    fwd_body(base, *rest)


def fwd_body(
    base, normed_ref, wg_ref, wv_ref, taps_ref, ea_ref, eb_ref, cum_ref, cumt_ref, c_ref, bt_ref, s_ref, mask_ref,
    z_ref, cin_ref, y_ref, h_ref, cs_scr, e_scr,
):
    group = pl.program_id(0) + base
    tokens = normed_ref.shape[0]
    normed = normed_ref[...]
    z_ref[...] = dot(normed, wg_ref[...]).astype(bf16)
    cin_low = dot(normed, wv_ref[...]).astype(bf16)
    cin_ref[...] = cin_low
    cs_scr[0:8, :] = jnp.zeros((8, GROUP), f32)
    cs_scr[pl.ds(8, tokens), :] = cin_low.astype(f32)
    fill_spread(e_scr, group)
    taps = taps_ref[...]
    m_low, m_high = pair_masks()

    state = jnp.zeros((128, GROUP), f32)
    blocks = tokens // BLOCK
    for k in range(blocks):
        t0 = k * BLOCK
        rows = pl.ds(t0, BLOCK)
        mask = mask_ref[rows, :]
        conv, _ = conv_block(cs_scr[pl.ds(t0, BLOCK + 8), :], mask, taps, 4)
        v = conv * sigmoid(conv)
        ea = dot(ea_ref[rows, :], e_scr[:, : 2 * GROUP])
        wx = dot(eb_ref[rows, :], e_scr[:, 2 * GROUP :])
        dtx, ex = ea[:, :GROUP], ea[:, GROUP:]
        vd_low = (v * dtx).astype(bf16)
        h_low = state.astype(bf16)
        h_ref[rows, :] = h_low
        cums = pltpu.roll(cum_ref[rows, :], 128 - 4 * group, 1)
        s = s_ref[rows, :]
        inside = []
        for pair in range(2):
            weights = []
            for j in (2 * pair, 2 * pair + 1):
                spread = cums[:, j : j + 1] - cumt_ref[0, j : j + 1, rows]
                weights.append((jnp.exp2(jnp.minimum(spread, 0.0)) * s).astype(bf16))
            vp = vd_low[:, pair * 128 : pair * 128 + 128]
            stack = jnp.concatenate([vp * m_low, vp * m_high], axis=0)
            inside.append(dot(jnp.concatenate(weights, axis=1), stack))
        y = jnp.concatenate(inside, axis=1) + taps[5:6] * v
        if k > 0:
            y = y + dot(c_ref[rows, :], h_low) * ex
        y_ref[rows, :] = y
        if k < blocks - 1:
            fresh = dot(bt_ref[:, rows], (vd_low.astype(f32) * wx).astype(bf16))
            state = state * ex[BLOCK - 1 :] + fresh


def fwd(base, count, offset, ring, sm, normed, gates, values, inner, taps, pre):
    tokens, width = normed.shape
    full = lambda a: whole(a.shape)
    ea, eb, cum, cumt, c, bt, s, mask = pre
    first = inner // GROUP
    col = lambda rows, dtype: struct((rows, count * GROUP), dtype)
    block = lambda rows: pl.BlockSpec((rows, GROUP), lambda g: (0, g))
    outs = [col(tokens, bf16), col(tokens, bf16), col(tokens, f32), col(tokens, bf16)]
    if ring:
        w_specs = [pl.BlockSpec((a.shape[0], GROUP), lambda g: (0, offset + g)) for a in (*gates, *values)]
        outs += [col(width, bf16)] * 2
    else:
        w_specs = [
            pl.BlockSpec((width, GROUP), lambda g: (0, base + g)),
            pl.BlockSpec((width, GROUP), lambda g: (0, first + base + g)),
        ]
    return call(
        functools.partial(fwd_kernel, base, ring),
        outs,
        grid=(count,),
        in_specs=[SMEM] + w_specs + [
            full(normed),
            pl.BlockSpec((8, GROUP), lambda g: (0, base + g)),
            full(ea), full(eb), full(cum),
            pl.BlockSpec((1, 4, tokens), lambda g: (base + g, 0, 0)),
            full(c), full(bt), full(s), full(mask),
        ],
        out_specs=[block(o.shape[0]) for o in outs],
        scratch=[pltpu.VMEM((tokens + 8, GROUP), f32), pltpu.VMEM((128, 3 * GROUP), bf16)],
        name=f"fwd{base}",
        us=count * 6.6,
    )(sm, *gates, *values, normed, taps, ea, eb, cum, cumt, c, bt, s, mask)


MID = 256
WIDE = 512
MID_C = 512


def mid_kernel(ring, chunks, cot_ref, w_ref, taps_ref, mask_ref, *refs):
    zs, ys = refs[:chunks], refs[chunks : 2 * chunks]
    mixed_ref, dz_ref, dy_ref, gg_ref, flip_ref, low_ref, g_scr, u_scr = refs[2 * chunks :]

    @pl.when(pl.program_id(0) == 0)
    def _():
        gg_ref[...] = jnp.zeros(gg_ref.shape, f32)

    inner = dz_ref.shape[1]
    alive = mask_ref[:, 3:4]
    cot_low = cot_ref[...].astype(bf16)
    low_ref[...] = cot_low
    square = jnp.zeros((MID, 128), f32)
    parts = [slice(i, i + MID_C) for i in range(0, inner, MID_C)]
    here = [(z, y, slice(i, i + MID_C)) for z, y in zip(zs, ys) for i in range(0, z.shape[1], MID_C)]
    for part, (z_ref, y_ref, cut) in zip(parts, here):
        z = z_ref[:, cut].astype(f32)
        g = y_ref[:, cut] * (z * sigmoid(z))
        g_scr[:, part] = g
        sq = g * g
        for i in range(0, MID_C, 128):
            square = square + sq[:, i : i + 128]
    r = lax.rsqrt(jnp.sum(square, axis=-1, keepdims=True) * (1.0 / inner) + EPS)
    r_alive = r * alive
    cross = jnp.zeros((MID, 128), f32)
    for part in parts:
        gain = taps_ref[6:7, part]
        dm = dot_nt(cot_low, w_ref[part, :])
        g = g_scr[:, part]
        u = dm * gain
        u_scr[:, part] = u
        ug = u * g
        for i in range(0, MID_C, 128):
            cross = cross + ug[:, i : i + 128]
        gr = g * r_alive
        mixed = gr * gain
        mixed_ref[:, part] = mixed.astype(bf16)
        gg_ref[:, part] += rows8(dm * gr)
        flipped = mixed.T.astype(bf16)
        for i in range(0, MID_C, 32):
            shard, half = (part.start + i) // 64, i // 32 % 2
            place = core_first(shard) // 16 * 32 + half * 16 + core_first(shard) % 16 if ring else (part.start + i) // 32
            flip_ref[place * 32 : place * 32 + 32, :] = flipped[i : i + 32, :]
    r3 = r_alive * r * r * (jnp.sum(cross, axis=-1, keepdims=True) * (1.0 / inner))
    for part, (z_ref, y_ref, cut) in zip(parts, here):
        z = z_ref[:, cut].astype(f32)
        sig = sigmoid(z)
        dg = u_scr[:, part] * r_alive - g_scr[:, part] * r3
        silu = z * sig
        dy_ref[:, part] = (dg * silu).astype(bf16)
        dz_ref[:, part] = (dg * y_ref[:, cut] * (sig + silu * (1.0 - sig))).astype(bf16)


def mid(ring, cot, w_out, taps, mask, zs, ys):
    tokens, width = cot.shape
    inner = w_out.shape[0]
    row = lambda n: pl.BlockSpec((MID, n), lambda g: (g, 0))
    wide = struct((tokens, inner), bf16)
    outs = [wide, wide, wide, struct((8, inner)), struct((inner, tokens), bf16), struct(cot.shape, bf16)]
    return call(
        functools.partial(mid_kernel, ring, len(zs)),
        outs,
        grid=(tokens // MID,),
        in_specs=[row(width), whole(w_out.shape), whole(taps.shape), row(128)] + [row(a.shape[1]) for a in (*zs, *ys)],
        out_specs=[row(inner)] * 3 + [whole((8, inner)), pl.BlockSpec((inner, MID), lambda g: (0, g)), row(width)],
        scratch=[pltpu.VMEM((MID, inner), f32), pltpu.VMEM((MID, inner), f32)],
        name="mid",
        us=25.0,
    )(cot, w_out, taps, mask, *zs, *ys)


def branch_kernel(x_ref, m_ref, w_ref, out_ref):
    out_ref[...] = x_ref[...] + dot(m_ref[...], w_ref[...])


def branch(x, mixed, w_out):
    tokens, width = x.shape
    row = lambda n: pl.BlockSpec((WIDE, n), lambda g: (g, 0))
    return call(
        branch_kernel,
        struct(x.shape),
        grid=(tokens // WIDE,),
        in_specs=[row(width), row(mixed.shape[1]), whole(w_out.shape)],
        out_specs=row(width),
        name="branch",
        us=9.0,
    )(x, mixed, w_out)


def bwd_kernel(
    base, cin_ref, y_ref, dy_ref, taps_ref, ea_ref, eb_ref, cum_ref, cumt_ref, b_ref, c_ref, ct_ref, st_ref, mask_ref, h_ref,
    dcin_ref, grad_ref, dst_ref, db_ref, dc_ref, dcum_ref, ddt_ref, cs_scr, e_scr, et_scr,
):
    group = pl.program_id(0) + base
    tokens = cin_ref.shape[0]
    cs_scr[0:8, :] = jnp.zeros((8, GROUP), f32)
    cs_scr[pl.ds(8, tokens), :] = cin_ref[...].astype(f32)
    fill_spread(e_scr, group)
    row, col = iota((GROUP, 128), 0), iota((GROUP, 128), 1)
    et_scr[...] = jnp.where(col == 4 * group + row // 64, 1.0, 0.0).astype(bf16)
    taps = taps_ref[...]
    m_low, m_high = pair_masks()

    @pl.when(pl.program_id(0) == 0)
    def _():
        for ref in (dst_ref, db_ref, dc_ref, dcum_ref, ddt_ref):
            ref[...] = jnp.zeros(ref.shape, f32)

    def to_heads(v):
        hi = v.astype(bf16)
        lo = (v - hi.astype(f32)).astype(bf16)
        return dot(hi, et_scr[...]) + dot(lo, et_scr[...])

    blocks = tokens // BLOCK

    dstate = jnp.zeros((128, GROUP), f32)
    behind = jnp.zeros((8, GROUP), f32)
    totals = [jnp.zeros((8, GROUP), f32) for _ in range(6)]
    for k in reversed(range(blocks)):
        t0 = k * BLOCK
        more = k < blocks - 1
        rows = pl.ds(t0, BLOCK)
        mask = mask_ref[rows, :]
        conv, shifted = conv_block(cs_scr[pl.ds(t0, BLOCK + 8), :], mask, taps, 4)
        sig = sigmoid(conv)
        v = conv * sig
        ea = dot(ea_ref[rows, :], e_scr[:, : 2 * GROUP])
        wx = dot(eb_ref[rows, :], e_scr[:, 2 * GROUP :])
        dtx, ex = ea[:, :GROUP], ea[:, GROUP:]
        vd_low = (v * dtx).astype(bf16)
        vd = vd_low.astype(f32)
        dy_low = dy_ref[rows, :]
        dy = dy_low.astype(f32)
        skip = taps[5:6]
        h_low = h_ref[rows, :]
        if k > 0:
            dye = (dy * ex).astype(bf16)
            dc_ref[rows, :] += dot_nt(dye, h_low)
        if more:
            dh_low = dstate.astype(bf16)
            db_ref[rows, :] += dot_nt((vd * wx).astype(bf16), dh_low)
            dvd_end = dot(b_ref[rows, :], dh_low) * wx
        cums = pltpu.roll(cum_ref[rows, :], 128 - 4 * group, 1)
        st = st_ref[rows, :]
        inside = []
        dst = jnp.zeros((BLOCK, BLOCK), f32)
        for pair in range(2):
            cols = slice(pair * 128, pair * 128 + 128)
            decays, weights = [], []
            for j in (2 * pair, 2 * pair + 1):
                spread = cumt_ref[0, j : j + 1, rows] - cums[:, j : j + 1]
                decay = jnp.exp2(jnp.minimum(spread, 0.0))
                decays.append(decay)
                weights.append((decay * st).astype(bf16))
            dyp = dy_low[:, cols]
            stack = jnp.concatenate([dyp * m_low, dyp * m_high], axis=0)
            inside.append(dot(jnp.concatenate(weights, axis=1), stack))
            cross = dot_nt(vd_low[:, cols], stack)
            dst = dst + cross[:, :128] * decays[0] + cross[:, 128:] * decays[1]
        dst_ref[rows, :] += dst
        dvd = jnp.concatenate(inside, axis=1)
        through = ex[BLOCK - 1 :]
        if more:
            dvd = dvd + dvd_end
            ends = rows8(vd * dvd_end)
            if k > 0:
                ends = ends + through * rows8(dstate * h_low.astype(f32))
        p = dy * (y_ref[rows, :] - skip * v) - vd * dvd
        if more:
            p = jnp.concatenate([p[: BLOCK - 8], p[BLOCK - 8 :] + jnp.where(iota((8, 1), 0) == 7, jnp.sum(ends, axis=0, keepdims=True), 0.0)], axis=0)
        dcum_ref[rows, :] += to_heads(p)
        ddt_ref[rows, :] += to_heads(dvd * v)
        if k > 0:
            dstate = dstate * through + dot(ct_ref[:, rows], dye)
        dconv = (dvd * dtx + skip * dy) * (sig * (1.0 + conv * (1.0 - sig)))
        window = jnp.concatenate([dconv, behind], axis=0)
        behind = dconv[:8]
        for i, term in enumerate([*[dconv * shifted[3 - i] for i in range(4)], dconv, dy * v]):
            totals[i] = totals[i] + rows8(term)
        dcin_ref[rows, :] = conv_back(
            window, mask_ref[pl.ds(t0, BLOCK + 8), :], taps, 4
        ).astype(bf16)
    rows = [jnp.sum(t, axis=0, keepdims=True) for t in totals]
    grad_ref[...] = jnp.concatenate([*rows, jnp.zeros((2, GROUP), f32)], axis=0)


def bwd(base, count, cin, y, dy, taps, pre, h):
    tokens = cin.shape[0]
    full = lambda a: whole(a.shape)
    ea, eb, cum, cumt, b, c, ct, st, mask = pre
    local = lambda rows: pl.BlockSpec((rows, GROUP), lambda g: (0, g))
    global_ = lambda rows: pl.BlockSpec((rows, GROUP), lambda g: (0, base + g))
    wide = struct((tokens, 128))
    return call(
        functools.partial(bwd_kernel, base),
        [struct((tokens, count * GROUP), bf16), struct((8, count * GROUP))] + [wide] * 5,
        grid=(count,),
        in_specs=[
            local(tokens), local(tokens), global_(tokens), global_(8),
            full(ea), full(eb), full(cum),
            pl.BlockSpec((1, 4, tokens), lambda g: (base + g, 0, 0)),
            full(b), full(c), full(ct), full(st), full(mask), local(tokens),
        ],
        out_specs=[local(tokens), local(8)] + [whole(wide.shape)] * 5,
        scratch=[
            pltpu.VMEM((tokens + 8, GROUP), f32), pltpu.VMEM((128, 3 * GROUP), bf16), pltpu.VMEM((GROUP, 128), bf16),
        ],
        name=f"bwd{base}",
        us=count * 8.4,
    )(cin, y, dy, taps, ea, eb, cum, cumt, b, c, ct, st, mask, h)


def tail_kernel(sm, cin_ref, taps_ref, head_ref, b_ref, c_ref, step_ref, mask_ref, *refs):
    dp_ref, grad_ref, stat_ref, cs_scr, ds_scr = refs[-5:]
    sums = refs[:-5]
    tokens = cin_ref.shape[0]
    cs_scr[0:8, :] = jnp.zeros((8, 256), f32)
    cs_scr[pl.ds(8, tokens), :] = cin_ref[...].astype(f32)
    ds_scr[...] = jnp.zeros(ds_scr.shape, f32)
    taps = taps_ref[...]
    grad_ref[...] = jnp.zeros(grad_ref.shape, f32)
    stat_ref[...] = jnp.zeros(stat_ref.shape, f32)
    blocks = tokens // BLOCK

    def block(step, _):
        k = blocks - 1 - step
        t0 = pl.multiple_of(k * BLOCK, BLOCK)
        rows = pl.ds(t0, BLOCK)
        row, lane = iota((BLOCK, 128), 0), iota((BLOCK, 128), 1)
        dst_sum, db_sum, dc_sum, dcum_sum, ddt_sum = [
            functools.reduce(jnp.add, [ref[rows, :] for ref in sums[i::5]]) for i in range(5)
        ]
        keep = (lane >= row) & (scene_of(lane + t0, sm) == scene_of(row + t0, sm))
        dst = jnp.where(keep, dst_sum, 0.0).astype(bf16)
        db = db_sum + dot(dst, c_ref[rows, :])
        dc = dc_sum + dot_tn(dst, b_ref[rows, :])
        conv, shifted = conv_block(cs_scr[pl.ds(t0, BLOCK + 8), :], mask_ref[rows, :], taps, 4)
        sig = sigmoid(conv)
        dconv = jnp.concatenate([db, dc], axis=1) * (sig * (1.0 + conv * (1.0 - sig)))
        window = jnp.concatenate([dconv, ds_scr[...]], axis=0)
        ds_scr[...] = dconv[:8]
        grads = [jnp.sum(rows8(dconv * shifted[3 - i]), axis=0, keepdims=True) for i in range(4)]
        grads.append(jnp.sum(rows8(dconv), axis=0, keepdims=True))
        grads.append(jnp.zeros((3, 256), f32))
        grad_ref[...] += jnp.concatenate(grads, axis=0)
        dcin = conv_back(window, mask_ref[pl.ds(t0, BLOCK + 8), :], taps, 4)
        upper = jnp.where(lane >= row, 1.0, 0.0)
        dlog = jnp.dot(upper, dcum_sum, precision=highest, preferred_element_type=f32)
        step_in = step_ref[rows, :]
        dt = jnp.maximum(step_in, 0.0) + jnp.log1p(jnp.exp(-jnp.abs(step_in)))
        rate = head_ref[1:2, :]
        dstep = (ddt_sum - dlog * rate) * sigmoid(step_in)
        dalog = -dlog * dt * rate
        stat_ref[...] += jnp.concatenate(
            [
                jnp.sum(rows8(dstep), axis=0, keepdims=True),
                jnp.sum(rows8(dalog), axis=0, keepdims=True),
                jnp.zeros((6, 128), f32),
            ],
            axis=0,
        )
        dp_ref[rows, :] = jnp.concatenate([dcin, dstep], axis=1).astype(bf16)
        return 0

    lax.fori_loop(0, blocks, block, 0, unroll=True)


def tail(sm, cin, taps, inner, head, b, c, step, mask, sums):
    tokens = cin.shape[0]
    args = (cin, taps, head, b, c, step, mask, *sums)
    outs = [struct((tokens, 384), bf16), struct((8, 256)), struct((8, 128))]
    return call(
        tail_kernel,
        outs,
        in_specs=[SMEM] + [whole(a.shape) if a is not taps else bc_taps(inner) for a in args],
        out_specs=[whole(o.shape) for o in outs],
        scratch=[pltpu.VMEM((tokens + 8, 256), f32), pltpu.VMEM((8, 256), f32)],
        name="tail",
        us=8.0,
    )(sm, *args)


def term_kernel(tiles, add, into, sm, left_ref, *refs):
    out_ref = refs[-1]
    parts = refs[: len(tiles)]

    def product(part):
        value = dot(left_ref[...], part[...])
        if add:
            value = value + refs[len(tiles)][:, : part.shape[1]].astype(f32)
        out_ref[:, : part.shape[1]] = value.astype(bf16)

    first = 0
    for part, count in zip(parts, tiles):
        step = pl.program_id(0)
        pl.when((step >= first) & (step < first + count))(functools.partial(product, part))
        first += count


def in_term(half, left, parts, name, add=None, into=None, columns=None):
    halves, width, tokens = left.shape
    n = sum(p.shape[1] for p in parts)
    wide = min(512, n)
    tiles = [pl.cdiv(p.shape[1], wide) for p in parts]
    first = [sum(tiles[:i]) for i in range(len(parts))]
    total = n if columns is None else columns
    at = 0 if into is None else (total - n) // wide
    args = [left, *parts]
    specs = [pl.BlockSpec((None, width, tokens), lambda g, sm: (sm[0], 0, 0))] + [
        pl.BlockSpec(
            (tokens, min(wide, p.shape[1])),
            functools.partial(lambda f, c, g, sm: (0, jnp.clip(g - f, 0, c - 1)), f, c),
        )
        for p, f, c in zip(parts, first, tiles)
    ]
    if add is not None:
        args.append(add)
        specs.append(pl.BlockSpec((width, wide), lambda g, sm: (0, g)))
    aliases = {}
    if into is not None:
        aliases = {len(args) + 1: 0}
        args.append(into)
        specs.append(pl.BlockSpec(memory_space=pl.ANY))
    spec = pltpu.PrefetchScalarGridSpec(
        num_scalar_prefetch=1,
        grid=(sum(tiles),),
        in_specs=specs,
        out_specs=pl.BlockSpec((width, wide), lambda g, sm: (0, at + g)),
    )
    return pl.pallas_call(
        functools.partial(term_kernel, tiles, add is not None, into is not None),
        out_shape=struct((width, total), bf16),
        grid_spec=spec,
        name=name,
        input_output_aliases=aliases,
        compiler_params=pltpu.CompilerParams(vmem_limit_bytes=VMEM_LIMIT, dimension_semantics=("arbitrary",)),
        cost_estimate=cost(width * tokens * n * 5e-9),
    )(half, *args)


def out_kernel(add, sm, left_ref, right_ref, *refs):
    value = dot(left_ref[...], right_ref[...])
    if add:
        value = value + refs[0][...].astype(f32)
    refs[-1][...] = value.astype(bf16)


def out_term(ring, half, flip, cot_low, name, add=None, columns=None):
    inner, tokens = flip.shape
    width = cot_low.shape[1]
    rows = inner // 4
    left = flip.reshape(4, rows, tokens)
    steps = 2 if ring else 4
    out = pl.BlockSpec((rows, width), (lambda g, sm: (0, g)) if ring else (lambda g, sm: (g, 0)))
    args, specs = [left, cot_low], [
        pl.BlockSpec((None, rows, tokens), lambda g, sm: (sm[0] * 2 + g, 0, 0)),
        pl.BlockSpec(cot_low.shape, lambda g, sm: (0, 0)),
    ]
    if add is not None:
        args.append(add)
        specs.append(out)
    spec = pltpu.PrefetchScalarGridSpec(num_scalar_prefetch=1, grid=(steps,), in_specs=specs, out_specs=out)
    return pl.pallas_call(
        functools.partial(out_kernel, add is not None),
        out_shape=struct((rows, columns or 2 * width) if ring else (inner, width), bf16),
        grid_spec=spec,
        name=name,
        compiler_params=pltpu.CompilerParams(vmem_limit_bytes=VMEM_LIMIT, dimension_semantics=("arbitrary",)),
        cost_estimate=cost(5.0),
    )(half, *args)


def last_kernel(count, x_ref, cot_ref, gain_ref, *refs):
    ds, ws, dx_ref = refs[:count], refs[count : 2 * count], refs[-1]
    x = x_ref[...]
    width = x.shape[1]
    dn = functools.reduce(jnp.add, [dot_nt(d[...], w[...]) for d, w in zip(ds, ws)])
    r = lax.rsqrt(jnp.mean(x * x, axis=-1, keepdims=True) + EPS)
    u = dn * gain_ref[0:1, :]
    xr = x * r
    mu = jnp.sum(u * xr, axis=-1, keepdims=True) * (1.0 / width)
    dx_ref[...] = cot_ref[...] + r * (u - xr * mu)


def last(x, cot, gain, pairs):
    tokens, width = x.shape
    row = lambda n: pl.BlockSpec((WIDE, n), lambda g: (g, 0))
    ds, ws = zip(*pairs)
    n = sum(k for _, k, _ in ds)
    return call(
        functools.partial(last_kernel, len(pairs)),
        struct(x.shape),
        grid=(tokens // WIDE,),
        in_specs=[row(width), row(width), whole(gain.shape)]
        + [pl.BlockSpec((WIDE, k), functools.partial(lambda i, g: (g, i), i)) for _, k, i in ds]
        + [pl.BlockSpec((width, k), functools.partial(lambda i, g: (0, i), i)) for _, k, i in ws],
        out_specs=row(width),
        name="last",
        us=18.0,
    )(x, cot, gain, *[d[0] for d in ds], *[w[0] for w in ws])


Y, CORE, X, Z1, Z2 = 1, 2, 4, 8, 16


def exchange(a, bit):
    return lax.ppermute(a, AXES, [(i, i ^ bit) for i in range(SHARDS)])


def after(a, *others):
    return lax.optimization_barrier((a, *others))[0] if others else a


def together(arrays, *others):
    return list(lax.optimization_barrier((*arrays, *others))[: len(arrays)])


def join(a, got):
    return jnp.concatenate([a, got], axis=0)


def gather_z(own):
    two = join(own, exchange(own, Z1))
    return join(two, exchange(two, Z2))


def by_place(first, second, x_first):
    return [*first, *second] if x_first else [first[0], second[0], first[1], second[1]]


def gather_core(four):
    return [*four, *[exchange(a, CORE) for a in four]]


def take(a, bit, axis):
    return lax.dynamic_index_in_dim(a, bit, axis, keepdims=False)


def scatter_start(keep):
    return [Z2, Z1, X, Y], keep.reshape(2, 2, 2, 2, keep.shape[0] // 16, keep.shape[1])


def scatter_send(place, state, bit):
    names, left = state
    axis = names.index(bit)
    mine = jnp.where((place & bit) > 0, 1, 0)
    names = names[:axis] + names[axis + 1 :]
    return names, take(left, mine, axis), exchange(take(left, 1 - mine, axis), bit)


def scatter_add(sent, got=None):
    names, left, flight = sent
    left = left.astype(f32) + (flight if got is None else got).astype(f32)
    return names, left.astype(bf16) if names else left


def both(a, b):
    return (a.astype(f32) + b.astype(f32)).astype(bf16)


def pad_to(a, rows, columns):
    return jnp.pad(a, ((0, rows - a.shape[0]), (0, columns - a.shape[1])))


def local(
    ring, block_input, cotangent, scene_lengths, norm_gain, in_weight, conv_weight, conv_bias, dt_bias, a_log, skip_gain,
    gated_gain, out_weight,
):
    tokens, width = block_input.shape
    heads = a_log.shape[0]
    inner = out_weight.shape[0] * lax.axis_size(AXES)
    channels = conv_bias.shape[0] * lax.axis_size(AXES)
    proj = in_weight.shape[1]
    bc = proj - 2 * inner
    place = lax.axis_index(AXES).astype(jnp.int32)
    bounds = jnp.cumsum(scene_lengths[0]).astype(jnp.int32)
    sm = jnp.concatenate([bounds, place[None], jnp.zeros((4,), jnp.int32)])
    groups = inner // GROUP

    def pack(grads, gg, stat):
        d_skip = jnp.sum(grads[5, :inner].reshape(heads, -1), axis=1)
        side = jnp.concatenate([stat[0, :heads], stat[1, :heads], d_skip])[None]
        return jnp.concatenate([grads[:5], pad_to(jnp.sum(gg, axis=0)[None], 1, channels), pad_to(side, 2, channels)], axis=0)

    gather = lambda a: lax.all_gather(a.astype(bf16), AXES, axis=0, tiled=True)
    skip_row = jnp.repeat(skip_gain, inner // heads)[None]
    w_low = in_weight.astype(bf16)
    if ring:
        small = jnp.concatenate(
            [
                jnp.concatenate([norm_gain, gated_gain])[None],
                pad_to(conv_weight.T, 4, 96),
                pad_to(conv_bias[None], 27, 96),
            ],
            axis=0,
        )
        first = jnp.concatenate([w_low[:, 2 * inner :], small.astype(bf16)], axis=1)
        four = gather_z(first)
        two = [four, exchange(four, X)]
        pieces = gather_core(by_place(two, [exchange(a, Y) for a in two], True))
        w_bc, taps, gain = unpack(sm, pieces, skip_row, channels, width)
        wide = inner // 2
        owns = [
            jnp.concatenate([w_low[:, at : at + wide], w_low[:, inner + at : inner + at + wide]], axis=1)
            for at in (0, wide)
        ]
        four = after(gather_z(owns[0]), *pieces)
        sides = [four[:, :wide], four[:, wide:]]
        back = after(owns[1], four)
        *got, came = together([exchange(sides[0], X), exchange(sides[1], Y), exchange(back, Z1)], w_bc)
        front = [[a, b] for a, b in zip(sides, got)]
        back = join(back, came)
    else:
        in_full, out_full = gather(in_weight), gather(out_weight)
        norm_full, conv_full, bias_full, gated_full = map(gather, (norm_gain, conv_weight, conv_bias, gated_gain))
        gain = jnp.broadcast_to(norm_full.astype(f32)[None], (8, width))
        w_bc = pad_to(in_full[:, 2 * inner :], width, 384)
        taps = jnp.concatenate(
            [
                conv_full.astype(f32).T,
                bias_full.astype(f32)[None],
                pad_to(jnp.concatenate([skip_row, gated_full.astype(f32)[None]], axis=0), 3, channels),
            ],
            axis=0,
        )
    head = jnp.pad(jnp.stack([dt_bias, jnp.exp(a_log)]), ((0, 6), (0, 128 - heads)))
    (normed, normt, cin_bc, b, c, bt, ct, s, st, cum, cumt, ea, eb, step, mask) = prep(
        ring, sm, block_input, gain, w_bc, taps, inner, head, heads
    )
    pre = (ea, eb, cum, cumt, c, bt, s, mask)
    scan = lambda base, count, offset, *w: fwd(base, count, offset, ring, sm, normed, *w, inner, taps, pre)
    if ring:
        flights = [exchange(a, Y) for a in front[0]] + [exchange(a, X) for a in front[1]] + [exchange(back, Z2)]
        *got, came = together(flights, normed)
        front = [gather_core(by_place(front[0], got[:2], True)), gather_core(by_place(front[1], got[2:], False))]
        four = join(back, came)
        sides = [four[:, :wide], four[:, wide:]]
        out_full = gather(after(out_weight, four))
        got = [exchange(sides[0], X), exchange(sides[1], Y)]
        back = [[a, b] for a, b in zip(sides, got)]
        normed = after(normed, *got)
        half, quarter = groups // 2, groups // 4
        runs = [(0, quarter, scan(0, quarter, 0, *front))]
        flights = [exchange(a, Y) for a in back[0]] + [exchange(a, X) for a in back[1]]
        got = together(flights, runs[0][2][2])
        back = [gather_core(by_place(back[0], got[:2], True)), gather_core(by_place(back[1], got[2:], False))]
        runs.append((quarter, quarter, scan(quarter, quarter, quarter, *front)))
        parts = together([*back[0], *back[1]], runs[1][2][2])
        runs.append((half, half, scan(half, half, 0, parts[: len(PIECES)], parts[len(PIECES) :])))
    else:
        runs = [(0, groups, scan(0, groups, 0, [in_full], [in_full]))]
    mixed, dz, dy, gg, flip, cot_low = mid(
        ring, cotangent, out_full, taps, mask, [r[0] for *_, r in runs], [r[2] for *_, r in runs]
    )
    normt = normt.reshape(2 if ring else 1, -1, tokens)
    core = sm[3:4] >> 1 & 1
    if ring:
        sent = out_term(ring, 1 - core, flip, cot_low, "out_away")
        out_away = exchange(sent, CORE)
        sent = in_term(1 - core, normt, [after(dz, sent)], "gate_away")
        gate_away = exchange(sent, CORE)
        out_here = out_term(ring, core, flip, cot_low, "out_here", after(out_away, sent))
        gate_here = in_term(core, normt, [dz], "gate_here", after(gate_away, out_here))
        outs, gates = scatter_start(out_here), scatter_start(gate_here)
        dy = after(dy, gate_here)
    pre = (ea, eb, cum, cumt, b, c, ct, st, mask)
    scan = lambda dy, base, count, run: bwd(base, count, run[1], run[2], dy, taps, pre, run[3])
    finish = lambda sums: tail(sm, cin_bc, taps, inner, head, b, c, step, mask, sums)
    if ring:

        def term(parts, name):
            away = exchange(in_term(1 - core, normt, parts, name + "_away"), CORE)
            return scatter_start(both(in_term(core, normt, parts, name + "_here"), away))

        send = functools.partial(scatter_send, place)
        gates, outs = send(gates, X), send(outs, Y)
        back = scan(dy, *runs[2])
        one, two = together([gates[2], outs[2]], back[0])
        gates, outs = send(scatter_add(gates, one), Y), send(scatter_add(outs, two), X)
        near = scan(after(dy, gates[1], outs[1], back[0]), *runs[0])
        one, two = together([gates[2], outs[2]], near[0])
        gates, outs = scatter_add(gates, one), scatter_add(outs, two)
        early = send((gates[0], jnp.concatenate([gates[1], outs[1]], axis=-1)), Z2)
        parts = [near[0], after(back[0], early[1])]
        away = in_term(1 - core, normt, parts, "late_away")
        here = in_term(core, normt, parts, "late_here")
        late = send(scatter_start(both(here, exchange(away, CORE))), X)
        mid_out = scan(after(dy, late[1], near[0]), *runs[1])
        sums = [a for out in (back, near, mid_out) for a in out[2:]]
        (one,) = together([late[2]], mid_out[0])
        late = send(scatter_add(late, one), Y)
        sums[0] = after(sums[0], late[1])
        dbc, grad_bc, stat = finish(sums)
        grads = jnp.concatenate([near[1], mid_out[1], back[1], grad_bc], axis=1)
        one, two = together([early[2], late[2]], dbc)
        early, late = send(scatter_add(early, one), Z1), send(scatter_add(late, two), Z2)
        small = pack(grads, gg, stat)
        flight = exchange(small, CORE)
        parts = [mid_out[0], after(dbc, early[1], late[1], small)]
        away = in_term(1 - core, normt, parts, "last_away")
        here = in_term(core, normt, parts, "last_here")
        one, two, flight = together([early[2], late[2], flight], here)
        early, late, small = scatter_add(early, one), send(scatter_add(late, two), Z1), small + flight
        flight = exchange(small, X)
        final = send(scatter_start(both(here, exchange(away, CORE))), X)
        x_last = after(block_input, final[1], small, late[1])
        pairs = []
        for (base, count, run), (dv, *_) in zip(runs, (near, mid_out, back)):
            wide = count * GROUP
            pairs.append(((dz, wide, base // count), (run[4], wide, 0)))
            pairs.append(((dv, wide, 0), (run[5], wide, 0)))
        x_last = after(block_input, final[1], small, late[1])
    else:
        scatter = lambda a: lax.psum_scatter(a.astype(f32), AXES, scatter_dimension=0, tiled=True)
        dv, grad, *sums = scan(dy, *runs[0])
        dbc, grad_bc, stat = finish(sums)
        grads = jnp.concatenate([grad, grad_bc], axis=1)
        in_grad = scatter(in_term(core * 0, normt, [dz, dv, dbc], "all")[:, :proj])
        out_grad = scatter(out_term(ring, core * 0, flip, cot_low, "out"))
        pairs = [((dz, inner, 0), (in_full, inner, 0)), ((dv, inner, 0), (in_full, inner, 1))]
        x_last = block_input
    pairs.append(((dbc, 384, 0), (w_bc, 384, 0)))
    input_grad = last(x_last, cotangent, gain, pairs)
    if ring:
        one, two, flight = together([late[2], final[2], flight], input_grad)
        late, final, small = scatter_add(late, one), send(scatter_add(final, two), Y), small + flight
        flight = exchange(small, Y)
        mixed = after(mixed, final[1], small)
    block_output = branch(block_input, mixed, out_full)
    if ring:
        one, flight = together([final[2], flight], block_output)
        final, small = send(scatter_add(final, one), Z2), small + flight
        small = small + exchange(small, Z1)
        final = scatter_add(send(scatter_add(final), Z1))
        small = small + exchange(small, Z2)
        gate_grad, out_grad = early[1][:, :inner], early[1][:, inner:]
        out_grad = jnp.concatenate([out_grad[:, :width], out_grad[:, width:]], axis=0)
        near, half = inner // 4, inner // 2
        in_grad = jnp.concatenate(
            [gate_grad, late[1][:, :near], final[1][:, :near], late[1][:, near:], final[1][:, near : near + bc]], axis=1
        )
    else:
        small = lax.psum(pack(grads, gg, stat), AXES)
    d_gain = jnp.sum(in_grad * w_low.astype(f32), axis=1) / norm_gain.astype(bf16).astype(f32)
    part = lambda row, n: lax.dynamic_slice_in_dim(row, place * n, n, axis=-1)
    side = small[6]
    return (
        block_output,
        input_grad,
        d_gain,
        in_grad,
        part(small[:4], conv_bias.shape[0]).T,
        part(small[4], conv_bias.shape[0]),
        side[:heads],
        side[heads : 2 * heads],
        side[2 * heads : 3 * heads],
        part(small[5], gated_gain.shape[0]),
        out_grad,
    )


def solution(mesh):
    dp, fsdp = mesh.devices.shape
    split = jax.sharding.Mesh(mesh.devices.reshape(dp // 2, 2, fsdp), AXES)
    row = P(AXES, None)
    flat = P(AXES)
    return jax.shard_map(
        functools.partial(local, (dp, fsdp) == (16, 2)),
        mesh=split,
        in_specs=(row, row, row, flat, row, row, flat, P(), P(), P(), flat, row),
        out_specs=(row, row, flat, row, row, flat, P(), P(), P(), flat, row),
        check_vma=False,
    )
```

```python
import functools

import jax
import jax.numpy as jnp
from jax import lax
from jax.experimental import pallas as pl
from jax.experimental.pallas import tpu as pltpu
from jax.sharding import PartitionSpec as P

AXES = ("chip", "core", "fsdp")
CHIPS = ("chip", "fsdp")
SHARDS = 32
PIECES = 2
BLOCK = 128
GROUP = 256
EPS = 1e-05
LOG2E = 1.4426950408889634
VMEM_LIMIT = 50 * 1024 * 1024
VMEM_LARGE = 60 * 1024 * 1024
f32 = jnp.float32
bf16 = jnp.bfloat16
highest = lax.Precision.HIGHEST


def dot(a, b):
    return jnp.dot(a, b, preferred_element_type=f32)


def dot_nt(a, b):
    return lax.dot_general(a, b, (((1,), (1,)), ((), ())), preferred_element_type=f32)


def dot_tn(a, b):
    return lax.dot_general(a, b, (((0,), (0,)), ((), ())), preferred_element_type=f32)


def sigmoid(v):
    return 0.5 * jnp.tanh(0.5 * v) + 0.5


def iota(shape, axis):
    return lax.broadcasted_iota(jnp.int32, shape, axis)


def rows8(v):
    return jnp.sum(v.reshape(v.shape[0] // 8, 8, v.shape[1]), axis=0)


def scene_of(place, sm):
    scene = jnp.zeros(place.shape, jnp.int32)
    for i in range(3):
        scene = scene + jnp.where(place >= sm[i], 1, 0)
    return scene


def cost(us):
    return pl.CostEstimate(flops=0, bytes_accessed=int(us * 3.69e6), transcendentals=0)


def call(kernel, out, grid=None, in_specs=None, out_specs=None, scratch=(), name=None, us=1.0, aliases=None, vmem=VMEM_LIMIT):
    return pl.pallas_call(
        kernel,
        out_shape=out,
        grid=grid or (1,),
        in_specs=in_specs,
        out_specs=out_specs,
        scratch_shapes=scratch,
        name=name,
        compiler_params=pltpu.CompilerParams(
            vmem_limit_bytes=vmem, dimension_semantics=("arbitrary",)
        ),
        cost_estimate=cost(us),
        input_output_aliases=aliases or {},
    )


def whole(shape):
    return pl.BlockSpec(shape, lambda g: (0,) * len(shape))


def bc_taps(inner):
    return pl.BlockSpec((8, 256), lambda g: (0, inner // 256))


SMEM = pl.BlockSpec(memory_space=pltpu.SMEM)


def struct(shape, dtype=f32):
    return jax.ShapeDtypeStruct(shape, dtype)


def conv_block(window, masks, taps, width):
    current = window[8:]
    total = taps[4:5] + current * taps[3:4]
    shifted = [current]
    for off in range(1, width):
        moved = window[8 - off : 8 - off + BLOCK] * masks[:, off - 1 : off]
        shifted.append(moved)
        total = total + moved * taps[width - 1 - off : width - off]
    return total, shifted


def conv_back(window, masks, taps, width):
    total = window[:BLOCK] * taps[width - 1 : width]
    for off in range(1, width):
        moved = pltpu.roll(window * masks[:, off - 1 : off], window.shape[0] - off, 0)[:BLOCK]
        total = total + moved * taps[width - 1 - off : width - off]
    return total


def unpack_kernel(sm, *refs):
    pieces, (skip_ref, w_ref, taps_ref, gain_ref) = refs[:PIECES], refs[PIECES:]
    assemble(sm, pieces, w_ref, 32, True)
    row, col = iota((8 * SHARDS, 32 * SHARDS), 0), iota((8 * SHARDS, 32 * SHARDS), 1)
    pick = jnp.where(col == (row & (SHARDS - 1)) * 32 + row // SHARDS, 1.0, 0.0).astype(bf16)
    packed = dot(pick, w_ref[:, 256:384]).astype(bf16)

    def spread(kind, lane, size):
        total = size * SHARDS
        place = iota((1, total), 1)
        owner, within = place // size, place % size
        copy = jnp.where(iota((128, total), 0) == within + lane, 1.0, 0.0).astype(bf16)
        values = dot(packed[kind * SHARDS : (kind + 1) * SHARDS, :], copy)
        return jnp.sum(jnp.where(iota((SHARDS, total), 0) == owner, values, 0.0), axis=0, keepdims=True)

    taps_ref[...] = jnp.zeros(taps_ref.shape, f32)
    gain_ref[...] = jnp.broadcast_to(spread(0, 32, 32), gain_ref.shape)
    inner = skip_ref.shape[1]
    taps_ref[6:7, :inner] = spread(0, 64, inner // SHARDS)
    channels = taps_ref.shape[1]
    for k in range(5):
        taps_ref[k : k + 1, :] = spread(k + 1, 32, channels // SHARDS)
    taps_ref[5:6, :inner] = skip_ref[0:1, :]


def unpack(sm, pieces, skip, channels, width):
    outs = [struct((width, 384), bf16), struct((8, channels)), struct((8, width))]
    return call(
        unpack_kernel,
        outs,
        in_specs=[SMEM] + [whole(a.shape) for a in (*pieces, skip)],
        out_specs=[whole(o.shape) for o in outs],
        name="unpack",
        us=3.0,
    )(sm, *pieces, skip)


def core_first(shard):
    return (shard >> 1 & 1) * 16 + (shard >> 2) * 2 + (shard & 1)


def prep_kernel(
    ring, sm, x_ref, gain_ref, w_ref, taps_ref, head_ref,
    normed_ref, normt_ref, cin_ref, b_ref, c_ref, bt_ref, ct_ref, s_ref, st_ref,
    cum_ref, cumt_ref, ea_ref, eb_ref, step_ref, mask_ref, cs_scr,
):
    tokens = x_ref.shape[0]
    x = x_ref[...]
    scale = lax.rsqrt(jnp.mean(x * x, axis=-1, keepdims=True) + EPS)
    normed_low = (x * scale * gain_ref[0:1, :]).astype(bf16)
    normed_ref[...] = normed_low
    flipped = normed_low.astype(f32).T.astype(bf16)
    if ring:
        for shard in range(SHARDS):
            at = core_first(shard) * 32
            normt_ref[at : at + 32, :] = flipped[shard * 32 : shard * 32 + 32, :]
    else:
        normt_ref[...] = flipped
    proj = dot(normed_low, w_ref[...])
    lanes = iota((1, 128), 1)
    heads = 4 * cumt_ref.shape[0]
    is_head = lanes < heads
    cin_low = proj[:, :256].astype(bf16)
    cin_ref[...] = cin_low
    cs_scr[0:8, :] = jnp.zeros((8, 256), f32)
    cs_scr[pl.ds(8, tokens), :] = cin_low.astype(f32)
    step_ref[...] = jnp.where(is_head, proj[:, 256:384] + head_ref[0:1, :], 0.0)
    taps = taps_ref[...]

    for k in range(tokens // BLOCK):
        t0 = k * BLOCK
        rows = pl.ds(t0, BLOCK)
        place = iota((BLOCK, 128), 0) + t0
        lane = iota((BLOCK, 128), 1)
        scene = scene_of(place, sm)
        before = place - lane - 1
        same = (before >= 0) & (scene_of(before, sm) == scene)
        mask = jnp.where(lane < 3, jnp.where(same, 1.0, 0.0), jnp.where(place < sm[2], 1.0, 0.0))
        mask_ref[rows, :] = mask
        conv, _ = conv_block(cs_scr[pl.ds(t0, BLOCK + 8), :], mask, taps, 4)
        act = conv * sigmoid(conv)
        b_low = act[:, :128].astype(bf16)
        c_low = act[:, 128:].astype(bf16)
        b_ref[rows, :] = b_low
        c_ref[rows, :] = c_low
        bt_ref[:, rows] = act[:, :128].T.astype(bf16)
        ct_ref[:, rows] = act[:, 128:].T.astype(bf16)
        other = scene_of(lane + t0, sm)
        low = (lane + t0 <= place) & (other == scene)
        s_ref[rows, :] = jnp.where(low, dot_nt(c_low, b_low), 0.0)
        high = (lane + t0 >= place) & (other == scene)
        st_ref[rows, :] = jnp.where(high, dot_nt(b_low, c_low), 0.0)
        step = step_ref[rows, :]
        dt = jnp.maximum(step, 0.0) + jnp.log1p(jnp.exp(-jnp.abs(step)))
        dt = jnp.where(is_head, dt, 0.0)
        log_decay = dt * (head_ref[1:2, :] * -LOG2E)
        lower = jnp.where(lane <= iota((BLOCK, 128), 0), 1.0, 0.0)
        cum = jnp.dot(lower, log_decay, precision=highest, preferred_element_type=f32)
        cum_ref[rows, :] = cum
        flat = cum.T
        for i in range(heads // 4):
            cumt_ref[i, :, rows] = flat[4 * i : 4 * i + 4, :]
        first = jnp.full((1, 128), t0 - 1, jnp.int32)
        last = jnp.full((1, 128), t0 + BLOCK - 1, jnp.int32)
        entering = (scene_of(first, sm) == scene) & (first >= 0) & is_head
        final = (scene_of(last, sm) == scene) & is_head
        grow = jnp.where(entering, jnp.exp2(cum), 0.0)
        end = jnp.where(final, jnp.exp2(cum[BLOCK - 1 :] - cum), 0.0)

        def packed(v):
            hi = v.astype(bf16).astype(f32)
            return hi + pltpu.roll((v - hi).astype(bf16).astype(f32), 32, 1)

        ea_ref[rows, :] = (packed(dt) + pltpu.roll(packed(grow), 64, 1)).astype(bf16)
        eb_ref[rows, :] = packed(end).astype(bf16)
    mask_ref[pl.ds(tokens, 8), :] = jnp.zeros((8, 128), f32)


def prep(ring, sm, x, gain, w_bc, taps, inner, head, heads):
    tokens, width = x.shape
    wide = (tokens, 128)
    outs = [
        struct(x.shape, bf16), struct((width, tokens), bf16), struct((tokens, 256), bf16),
        struct(wide, bf16), struct(wide, bf16), struct((128, tokens), bf16), struct((128, tokens), bf16),
        struct(wide), struct(wide), struct(wide), struct((heads // 4, 4, tokens)), struct(wide, bf16), struct(wide, bf16),
        struct(wide), struct((tokens + 8, 128)),
    ]
    args = (x, gain, w_bc, taps, head)
    return call(
        functools.partial(prep_kernel, ring),
        outs,
        in_specs=[SMEM] + [whole(a.shape) if a is not taps else bc_taps(inner) for a in args],
        out_specs=[whole(o.shape) for o in outs],
        scratch=[pltpu.VMEM((tokens + 8, 256), f32)],
        name="prep",
        us=13.0,
    )(sm, *args)


def fill_spread(e_scr, group):
    row = iota((128, 768), 0)
    col = iota((128, 768), 1)
    head = 4 * group + (col % GROUP) // 64
    part = jnp.where(col < GROUP, 0, jnp.where(col < 2 * GROUP, 64, 0))
    hit = (row == head + part) | (row == head + part + 32)
    e_scr[...] = jnp.where(hit, 1.0, 0.0).astype(bf16)


def pair_masks():
    low = jnp.where(iota((1, 128), 1) < 64, 1.0, 0.0).astype(bf16)
    high = jnp.where(iota((1, 128), 1) < 64, 0.0, 1.0).astype(bf16)
    return low, high


def assemble(sm, pieces, out_ref, block, x_first, columns=slice(None)):
    low, high = (4, 1) if x_first else (1, 4)
    for core, piece in enumerate(pieces):
        for j in range(SHARDS // 2):
            shard = sm[3] ^ (core << 1 | (j & 3) << 3 | (j >> 2 & 1) * low | (j >> 3) * high)
            out_ref[pl.ds(pl.multiple_of(shard * block, block), block), columns] = piece[j * block : (j + 1) * block, :]


def fwd_kernel(*refs):
    base, ring, into, sm = refs[:4]
    refs = refs[1:]
    if ring:
        n = PIECES
        gates, values = refs[3 : 3 + n], refs[3 + n : 3 + 2 * n]
        rest = list(refs[3 + 2 * n :])
        if into:
            del rest[10:16]
        wv_ref, wg_ref = rest.pop(15), rest.pop(14)
        assemble(sm, gates, wg_ref, 32, True)
        assemble(sm, values, wv_ref, 32, False)
        rest[1:1] = [wg_ref, wv_ref]
    else:
        rest = list(refs[5:])
        rest[1:1] = refs[3:5]
    fwd_body(base, *rest)


def fwd_body(
    base, normed_ref, wg_ref, wv_ref, taps_ref, ea_ref, eb_ref, cum_ref, cumt_ref, c_ref, bt_ref, s_ref, mask_ref,
    z_ref, cin_ref, y_ref, h_ref, cs_scr, e_scr, x_scr,
):
    group = pl.program_id(0) + base
    tokens = normed_ref.shape[0]
    normed = normed_ref[...]
    z_ref[...] = dot(normed, wg_ref[...]).astype(bf16)
    cin_low = dot(normed, wv_ref[...]).astype(bf16)
    cin_ref[...] = cin_low
    cs_scr[0:8, :] = jnp.zeros((8, GROUP), f32)
    cs_scr[pl.ds(8, tokens), :] = cin_low.astype(f32)
    fill_spread(e_scr, group)
    x_scr[:, : 2 * GROUP] = dot(ea_ref[...], e_scr[:, : 2 * GROUP])
    x_scr[:, 2 * GROUP :] = dot(eb_ref[...], e_scr[:, 2 * GROUP :])
    taps = taps_ref[...]
    m_low, m_high = pair_masks()

    state = jnp.zeros((128, GROUP), f32)
    blocks = tokens // BLOCK
    for k in range(blocks):
        t0 = k * BLOCK
        rows = pl.ds(t0, BLOCK)
        mask = mask_ref[rows, :]
        conv, _ = conv_block(cs_scr[pl.ds(t0, BLOCK + 8), :], mask, taps, 4)
        v = conv * sigmoid(conv)
        dtx, ex, wx = [x_scr[rows, i * GROUP : (i + 1) * GROUP] for i in range(3)]
        vd_low = (v * dtx).astype(bf16)
        h_low = state.astype(bf16)
        h_ref[rows, :] = h_low
        cums = pltpu.roll(cum_ref[rows, :], 128 - 4 * group, 1)
        s = s_ref[rows, :]
        inside = []
        for pair in range(2):
            weights = []
            for j in (2 * pair, 2 * pair + 1):
                spread = cums[:, j : j + 1] - cumt_ref[0, j : j + 1, rows]
                weights.append((jnp.exp2(jnp.minimum(spread, 0.0)) * s).astype(bf16))
            vp = vd_low[:, pair * 128 : pair * 128 + 128]
            stack = jnp.concatenate([vp * m_low, vp * m_high], axis=0)
            inside.append(dot(jnp.concatenate(weights, axis=1), stack))
        y = jnp.concatenate(inside, axis=1) + taps[5:6] * v
        if k > 0:
            y = y + dot(c_ref[rows, :], h_low) * ex
        y_ref[rows, :] = y
        if k < blocks - 1:
            fresh = dot(bt_ref[:, rows], (vd_low.astype(f32) * wx).astype(bf16))
            state = state * ex[BLOCK - 1 :] + fresh


def fwd(base, count, offset, ring, sm, normed, gates, values, inner, taps, pre, total=None, into=()):
    tokens, width = normed.shape
    full = lambda a: whole(a.shape)
    ea, eb, cum, cumt, c, bt, s, mask = pre
    first = inner // GROUP
    at = (total or count) - count if into else 0
    col = lambda rows, dtype: struct((rows, (total or count) * GROUP), dtype)
    block = lambda rows: pl.BlockSpec((rows, GROUP), lambda g: (0, at + g))
    outs = [col(tokens, bf16), col(tokens, bf16), col(tokens, f32), col(tokens, bf16)]
    if ring:
        w_specs = [pl.BlockSpec((a.shape[0], GROUP), lambda g: (0, offset + g)) for a in (*gates, *values)]
        outs += [col(width, bf16)] * 2
    else:
        w_specs = [
            pl.BlockSpec((width, GROUP), lambda g: (0, base + g)),
            pl.BlockSpec((width, GROUP), lambda g: (0, first + base + g)),
        ]
    return call(
        functools.partial(fwd_kernel, base, ring, bool(into)),
        outs,
        grid=(count,),
        in_specs=[SMEM] + w_specs + [
            full(normed),
            pl.BlockSpec((8, GROUP), lambda g: (0, base + g)),
            full(ea), full(eb), full(cum),
            pl.BlockSpec((1, 4, tokens), lambda g: (base + g, 0, 0)),
            full(c), full(bt), full(s), full(mask),
        ] + [pl.BlockSpec(memory_space=pl.ANY)] * len(into),
        out_specs=[block(o.shape[0]) for o in outs],
        aliases={11 + 2 * len(gates) + i: i for i in range(len(into))},
        scratch=[pltpu.VMEM((tokens + 8, GROUP), f32), pltpu.VMEM((128, 3 * GROUP), bf16), pltpu.VMEM((tokens, 3 * GROUP), f32)],
        name=f"fwd{base}",
        us=count * 6.6,
    )(sm, *gates, *values, normed, taps, ea, eb, cum, cumt, c, bt, s, mask, *into)


MID = 256
WIDE = 512
MID_C = 512


def mid_kernel(ring, chunks, sm, cot_ref, taps_ref, mask_ref, *refs):
    zs, ys = refs[:chunks], refs[chunks : 2 * chunks]
    *pieces, mixed_ref, dz_ref, dy_ref, gg_ref, flip_ref, low_ref, w_ref, g_scr, u_scr = refs[2 * chunks :]
    if not ring:
        pieces, w_ref = [], pieces[0]
    half = w_ref.shape[1] // 2

    @pl.when(pl.program_id(0) == 0)
    def _():
        gg_ref[...] = jnp.zeros(gg_ref.shape, f32)
        if ring:
            assemble(sm, pieces[:PIECES], w_ref, 64, True, slice(0, half))
            assemble(sm, pieces[PIECES:], w_ref, 64, False, slice(half, 2 * half))

    inner = dz_ref.shape[1]
    alive = mask_ref[:, 3:4]
    cot_low = cot_ref[...].astype(bf16)
    low_ref[...] = cot_low
    square = jnp.zeros((MID, 128), f32)
    parts = [slice(i, i + MID_C) for i in range(0, inner, MID_C)]
    here = [(z, y, slice(i, i + MID_C)) for z, y in zip(zs, ys) for i in range(0, z.shape[1], MID_C)]
    for part, (z_ref, y_ref, cut) in zip(parts, here):
        z = z_ref[:, cut].astype(f32)
        g = y_ref[:, cut] * (z * sigmoid(z))
        g_scr[:, part] = g
        sq = g * g
        for i in range(0, MID_C, 128):
            square = square + sq[:, i : i + 128]
    r = lax.rsqrt(jnp.sum(square, axis=-1, keepdims=True) * (1.0 / inner) + EPS)
    r_alive = r * alive
    cross = jnp.zeros((MID, 128), f32)
    for part in parts:
        gain = taps_ref[6:7, part]
        dm = dot_nt(cot_low, w_ref[part, :])
        g = g_scr[:, part]
        u = dm * gain
        u_scr[:, part] = u
        ug = u * g
        for i in range(0, MID_C, 128):
            cross = cross + ug[:, i : i + 128]
        gr = g * r_alive
        mixed = gr * gain
        mixed_ref[:, part] = mixed.astype(bf16)
        gg_ref[:, part] += rows8(dm * gr)
        flipped = mixed.T.astype(bf16)
        for i in range(0, MID_C, 32):
            shard, half = (part.start + i) // 64, i // 32 % 2
            place = core_first(shard) // 16 * 32 + half * 16 + core_first(shard) % 16 if ring else (part.start + i) // 32
            flip_ref[place * 32 : place * 32 + 32, :] = flipped[i : i + 32, :]
    r3 = r_alive * r * r * (jnp.sum(cross, axis=-1, keepdims=True) * (1.0 / inner))
    for part, (z_ref, y_ref, cut) in zip(parts, here):
        z = z_ref[:, cut].astype(f32)
        sig = sigmoid(z)
        dg = u_scr[:, part] * r_alive - g_scr[:, part] * r3
        silu = z * sig
        dy_ref[:, part] = (dg * silu).astype(bf16)
        dz_ref[:, part] = (dg * y_ref[:, cut] * (sig + silu * (1.0 - sig))).astype(bf16)


def mid(ring, sm, cot, pieces, inner, taps, mask, zs, ys):
    tokens, width = cot.shape
    row = lambda n: pl.BlockSpec((MID, n), lambda g: (g, 0))
    wide = struct((tokens, inner), bf16)
    outs = [wide, wide, wide, struct((8, inner)), struct((inner, tokens), bf16), struct(cot.shape, bf16)]
    outs.append(struct((inner, width) if ring else (8, 128), bf16))
    return call(
        functools.partial(mid_kernel, ring, len(zs)),
        outs,
        grid=(tokens // MID,),
        in_specs=[SMEM, row(width), whole(taps.shape), row(128)]
        + [row(a.shape[1]) for a in (*zs, *ys)]
        + [whole(a.shape) for a in pieces],
        out_specs=[row(inner)] * 3 + [whole((8, inner)), pl.BlockSpec((inner, MID), lambda g: (0, g)), row(width), whole(outs[-1].shape)],
        scratch=[pltpu.VMEM((MID, inner), f32), pltpu.VMEM((MID, inner), f32)],
        name="mid",
        us=25.0,
        vmem=VMEM_LARGE,
    )(sm, cot, taps, mask, *zs, *ys, *pieces)


def branch_kernel(x_ref, m_ref, w_ref, out_ref):
    out_ref[...] = x_ref[...] + dot(m_ref[...], w_ref[...])


def branch(x, mixed, w_out):
    tokens, width = x.shape
    row = lambda n: pl.BlockSpec((WIDE, n), lambda g: (g, 0))
    return call(
        branch_kernel,
        struct(x.shape),
        grid=(tokens // WIDE,),
        in_specs=[row(width), row(mixed.shape[1]), whole(w_out.shape)],
        out_specs=row(width),
        name="branch",
        us=9.0,
    )(x, mixed, w_out)


def bwd_kernel(
    base, cin_ref, y_ref, dy_ref, taps_ref, ea_ref, eb_ref, cum_ref, cumt_ref, b_ref, c_ref, ct_ref, st_ref, mask_ref, h_ref,
    dcin_ref, grad_ref, dst_ref, db_ref, dc_ref, dcum_ref, ddt_ref, cs_scr, e_scr, et_scr,
):
    group = pl.program_id(0) + base
    tokens = cin_ref.shape[0]
    cs_scr[0:8, :] = jnp.zeros((8, GROUP), f32)
    cs_scr[pl.ds(8, tokens), :] = cin_ref[...].astype(f32)
    fill_spread(e_scr, group)
    row, col = iota((GROUP, 128), 0), iota((GROUP, 128), 1)
    et_scr[...] = jnp.where(col == 4 * group + row // 64, 1.0, 0.0).astype(bf16)
    taps = taps_ref[...]
    m_low, m_high = pair_masks()

    @pl.when(pl.program_id(0) == 0)
    def _():
        for ref in (dst_ref, db_ref, dc_ref, dcum_ref, ddt_ref):
            ref[...] = jnp.zeros(ref.shape, f32)

    def to_heads(v):
        hi = v.astype(bf16)
        lo = (v - hi.astype(f32)).astype(bf16)
        return dot(hi, et_scr[...]) + dot(lo, et_scr[...])

    blocks = tokens // BLOCK

    dstate = jnp.zeros((128, GROUP), f32)
    behind = jnp.zeros((8, GROUP), f32)
    totals = [jnp.zeros((8, GROUP), f32) for _ in range(6)]
    for k in reversed(range(blocks)):
        t0 = k * BLOCK
        more = k < blocks - 1
        rows = pl.ds(t0, BLOCK)
        mask = mask_ref[rows, :]
        conv, shifted = conv_block(cs_scr[pl.ds(t0, BLOCK + 8), :], mask, taps, 4)
        sig = sigmoid(conv)
        v = conv * sig
        ea = dot(ea_ref[rows, :], e_scr[:, : 2 * GROUP])
        wx = dot(eb_ref[rows, :], e_scr[:, 2 * GROUP :])
        dtx, ex = ea[:, :GROUP], ea[:, GROUP:]
        vd_low = (v * dtx).astype(bf16)
        vd = vd_low.astype(f32)
        dy_low = dy_ref[rows, :]
        dy = dy_low.astype(f32)
        skip = taps[5:6]
        h_low = h_ref[rows, :]
        if k > 0:
            dye = (dy * ex).astype(bf16)
            dc_ref[rows, :] += dot_nt(dye, h_low)
        if more:
            dh_low = dstate.astype(bf16)
            db_ref[rows, :] += dot_nt((vd * wx).astype(bf16), dh_low)
            dvd_end = dot(b_ref[rows, :], dh_low) * wx
        cums = pltpu.roll(cum_ref[rows, :], 128 - 4 * group, 1)
        st = st_ref[rows, :]
        inside = []
        dst = jnp.zeros((BLOCK, BLOCK), f32)
        for pair in range(2):
            cols = slice(pair * 128, pair * 128 + 128)
            decays, weights = [], []
            for j in (2 * pair, 2 * pair + 1):
                spread = cumt_ref[0, j : j + 1, rows] - cums[:, j : j + 1]
                decay = jnp.exp2(jnp.minimum(spread, 0.0))
                decays.append(decay)
                weights.append((decay * st).astype(bf16))
            dyp = dy_low[:, cols]
            stack = jnp.concatenate([dyp * m_low, dyp * m_high], axis=0)
            inside.append(dot(jnp.concatenate(weights, axis=1), stack))
            cross = dot_nt(vd_low[:, cols], stack)
            dst = dst + cross[:, :128] * decays[0] + cross[:, 128:] * decays[1]
        dst_ref[rows, :] += dst
        dvd = jnp.concatenate(inside, axis=1)
        through = ex[BLOCK - 1 :]
        if more:
            dvd = dvd + dvd_end
            ends = rows8(vd * dvd_end)
            if k > 0:
                ends = ends + through * rows8(dstate * h_low.astype(f32))
        p = dy * (y_ref[rows, :] - skip * v) - vd * dvd
        if more:
            p = jnp.concatenate([p[: BLOCK - 8], p[BLOCK - 8 :] + jnp.where(iota((8, 1), 0) == 7, jnp.sum(ends, axis=0, keepdims=True), 0.0)], axis=0)
        dcum_ref[rows, :] += to_heads(p)
        ddt_ref[rows, :] += dot((dvd * v).astype(bf16), et_scr[...])
        if k > 0:
            dstate = dstate * through + dot(ct_ref[:, rows], dye)
        dconv = (dvd * dtx + skip * dy) * (sig * (1.0 + conv * (1.0 - sig)))
        window = jnp.concatenate([dconv, behind], axis=0)
        behind = dconv[:8]
        for i, term in enumerate([*[dconv * shifted[3 - i] for i in range(4)], dconv, dy * v]):
            totals[i] = totals[i] + rows8(term)
        dcin_ref[rows, :] = conv_back(
            window, mask_ref[pl.ds(t0, BLOCK + 8), :], taps, 4
        ).astype(bf16)
    rows = [jnp.sum(t, axis=0, keepdims=True) for t in totals]
    grad_ref[...] = jnp.concatenate([*rows, jnp.zeros((2, GROUP), f32)], axis=0)


def bwd(base, count, cin, y, dy, taps, pre, h):
    tokens = cin.shape[0]
    full = lambda a: whole(a.shape)
    ea, eb, cum, cumt, b, c, ct, st, mask = pre
    local = lambda rows: pl.BlockSpec((rows, GROUP), lambda g: (0, g))
    global_ = lambda rows: pl.BlockSpec((rows, GROUP), lambda g: (0, base + g))
    wide = struct((tokens, 128))
    return call(
        functools.partial(bwd_kernel, base),
        [struct((tokens, count * GROUP), bf16), struct((8, count * GROUP))] + [wide] * 5,
        grid=(count,),
        in_specs=[
            local(tokens), local(tokens), global_(tokens), global_(8),
            full(ea), full(eb), full(cum),
            pl.BlockSpec((1, 4, tokens), lambda g: (base + g, 0, 0)),
            full(b), full(c), full(ct), full(st), full(mask), local(tokens),
        ],
        out_specs=[local(tokens), local(8)] + [whole(wide.shape)] * 5,
        scratch=[
            pltpu.VMEM((tokens + 8, GROUP), f32), pltpu.VMEM((128, 3 * GROUP), bf16), pltpu.VMEM((GROUP, 128), bf16),
        ],
        name=f"bwd{base}",
        us=count * 8.4,
    )(cin, y, dy, taps, ea, eb, cum, cumt, b, c, ct, st, mask, h)


def tail_kernel(sm, cin_ref, taps_ref, head_ref, b_ref, c_ref, step_ref, mask_ref, *refs):
    dp_ref, grad_ref, stat_ref, cs_scr, ds_scr = refs[-5:]
    sums = refs[:-5]
    tokens = cin_ref.shape[0]
    cs_scr[0:8, :] = jnp.zeros((8, 256), f32)
    cs_scr[pl.ds(8, tokens), :] = cin_ref[...].astype(f32)
    ds_scr[...] = jnp.zeros(ds_scr.shape, f32)
    taps = taps_ref[...]
    grad_ref[...] = jnp.zeros(grad_ref.shape, f32)
    stat_ref[...] = jnp.zeros(stat_ref.shape, f32)
    blocks = tokens // BLOCK

    def block(step, _):
        k = blocks - 1 - step
        t0 = pl.multiple_of(k * BLOCK, BLOCK)
        rows = pl.ds(t0, BLOCK)
        row, lane = iota((BLOCK, 128), 0), iota((BLOCK, 128), 1)
        dst_sum, db_sum, dc_sum, dcum_sum, ddt_sum = [
            functools.reduce(jnp.add, [ref[rows, :] for ref in sums[i::5]]) for i in range(5)
        ]
        keep = (lane >= row) & (scene_of(lane + t0, sm) == scene_of(row + t0, sm))
        dst = jnp.where(keep, dst_sum, 0.0).astype(bf16)
        db = db_sum + dot(dst, c_ref[rows, :])
        dc = dc_sum + dot_tn(dst, b_ref[rows, :])
        conv, shifted = conv_block(cs_scr[pl.ds(t0, BLOCK + 8), :], mask_ref[rows, :], taps, 4)
        sig = sigmoid(conv)
        dconv = jnp.concatenate([db, dc], axis=1) * (sig * (1.0 + conv * (1.0 - sig)))
        window = jnp.concatenate([dconv, ds_scr[...]], axis=0)
        ds_scr[...] = dconv[:8]
        grads = [jnp.sum(rows8(dconv * shifted[3 - i]), axis=0, keepdims=True) for i in range(4)]
        grads.append(jnp.sum(rows8(dconv), axis=0, keepdims=True))
        grads.append(jnp.zeros((3, 256), f32))
        grad_ref[...] += jnp.concatenate(grads, axis=0)
        dcin = conv_back(window, mask_ref[pl.ds(t0, BLOCK + 8), :], taps, 4)
        upper = jnp.where(lane >= row, 1.0, 0.0)
        dlog = jnp.dot(upper, dcum_sum, precision=highest, preferred_element_type=f32)
        step_in = step_ref[rows, :]
        dt = jnp.maximum(step_in, 0.0) + jnp.log1p(jnp.exp(-jnp.abs(step_in)))
        rate = head_ref[1:2, :]
        dstep = (ddt_sum - dlog * rate) * sigmoid(step_in)
        dalog = -dlog * dt * rate
        stat_ref[...] += jnp.concatenate(
            [
                jnp.sum(rows8(dstep), axis=0, keepdims=True),
                jnp.sum(rows8(dalog), axis=0, keepdims=True),
                jnp.zeros((6, 128), f32),
            ],
            axis=0,
        )
        dp_ref[rows, :] = jnp.concatenate([dcin, dstep], axis=1).astype(bf16)
        return 0

    lax.fori_loop(0, blocks, block, 0, unroll=True)


def tail(sm, cin, taps, inner, head, b, c, step, mask, sums):
    tokens = cin.shape[0]
    args = (cin, taps, head, b, c, step, mask, *sums)
    outs = [struct((tokens, 384), bf16), struct((8, 256)), struct((8, 128))]
    return call(
        tail_kernel,
        outs,
        in_specs=[SMEM] + [whole(a.shape) if a is not taps else bc_taps(inner) for a in args],
        out_specs=[whole(o.shape) for o in outs],
        scratch=[pltpu.VMEM((tokens + 8, 256), f32), pltpu.VMEM((8, 256), f32)],
        name="tail",
        us=8.0,
    )(sm, *args)


def term_kernel(tiles, add, into, sm, left_ref, *refs):
    out_ref = refs[-1]
    parts = refs[: len(tiles)]

    def product(part):
        value = dot(left_ref[...], part[...])
        if add:
            value = value + refs[len(tiles)][:, : part.shape[1]].astype(f32)
        out_ref[:, : part.shape[1]] = value.astype(bf16)

    first = 0
    for part, count in zip(parts, tiles):
        step = pl.program_id(0)
        pl.when((step >= first) & (step < first + count))(functools.partial(product, part))
        first += count


def in_term(half, left, parts, name, add=None, into=None, columns=None):
    halves, width, tokens = left.shape
    n = sum(p.shape[1] for p in parts)
    wide = min(512, n)
    tiles = [pl.cdiv(p.shape[1], wide) for p in parts]
    first = [sum(tiles[:i]) for i in range(len(parts))]
    total = n if columns is None else columns
    at = 0 if into is None else (total - n) // wide
    args = [left, *parts]
    specs = [pl.BlockSpec((None, width, tokens), lambda g, sm: (sm[0], 0, 0))] + [
        pl.BlockSpec(
            (tokens, min(wide, p.shape[1])),
            functools.partial(lambda f, c, g, sm: (0, jnp.clip(g - f, 0, c - 1)), f, c),
        )
        for p, f, c in zip(parts, first, tiles)
    ]
    if add is not None:
        args.append(add)
        specs.append(pl.BlockSpec((width, wide), lambda g, sm: (0, g)))
    aliases = {}
    if into is not None:
        aliases = {len(args) + 1: 0}
        args.append(into)
        specs.append(pl.BlockSpec(memory_space=pl.ANY))
    spec = pltpu.PrefetchScalarGridSpec(
        num_scalar_prefetch=1,
        grid=(sum(tiles),),
        in_specs=specs,
        out_specs=pl.BlockSpec((width, wide), lambda g, sm: (0, at + g)),
    )
    return pl.pallas_call(
        functools.partial(term_kernel, tiles, add is not None, into is not None),
        out_shape=struct((width, total), bf16),
        grid_spec=spec,
        name=name,
        input_output_aliases=aliases,
        compiler_params=pltpu.CompilerParams(vmem_limit_bytes=VMEM_LIMIT, dimension_semantics=("arbitrary",)),
        cost_estimate=cost(width * tokens * n * 5e-9),
    )(half, *args)


def out_kernel(add, sm, left_ref, right_ref, *refs):
    value = dot(left_ref[...], right_ref[...])
    if add:
        value = value + refs[0][...].astype(f32)
    refs[-1][...] = value.astype(bf16)


def out_term(ring, half, flip, cot_low, name, add=None, columns=None):
    inner, tokens = flip.shape
    width = cot_low.shape[1]
    rows = inner // 4
    left = flip.reshape(4, rows, tokens)
    steps = 2 if ring else 4
    out = pl.BlockSpec((rows, width), (lambda g, sm: (0, g)) if ring else (lambda g, sm: (g, 0)))
    args, specs = [left, cot_low], [
        pl.BlockSpec((None, rows, tokens), lambda g, sm: (sm[0] * 2 + g, 0, 0)),
        pl.BlockSpec(cot_low.shape, lambda g, sm: (0, 0)),
    ]
    if add is not None:
        args.append(add)
        specs.append(out)
    spec = pltpu.PrefetchScalarGridSpec(num_scalar_prefetch=1, grid=(steps,), in_specs=specs, out_specs=out)
    return pl.pallas_call(
        functools.partial(out_kernel, add is not None),
        out_shape=struct((rows, columns or 2 * width) if ring else (inner, width), bf16),
        grid_spec=spec,
        name=name,
        compiler_params=pltpu.CompilerParams(vmem_limit_bytes=VMEM_LIMIT, dimension_semantics=("arbitrary",)),
        cost_estimate=cost(5.0),
    )(half, *args)


def last_kernel(count, x_ref, cot_ref, gain_ref, *refs):
    ds, ws, dx_ref = refs[:count], refs[count : 2 * count], refs[-1]
    x = x_ref[...]
    width = x.shape[1]
    dn = functools.reduce(jnp.add, [dot_nt(d[...], w[...]) for d, w in zip(ds, ws)])
    r = lax.rsqrt(jnp.mean(x * x, axis=-1, keepdims=True) + EPS)
    u = dn * gain_ref[0:1, :]
    xr = x * r
    mu = jnp.sum(u * xr, axis=-1, keepdims=True) * (1.0 / width)
    dx_ref[...] = cot_ref[...] + r * (u - xr * mu)


def last(x, cot, gain, pairs):
    tokens, width = x.shape
    row = lambda n: pl.BlockSpec((MID, n), lambda g: (g, 0))
    ds, ws = zip(*pairs)
    n = sum(k for _, k, _ in ds)
    return call(
        functools.partial(last_kernel, len(pairs)),
        struct(x.shape),
        grid=(tokens // MID,),
        in_specs=[row(width), row(width), whole(gain.shape)]
        + [pl.BlockSpec((MID, k), functools.partial(lambda i, g: (g, i), i)) for _, k, i in ds]
        + [pl.BlockSpec((width, k), functools.partial(lambda i, g: (0, i), i)) for _, k, i in ws],
        out_specs=row(width),
        name="last",
        us=18.0,
        vmem=VMEM_LARGE,
    )(x, cot, gain, *[d[0] for d in ds], *[w[0] for w in ws])


Y, CORE, X, Z1, Z2 = 1, 2, 4, 8, 16


def exchange(a, bit):
    return lax.ppermute(a, AXES, [(i, i ^ bit) for i in range(SHARDS)])


def after(a, *others):
    return lax.optimization_barrier((a, *others))[0] if others else a


def together(arrays, *others):
    return list(lax.optimization_barrier((*arrays, *others))[: len(arrays)])


def join(a, got):
    return jnp.concatenate([a, got], axis=0)


def gather_z(own):
    two = join(own, exchange(own, Z1))
    return join(two, exchange(two, Z2))


def take(a, bit, axis):
    return lax.dynamic_index_in_dim(a, bit, axis, keepdims=False)


def scatter_start(keep):
    return [Z2, Z1, X, Y], keep.reshape(2, 2, 2, 2, keep.shape[0] // 16, keep.shape[1])


def scatter_send(place, state, bit):
    names, left = state
    axis = names.index(bit)
    mine = jnp.where((place & bit) > 0, 1, 0)
    names = names[:axis] + names[axis + 1 :]
    return names, take(left, mine, axis), exchange(take(left, 1 - mine, axis), bit)


def scatter_add(sent, got=None):
    names, left, flight = sent
    left = left.astype(f32) + (flight if got is None else got).astype(f32)
    return names, left.astype(bf16) if names else left


def both(a, b):
    return (a.astype(f32) + b.astype(f32)).astype(bf16)


def pad_to(a, rows, columns):
    return jnp.pad(a, ((0, rows - a.shape[0]), (0, columns - a.shape[1])))


def local(
    ring, block_input, cotangent, scene_lengths, norm_gain, in_weight, conv_weight, conv_bias, dt_bias, a_log, skip_gain,
    gated_gain, out_weight,
):
    tokens, width = block_input.shape
    heads = a_log.shape[0]
    inner = out_weight.shape[0] * lax.axis_size(AXES)
    channels = conv_bias.shape[0] * lax.axis_size(AXES)
    proj = in_weight.shape[1]
    bc = proj - 2 * inner
    place = lax.axis_index(AXES).astype(jnp.int32)
    bounds = jnp.cumsum(scene_lengths[0]).astype(jnp.int32)
    sm = jnp.concatenate([bounds, place[None], jnp.zeros((4,), jnp.int32)])
    groups = inner // GROUP

    def pack(grads, gg, stat):
        d_skip = jnp.sum(grads[5, :inner].reshape(heads, -1), axis=1)
        side = jnp.concatenate([stat[0, :heads], stat[1, :heads], d_skip])[None]
        return jnp.concatenate([grads[:5], pad_to(jnp.sum(gg, axis=0)[None], 1, channels), pad_to(side, 2, channels)], axis=0)

    gather = lambda a: lax.all_gather(a.astype(bf16), AXES, axis=0, tiled=True)
    skip_row = jnp.repeat(skip_gain, inner // heads)[None]
    w_low = in_weight.astype(bf16)
    if ring:
        small = jnp.concatenate(
            [
                jnp.concatenate([norm_gain, gated_gain])[None],
                pad_to(conv_weight.T, 4, 96),
                pad_to(conv_bias[None], 27, 96),
            ],
            axis=0,
        )
        first = jnp.concatenate([w_low[:, 2 * inner :], small.astype(bf16)], axis=1)
        wide = inner // 2
        one, two = [
            jnp.concatenate([w_low[:, at : at + wide], w_low[:, inner + at : inner + at + wide]], axis=1)
            for at in (0, wide)
        ]
        halves = lambda a: [a[:, : a.shape[1] // 2], a[:, a.shape[1] // 2 :]]
        outward = lambda a, bits: [exchange(part, bit) for part, bit in zip(a, bits)]
        joined = lambda a, got: [join(part, came) for part, came in zip(a, got)]
        row = join(first, exchange(first, Z1))
        row, one = joined([row, one], together([exchange(row, Z2), exchange(one, Z1)]))
        two = after(two, row)
        row, one, two = joined([row, one, two], together([exchange(row, X), exchange(one, Z2), exchange(two, Z1)]))
        two_flight = exchange(two, Z2)
        one = halves(one)
        row, *one = joined([row, *one], together([exchange(row, Y), *outward(one, (X, Y))]))
        one_flights = outward(one, (Y, X))
        w_bc, taps, gain = unpack(sm, [row, exchange(row, CORE)], skip_row, channels, width)
        two = halves(join(two, together([two_flight], w_bc)[0]))
        two_flights = outward(two, (X, Y))
        x_first = after(block_input, *two)
    else:
        in_full, outside, x_first = gather(in_weight), [gather(out_weight)], block_input
        norm_full, conv_full, bias_full, gated_full = map(gather, (norm_gain, conv_weight, conv_bias, gated_gain))
        gain = jnp.broadcast_to(norm_full.astype(f32)[None], (8, width))
        w_bc = pad_to(in_full[:, 2 * inner :], width, 384)
        taps = jnp.concatenate(
            [
                conv_full.astype(f32).T,
                bias_full.astype(f32)[None],
                pad_to(jnp.concatenate([skip_row, gated_full.astype(f32)[None]], axis=0), 3, channels),
            ],
            axis=0,
        )
    head = jnp.pad(jnp.stack([dt_bias, jnp.exp(a_log)]), ((0, 6), (0, 128 - heads)))
    (normed, normt, cin_bc, b, c, bt, ct, s, st, cum, cumt, ea, eb, step, mask) = prep(
        ring, sm, x_first, gain, w_bc, taps, inner, head, heads
    )
    pre = (ea, eb, cum, cumt, c, bt, s, mask)
    def scan(base, count, offset, *w, first=(), **more):
        return fwd(base, count, offset, ring, sm, after(normed, *first), *w, inner, taps, pre, **more)

    if ring:
        half, quarter = groups // 2, groups // 4
        pairs = lambda a, got: list(zip(a, got))
        got = together([*one_flights, *two_flights], normed)
        one, two = joined(one, got[:2]), joined(two, got[2:])
        flights = outward(one, (CORE, CORE))
        two_flights = outward(two, (Y, X))
        out = after(out_weight, one[0]).astype(bf16)
        *got, came = together([*flights, exchange(out, Z1)])
        out = join(out, came)
        front = pairs(one, got)
        out_flight = exchange(out, Z2)
        near = scan(0, quarter, 0, *front, first=[out, *two])
        *got, came = together([*two_flights, out_flight], near[2])
        two, out = joined(two, got), halves(join(out, came))
        flights = outward(two, (CORE, CORE)) + outward(out, (X, Y))
        next_ = scan(quarter, quarter, quarter, *front, first=[*two, *out])
        got = together(flights, next_[2])
        back, out = pairs(two, got[:2]), joined(out, got[2:])
        flights = outward(out, (Y, X))
        far = scan(half, quarter, 0, *back, first=out, total=half)
        out = joined(out, together(flights, far[2]))
        flights = outward(out, (CORE, CORE))
        far = scan(half + quarter, quarter, quarter, *back, first=out, total=half, into=far)
        got = together(flights, far[2])
        outside = [out[0], got[0], out[1], got[1]]
        runs = [(0, quarter, near), (quarter, quarter, next_), (half, half, far)]
    else:
        runs = [(0, groups, scan(0, groups, 0, [in_full], [in_full]))]
    mixed, dz, dy, gg, flip, cot_low, *w_out = mid(
        ring, sm, cotangent, outside, inner, taps, mask, [r[0] for *_, r in runs], [r[2] for *_, r in runs]
    )
    out_full = w_out[0] if ring else outside[0]
    normt = normt.reshape(2 if ring else 1, -1, tokens)
    core = sm[3:4] >> 1 & 1
    if ring:
        sent = out_term(ring, 1 - core, flip, cot_low, "out_away")
        out_away = exchange(sent, CORE)
        sent = in_term(1 - core, normt, [after(dz, sent)], "gate_away")
        gate_away = exchange(sent, CORE)
        out_here = out_term(ring, core, flip, cot_low, "out_here", after(out_away, sent))
        gate_here = in_term(core, normt, [dz], "gate_here", after(gate_away, out_here))
        outs, gates = scatter_start(out_here), scatter_start(gate_here)
        dy = after(dy, gate_here)
    pre = (ea, eb, cum, cumt, b, c, ct, st, mask)
    scan = lambda dy, base, count, run: bwd(base, count, run[1], run[2], dy, taps, pre, run[3])
    finish = lambda sums: tail(sm, cin_bc, taps, inner, head, b, c, step, mask, sums)
    if ring:

        def term(parts, name):
            away = exchange(in_term(1 - core, normt, parts, name + "_away"), CORE)
            return scatter_start(both(in_term(core, normt, parts, name + "_here"), away))

        send = functools.partial(scatter_send, place)
        gates, outs = send(gates, X), send(outs, Y)
        back = scan(dy, *runs[2])
        one, two = together([gates[2], outs[2]], back[0])
        gates, outs = send(scatter_add(gates, one), Y), send(scatter_add(outs, two), X)
        near = scan(after(dy, gates[1], outs[1], back[0]), *runs[0])
        one, two = together([gates[2], outs[2]], near[0])
        gates, outs = scatter_add(gates, one), scatter_add(outs, two)
        early = send((gates[0], jnp.concatenate([gates[1], outs[1]], axis=-1)), Z2)
        parts = [near[0], after(back[0], early[1])]
        away = in_term(1 - core, normt, parts, "late_away")
        here = in_term(core, normt, parts, "late_here")
        late = send(scatter_start(both(here, exchange(away, CORE))), X)
        mid_out = scan(after(dy, late[1], near[0]), *runs[1])
        sums = [a for out in (back, near, mid_out) for a in out[2:]]
        (one,) = together([late[2]], mid_out[0])
        late = send(scatter_add(late, one), Y)
        sums[0] = after(sums[0], late[1])
        dbc, grad_bc, stat = finish(sums)
        grads = jnp.concatenate([near[1], mid_out[1], back[1], grad_bc], axis=1)
        one, two = together([early[2], late[2]], dbc)
        early, late = send(scatter_add(early, one), Z1), send(scatter_add(late, two), Z2)
        small = pack(grads, gg, stat)
        flight = exchange(small, CORE)
        parts = [mid_out[0], after(dbc, early[1], late[1], small)]
        away = in_term(1 - core, normt, parts, "last_away")
        here = in_term(core, normt, parts, "last_here")
        one, two, flight = together([early[2], late[2], flight], here)
        early, late, small = scatter_add(early, one), send(scatter_add(late, two), Z1), small + flight
        flight = exchange(small, X)
        final = send(scatter_start(both(here, exchange(away, CORE))), X)
        x_last = after(block_input, final[1], small, late[1])
        pairs = []
        for (base, count, run), (dv, *_) in zip(runs, (near, mid_out, back)):
            wide = count * GROUP
            pairs.append(((dz, wide, base // count), (run[4], wide, 0)))
            pairs.append(((dv, wide, 0), (run[5], wide, 0)))
        x_last = after(block_input, final[1], small, late[1])
    else:
        scatter = lambda a: lax.psum_scatter(a.astype(f32), AXES, scatter_dimension=0, tiled=True)
        dv, grad, *sums = scan(dy, *runs[0])
        dbc, grad_bc, stat = finish(sums)
        grads = jnp.concatenate([grad, grad_bc], axis=1)
        in_grad = scatter(in_term(core * 0, normt, [dz, dv, dbc], "all")[:, :proj])
        out_grad = scatter(out_term(ring, core * 0, flip, cot_low, "out"))
        pairs = [((dz, inner, 0), (in_full, inner, 0)), ((dv, inner, 0), (in_full, inner, 1))]
        x_last = block_input
    pairs.append(((dbc, 384, 0), (w_bc, 384, 0)))
    input_grad = last(x_last, cotangent, gain, pairs)
    if ring:
        one, two, flight = together([late[2], final[2], flight], input_grad)
        late, final, small = scatter_add(late, one), send(scatter_add(final, two), Y), small + flight
        flight = exchange(small, Y)
        mixed = after(mixed, final[1], small)
    block_output = branch(block_input, mixed, out_full)
    if ring:
        one, flight = together([final[2], flight], block_output)
        final, small = send(scatter_add(final, one), Z2), small + flight
        small = small + exchange(small, Z1)
        final = scatter_add(send(scatter_add(final), Z1))
        small = small + exchange(small, Z2)
        gate_grad, out_grad = early[1][:, :inner], early[1][:, inner:]
        out_grad = jnp.concatenate([out_grad[:, :width], out_grad[:, width:]], axis=0)
        near, half = inner // 4, inner // 2
        in_grad = jnp.concatenate(
            [gate_grad, late[1][:, :near], final[1][:, :near], late[1][:, near:], final[1][:, near : near + bc]], axis=1
        )
    else:
        small = lax.psum(pack(grads, gg, stat), AXES)
    d_gain = jnp.sum(in_grad * w_low.astype(f32), axis=1) / norm_gain.astype(bf16).astype(f32)
    part = lambda row, n: lax.dynamic_slice_in_dim(row, place * n, n, axis=-1)
    side = small[6]
    return (
        block_output,
        input_grad,
        d_gain,
        in_grad,
        part(small[:4], conv_bias.shape[0]).T,
        part(small[4], conv_bias.shape[0]),
        side[:heads],
        side[heads : 2 * heads],
        side[2 * heads : 3 * heads],
        part(small[5], gated_gain.shape[0]),
        out_grad,
    )


def solution(mesh):
    dp, fsdp = mesh.devices.shape
    split = jax.sharding.Mesh(mesh.devices.reshape(dp // 2, 2, fsdp), AXES)
    row = P(AXES, None)
    flat = P(AXES)
    return jax.shard_map(
        functools.partial(local, (dp, fsdp) == (16, 2)),
        mesh=split,
        in_specs=(row, row, row, flat, row, row, flat, P(), P(), P(), flat, row),
        out_specs=(row, row, flat, row, row, flat, P(), P(), P(), flat, row),
        check_vma=False,
    )
```

```python
import functools

import jax
import jax.numpy as jnp
from jax import lax
from jax.experimental import pallas as pl
from jax.experimental.pallas import tpu as pltpu
from jax.sharding import PartitionSpec as P

AXES = ("chip", "core", "fsdp")
CHIPS = ("chip", "fsdp")
SHARDS = 32
PIECES = 2
BLOCK = 128
GROUP = 256
EPS = 1e-05
LOG2E = 1.4426950408889634
VMEM_LIMIT = 50 * 1024 * 1024
VMEM_LARGE = 60 * 1024 * 1024
f32 = jnp.float32
bf16 = jnp.bfloat16
highest = lax.Precision.HIGHEST


def dot(a, b):
    return jnp.dot(a, b, preferred_element_type=f32)


def dot_nt(a, b):
    return lax.dot_general(a, b, (((1,), (1,)), ((), ())), preferred_element_type=f32)


def dot_tn(a, b):
    return lax.dot_general(a, b, (((0,), (0,)), ((), ())), preferred_element_type=f32)


def sigmoid(v):
    return 0.5 * jnp.tanh(0.5 * v) + 0.5


def iota(shape, axis):
    return lax.broadcasted_iota(jnp.int32, shape, axis)


def rows8(v):
    return jnp.sum(v.reshape(v.shape[0] // 8, 8, v.shape[1]), axis=0)


def scene_of(place, sm):
    scene = jnp.zeros(place.shape, jnp.int32)
    for i in range(3):
        scene = scene + jnp.where(place >= sm[i], 1, 0)
    return scene


def cost(us):
    return pl.CostEstimate(flops=0, bytes_accessed=int(us * 3.69e6), transcendentals=0)


def call(kernel, out, grid=None, in_specs=None, out_specs=None, scratch=(), name=None, us=1.0, aliases=None, vmem=VMEM_LIMIT):
    return pl.pallas_call(
        kernel,
        out_shape=out,
        grid=grid or (1,),
        in_specs=in_specs,
        out_specs=out_specs,
        scratch_shapes=scratch,
        name=name,
        compiler_params=pltpu.CompilerParams(
            vmem_limit_bytes=vmem, dimension_semantics=("arbitrary",)
        ),
        cost_estimate=cost(us),
        input_output_aliases=aliases or {},
    )


def whole(shape):
    return pl.BlockSpec(shape, lambda g: (0,) * len(shape))


def bc_taps(inner):
    return pl.BlockSpec((8, 256), lambda g: (0, inner // 256))


SMEM = pl.BlockSpec(memory_space=pltpu.SMEM)


def struct(shape, dtype=f32):
    return jax.ShapeDtypeStruct(shape, dtype)


def conv_block(window, masks, taps, width):
    current = window[8:]
    total = taps[4:5] + current * taps[3:4]
    shifted = [current]
    for off in range(1, width):
        moved = window[8 - off : 8 - off + BLOCK] * masks[:, off - 1 : off]
        shifted.append(moved)
        total = total + moved * taps[width - 1 - off : width - off]
    return total, shifted


def conv_back(window, masks, taps, width):
    total = window[:BLOCK] * taps[width - 1 : width]
    for off in range(1, width):
        moved = pltpu.roll(window * masks[:, off - 1 : off], window.shape[0] - off, 0)[:BLOCK]
        total = total + moved * taps[width - 1 - off : width - off]
    return total


def unpack_kernel(sm, *refs):
    pieces, (skip_ref, w_ref, taps_ref, gain_ref) = refs[:PIECES], refs[PIECES:]
    assemble(sm, pieces, w_ref, 32, True)
    row, col = iota((8 * SHARDS, 32 * SHARDS), 0), iota((8 * SHARDS, 32 * SHARDS), 1)
    pick = jnp.where(col == (row & (SHARDS - 1)) * 32 + row // SHARDS, 1.0, 0.0).astype(bf16)
    packed = dot(pick, w_ref[:, 256:384]).astype(bf16)

    def spread(kind, lane, size):
        total = size * SHARDS
        place = iota((1, total), 1)
        owner, within = place // size, place % size
        copy = jnp.where(iota((128, total), 0) == within + lane, 1.0, 0.0).astype(bf16)
        values = dot(packed[kind * SHARDS : (kind + 1) * SHARDS, :], copy)
        return jnp.sum(jnp.where(iota((SHARDS, total), 0) == owner, values, 0.0), axis=0, keepdims=True)

    taps_ref[...] = jnp.zeros(taps_ref.shape, f32)
    gain_ref[...] = jnp.broadcast_to(spread(0, 32, 32), gain_ref.shape)
    inner = skip_ref.shape[1]
    taps_ref[6:7, :inner] = spread(0, 64, inner // SHARDS)
    channels = taps_ref.shape[1]
    for k in range(5):
        taps_ref[k : k + 1, :] = spread(k + 1, 32, channels // SHARDS)
    taps_ref[5:6, :inner] = skip_ref[0:1, :]


def unpack(sm, pieces, skip, channels, width):
    outs = [struct((width, 384), bf16), struct((8, channels)), struct((8, width))]
    return call(
        unpack_kernel,
        outs,
        in_specs=[SMEM] + [whole(a.shape) for a in (*pieces, skip)],
        out_specs=[whole(o.shape) for o in outs],
        name="unpack",
        us=3.0,
    )(sm, *pieces, skip)


def core_first(shard):
    return (shard >> 1 & 1) * 16 + (shard >> 2) * 2 + (shard & 1)


def prep_kernel(
    ring, sm, x_ref, gain_ref, w_ref, taps_ref, head_ref,
    normed_ref, normt_ref, cin_ref, b_ref, c_ref, bt_ref, ct_ref, s_ref, st_ref,
    cum_ref, cumt_ref, ea_ref, eb_ref, step_ref, mask_ref, cs_scr,
):
    tokens = x_ref.shape[0]
    x = x_ref[...]
    scale = lax.rsqrt(jnp.mean(x * x, axis=-1, keepdims=True) + EPS)
    normed_low = (x * scale * gain_ref[0:1, :]).astype(bf16)
    normed_ref[...] = normed_low
    flipped = normed_low.astype(f32).T.astype(bf16)
    if ring:
        for shard in range(SHARDS):
            at = core_first(shard) * 32
            normt_ref[at : at + 32, :] = flipped[shard * 32 : shard * 32 + 32, :]
    else:
        normt_ref[...] = flipped
    proj = dot(normed_low, w_ref[...])
    lanes = iota((1, 128), 1)
    heads = 4 * cumt_ref.shape[0]
    is_head = lanes < heads
    cin_low = proj[:, :256].astype(bf16)
    cin_ref[...] = cin_low
    cs_scr[0:8, :] = jnp.zeros((8, 256), f32)
    cs_scr[pl.ds(8, tokens), :] = cin_low.astype(f32)
    step_ref[...] = jnp.where(is_head, proj[:, 256:384] + head_ref[0:1, :], 0.0)
    taps = taps_ref[...]

    for k in range(tokens // BLOCK):
        t0 = k * BLOCK
        rows = pl.ds(t0, BLOCK)
        place = iota((BLOCK, 128), 0) + t0
        lane = iota((BLOCK, 128), 1)
        scene = scene_of(place, sm)
        before = place - lane - 1
        same = (before >= 0) & (scene_of(before, sm) == scene)
        mask = jnp.where(lane < 3, jnp.where(same, 1.0, 0.0), jnp.where(place < sm[2], 1.0, 0.0))
        mask_ref[rows, :] = mask
        conv, _ = conv_block(cs_scr[pl.ds(t0, BLOCK + 8), :], mask, taps, 4)
        act = conv * sigmoid(conv)
        b_low = act[:, :128].astype(bf16)
        c_low = act[:, 128:].astype(bf16)
        b_ref[rows, :] = b_low
        c_ref[rows, :] = c_low
        bt_ref[:, rows] = act[:, :128].T.astype(bf16)
        ct_ref[:, rows] = act[:, 128:].T.astype(bf16)
        other = scene_of(lane + t0, sm)
        low = (lane + t0 <= place) & (other == scene)
        s_ref[rows, :] = jnp.where(low, dot_nt(c_low, b_low), 0.0)
        high = (lane + t0 >= place) & (other == scene)
        st_ref[rows, :] = jnp.where(high, dot_nt(b_low, c_low), 0.0)
        step = step_ref[rows, :]
        dt = jnp.maximum(step, 0.0) + jnp.log1p(jnp.exp(-jnp.abs(step)))
        dt = jnp.where(is_head, dt, 0.0)
        log_decay = dt * (head_ref[1:2, :] * -LOG2E)
        lower = jnp.where(lane <= iota((BLOCK, 128), 0), 1.0, 0.0)
        cum = jnp.dot(lower, log_decay, precision=highest, preferred_element_type=f32)
        cum_ref[rows, :] = cum
        flat = cum.T
        for i in range(heads // 4):
            cumt_ref[i, :, rows] = flat[4 * i : 4 * i + 4, :]
        first = jnp.full((1, 128), t0 - 1, jnp.int32)
        last = jnp.full((1, 128), t0 + BLOCK - 1, jnp.int32)
        entering = (scene_of(first, sm) == scene) & (first >= 0) & is_head
        final = (scene_of(last, sm) == scene) & is_head
        grow = jnp.where(entering, jnp.exp2(cum), 0.0)
        end = jnp.where(final, jnp.exp2(cum[BLOCK - 1 :] - cum), 0.0)

        def packed(v):
            hi = v.astype(bf16).astype(f32)
            return hi + pltpu.roll((v - hi).astype(bf16).astype(f32), 32, 1)

        ea_ref[rows, :] = (packed(dt) + pltpu.roll(packed(grow), 64, 1)).astype(bf16)
        eb_ref[rows, :] = packed(end).astype(bf16)
    mask_ref[pl.ds(tokens, 8), :] = jnp.zeros((8, 128), f32)


def prep(ring, sm, x, gain, w_bc, taps, inner, head, heads):
    tokens, width = x.shape
    wide = (tokens, 128)
    outs = [
        struct(x.shape, bf16), struct((width, tokens), bf16), struct((tokens, 256), bf16),
        struct(wide, bf16), struct(wide, bf16), struct((128, tokens), bf16), struct((128, tokens), bf16),
        struct(wide), struct(wide), struct(wide), struct((heads // 4, 4, tokens)), struct(wide, bf16), struct(wide, bf16),
        struct(wide), struct((tokens + 8, 128)),
    ]
    args = (x, gain, w_bc, taps, head)
    return call(
        functools.partial(prep_kernel, ring),
        outs,
        in_specs=[SMEM] + [whole(a.shape) if a is not taps else bc_taps(inner) for a in args],
        out_specs=[whole(o.shape) for o in outs],
        scratch=[pltpu.VMEM((tokens + 8, 256), f32)],
        name="prep",
        us=13.0,
    )(sm, *args)


def fill_spread(e_scr, group):
    row = iota((128, 768), 0)
    col = iota((128, 768), 1)
    head = 4 * group + (col % GROUP) // 64
    part = jnp.where(col < GROUP, 0, jnp.where(col < 2 * GROUP, 64, 0))
    hit = (row == head + part) | (row == head + part + 32)
    e_scr[...] = jnp.where(hit, 1.0, 0.0).astype(bf16)


def pair_masks():
    low = jnp.where(iota((1, 128), 1) < 64, 1.0, 0.0).astype(bf16)
    high = jnp.where(iota((1, 128), 1) < 64, 0.0, 1.0).astype(bf16)
    return low, high


def assemble(sm, pieces, out_ref, block, x_first, columns=slice(None)):
    low, high = (4, 1) if x_first else (1, 4)
    for core, piece in enumerate(pieces):
        for j in range(SHARDS // 2):
            shard = sm[3] ^ (core << 1 | (j & 3) << 3 | (j >> 2 & 1) * low | (j >> 3) * high)
            out_ref[pl.ds(pl.multiple_of(shard * block, block), block), columns] = piece[j * block : (j + 1) * block, :]


def fwd_kernel(*refs):
    base, ring, into, sm = refs[:4]
    refs = refs[1:]
    if ring:
        n = PIECES
        gates, values = refs[3 : 3 + n], refs[3 + n : 3 + 2 * n]
        rest = list(refs[3 + 2 * n :])
        if into:
            del rest[10:16]
        wv_ref, wg_ref = rest.pop(15), rest.pop(14)
        assemble(sm, gates, wg_ref, 32, True)
        assemble(sm, values, wv_ref, 32, False)
        rest[1:1] = [wg_ref, wv_ref]
    else:
        rest = list(refs[5:])
        rest[1:1] = refs[3:5]
    fwd_body(base, *rest)


def fwd_body(
    base, normed_ref, wg_ref, wv_ref, taps_ref, ea_ref, eb_ref, cum_ref, cumt_ref, c_ref, bt_ref, s_ref, mask_ref,
    z_ref, cin_ref, y_ref, h_ref, cs_scr, e_scr, x_scr,
):
    group = pl.program_id(0) + base
    tokens = normed_ref.shape[0]
    normed = normed_ref[...]
    z_ref[...] = dot(normed, wg_ref[...]).astype(bf16)
    cin_low = dot(normed, wv_ref[...]).astype(bf16)
    cin_ref[...] = cin_low
    cs_scr[0:8, :] = jnp.zeros((8, GROUP), f32)
    cs_scr[pl.ds(8, tokens), :] = cin_low.astype(f32)
    fill_spread(e_scr, group)
    x_scr[:, : 2 * GROUP] = dot(ea_ref[...], e_scr[:, : 2 * GROUP])
    x_scr[:, 2 * GROUP :] = dot(eb_ref[...], e_scr[:, 2 * GROUP :])
    taps = taps_ref[...]
    m_low, m_high = pair_masks()

    state = jnp.zeros((128, GROUP), f32)
    blocks = tokens // BLOCK
    for k in range(blocks):
        t0 = k * BLOCK
        rows = pl.ds(t0, BLOCK)
        mask = mask_ref[rows, :]
        conv, _ = conv_block(cs_scr[pl.ds(t0, BLOCK + 8), :], mask, taps, 4)
        v = conv * sigmoid(conv)
        dtx, ex, wx = [x_scr[rows, i * GROUP : (i + 1) * GROUP] for i in range(3)]
        vd_low = (v * dtx).astype(bf16)
        h_low = state.astype(bf16)
        h_ref[rows, :] = h_low
        cums = pltpu.roll(cum_ref[rows, :], 128 - 4 * group, 1)
        s = s_ref[rows, :]
        inside = []
        for pair in range(2):
            weights = []
            for j in (2 * pair, 2 * pair + 1):
                spread = cums[:, j : j + 1] - cumt_ref[0, j : j + 1, rows]
                weights.append((jnp.exp2(jnp.minimum(spread, 0.0)) * s).astype(bf16))
            vp = vd_low[:, pair * 128 : pair * 128 + 128]
            stack = jnp.concatenate([vp * m_low, vp * m_high], axis=0)
            inside.append(dot(jnp.concatenate(weights, axis=1), stack))
        y = jnp.concatenate(inside, axis=1) + taps[5:6] * v
        if k > 0:
            y = y + dot(c_ref[rows, :], h_low) * ex
        y_ref[rows, :] = y
        if k < blocks - 1:
            fresh = dot(bt_ref[:, rows], (vd_low.astype(f32) * wx).astype(bf16))
            state = state * ex[BLOCK - 1 :] + fresh


def fwd(base, count, offset, ring, sm, normed, gates, values, inner, taps, pre, total=None, into=()):
    tokens, width = normed.shape
    full = lambda a: whole(a.shape)
    ea, eb, cum, cumt, c, bt, s, mask = pre
    first = inner // GROUP
    at = (total or count) - count if into else 0
    col = lambda rows, dtype: struct((rows, (total or count) * GROUP), dtype)
    block = lambda rows: pl.BlockSpec((rows, GROUP), lambda g: (0, at + g))
    outs = [col(tokens, bf16), col(tokens, bf16), col(tokens, f32), col(tokens, bf16)]
    if ring:
        w_specs = [pl.BlockSpec((a.shape[0], GROUP), lambda g: (0, offset + g)) for a in (*gates, *values)]
        outs += [col(width, bf16)] * 2
    else:
        w_specs = [
            pl.BlockSpec((width, GROUP), lambda g: (0, base + g)),
            pl.BlockSpec((width, GROUP), lambda g: (0, first + base + g)),
        ]
    return call(
        functools.partial(fwd_kernel, base, ring, bool(into)),
        outs,
        grid=(count,),
        in_specs=[SMEM] + w_specs + [
            full(normed),
            pl.BlockSpec((8, GROUP), lambda g: (0, base + g)),
            full(ea), full(eb), full(cum),
            pl.BlockSpec((1, 4, tokens), lambda g: (base + g, 0, 0)),
            full(c), full(bt), full(s), full(mask),
        ] + [pl.BlockSpec(memory_space=pl.ANY)] * len(into),
        out_specs=[block(o.shape[0]) for o in outs],
        aliases={11 + 2 * len(gates) + i: i for i in range(len(into))},
        scratch=[pltpu.VMEM((tokens + 8, GROUP), f32), pltpu.VMEM((128, 3 * GROUP), bf16), pltpu.VMEM((tokens, 3 * GROUP), f32)],
        name=f"fwd{base}",
        us=count * 6.6,
    )(sm, *gates, *values, normed, taps, ea, eb, cum, cumt, c, bt, s, mask, *into)


MID = 256
WIDE = 512
MID_C = 512


def mid_kernel(ring, chunks, sm, cot_ref, taps_ref, mask_ref, *refs):
    zs, ys = refs[:chunks], refs[chunks : 2 * chunks]
    *pieces, mixed_ref, dz_ref, dy_ref, gg_ref, flip_ref, low_ref, w_ref, g_scr, u_scr = refs[2 * chunks :]
    if not ring:
        pieces, w_ref = [], pieces[0]
    half = w_ref.shape[1] // 2

    @pl.when(pl.program_id(0) == 0)
    def _():
        gg_ref[...] = jnp.zeros(gg_ref.shape, f32)
        if ring:
            assemble(sm, pieces[:PIECES], w_ref, 64, True, slice(0, half))
            assemble(sm, pieces[PIECES:], w_ref, 64, False, slice(half, 2 * half))

    inner = dz_ref.shape[1]
    alive = mask_ref[:, 3:4]
    cot_low = cot_ref[...].astype(bf16)
    low_ref[...] = cot_low
    square = jnp.zeros((MID, 128), f32)
    parts = [slice(i, i + MID_C) for i in range(0, inner, MID_C)]
    here = [(z, y, slice(i, i + MID_C)) for z, y in zip(zs, ys) for i in range(0, z.shape[1], MID_C)]
    for part, (z_ref, y_ref, cut) in zip(parts, here):
        z = z_ref[:, cut].astype(f32)
        g = y_ref[:, cut] * (z * sigmoid(z))
        g_scr[:, part] = g
        sq = g * g
        for i in range(0, MID_C, 128):
            square = square + sq[:, i : i + 128]
    r = lax.rsqrt(jnp.sum(square, axis=-1, keepdims=True) * (1.0 / inner) + EPS)
    r_alive = r * alive
    cross = jnp.zeros((MID, 128), f32)
    for part in parts:
        gain = taps_ref[6:7, part]
        dm = dot_nt(cot_low, w_ref[part, :])
        g = g_scr[:, part]
        u = dm * gain
        u_scr[:, part] = u
        ug = u * g
        for i in range(0, MID_C, 128):
            cross = cross + ug[:, i : i + 128]
        gr = g * r_alive
        mixed = gr * gain
        mixed_ref[:, part] = mixed.astype(bf16)
        gg_ref[:, part] += rows8(dm * gr)
        flipped = mixed.T.astype(bf16)
        for i in range(0, MID_C, 32):
            shard, half = (part.start + i) // 64, i // 32 % 2
            place = core_first(shard) // 16 * 32 + half * 16 + core_first(shard) % 16 if ring else (part.start + i) // 32
            flip_ref[place * 32 : place * 32 + 32, :] = flipped[i : i + 32, :]
    r3 = r_alive * r * r * (jnp.sum(cross, axis=-1, keepdims=True) * (1.0 / inner))
    for part, (z_ref, y_ref, cut) in zip(parts, here):
        z = z_ref[:, cut].astype(f32)
        sig = sigmoid(z)
        dg = u_scr[:, part] * r_alive - g_scr[:, part] * r3
        silu = z * sig
        dy_ref[:, part] = (dg * silu).astype(bf16)
        dz_ref[:, part] = (dg * y_ref[:, cut] * (sig + silu * (1.0 - sig))).astype(bf16)


def mid(ring, sm, cot, pieces, inner, taps, mask, zs, ys):
    tokens, width = cot.shape
    row = lambda n: pl.BlockSpec((MID, n), lambda g: (g, 0))
    wide = struct((tokens, inner), bf16)
    outs = [wide, wide, wide, struct((8, inner)), struct((inner, tokens), bf16), struct(cot.shape, bf16)]
    outs.append(struct((inner, width) if ring else (8, 128), bf16))
    return call(
        functools.partial(mid_kernel, ring, len(zs)),
        outs,
        grid=(tokens // MID,),
        in_specs=[SMEM, row(width), whole(taps.shape), row(128)]
        + [row(a.shape[1]) for a in (*zs, *ys)]
        + [whole(a.shape) for a in pieces],
        out_specs=[row(inner)] * 3 + [whole((8, inner)), pl.BlockSpec((inner, MID), lambda g: (0, g)), row(width), whole(outs[-1].shape)],
        scratch=[pltpu.VMEM((MID, inner), f32), pltpu.VMEM((MID, inner), f32)],
        name="mid",
        us=25.0,
        vmem=VMEM_LARGE,
    )(sm, cot, taps, mask, *zs, *ys, *pieces)


def branch_kernel(x_ref, m_ref, w_ref, out_ref):
    out_ref[...] = x_ref[...] + dot(m_ref[...], w_ref[...])


def branch(x, mixed, w_out):
    tokens, width = x.shape
    row = lambda n: pl.BlockSpec((WIDE, n), lambda g: (g, 0))
    return call(
        branch_kernel,
        struct(x.shape),
        grid=(tokens // WIDE,),
        in_specs=[row(width), row(mixed.shape[1]), whole(w_out.shape)],
        out_specs=row(width),
        name="branch",
        us=9.0,
    )(x, mixed, w_out)


def bwd_kernel(
    base, cin_ref, y_ref, dy_ref, taps_ref, ea_ref, eb_ref, cum_ref, cumt_ref, b_ref, c_ref, ct_ref, st_ref, mask_ref, h_ref,
    dcin_ref, grad_ref, dst_ref, db_ref, dc_ref, dcum_ref, ddt_ref, cs_scr, e_scr, et_scr,
):
    group = pl.program_id(0) + base
    tokens = cin_ref.shape[0]
    cs_scr[0:8, :] = jnp.zeros((8, GROUP), f32)
    cs_scr[pl.ds(8, tokens), :] = cin_ref[...].astype(f32)
    fill_spread(e_scr, group)
    row, col = iota((GROUP, 128), 0), iota((GROUP, 128), 1)
    et_scr[...] = jnp.where(col == 4 * group + row // 64, 1.0, 0.0).astype(bf16)
    taps = taps_ref[...]
    m_low, m_high = pair_masks()

    @pl.when(pl.program_id(0) == 0)
    def _():
        for ref in (dst_ref, db_ref, dc_ref, dcum_ref, ddt_ref):
            ref[...] = jnp.zeros(ref.shape, f32)

    def to_heads(v):
        hi = v.astype(bf16)
        lo = (v - hi.astype(f32)).astype(bf16)
        return dot(hi, et_scr[...]) + dot(lo, et_scr[...])

    blocks = tokens // BLOCK

    dstate = jnp.zeros((128, GROUP), f32)
    behind = jnp.zeros((8, GROUP), f32)
    totals = [jnp.zeros((8, GROUP), f32) for _ in range(6)]
    for k in reversed(range(blocks)):
        t0 = k * BLOCK
        more = k < blocks - 1
        rows = pl.ds(t0, BLOCK)
        mask = mask_ref[rows, :]
        conv, shifted = conv_block(cs_scr[pl.ds(t0, BLOCK + 8), :], mask, taps, 4)
        sig = sigmoid(conv)
        v = conv * sig
        ea = dot(ea_ref[rows, :], e_scr[:, : 2 * GROUP])
        wx = dot(eb_ref[rows, :], e_scr[:, 2 * GROUP :])
        dtx, ex = ea[:, :GROUP], ea[:, GROUP:]
        vd_low = (v * dtx).astype(bf16)
        vd = vd_low.astype(f32)
        dy_low = dy_ref[rows, :]
        dy = dy_low.astype(f32)
        skip = taps[5:6]
        h_low = h_ref[rows, :]
        if k > 0:
            dye = (dy * ex).astype(bf16)
            dc_ref[rows, :] += dot_nt(dye, h_low)
        if more:
            dh_low = dstate.astype(bf16)
            db_ref[rows, :] += dot_nt((vd * wx).astype(bf16), dh_low)
            dvd_end = dot(b_ref[rows, :], dh_low) * wx
        cums = pltpu.roll(cum_ref[rows, :], 128 - 4 * group, 1)
        st = st_ref[rows, :]
        inside = []
        dst = jnp.zeros((BLOCK, BLOCK), f32)
        for pair in range(2):
            cols = slice(pair * 128, pair * 128 + 128)
            decays, weights = [], []
            for j in (2 * pair, 2 * pair + 1):
                spread = cumt_ref[0, j : j + 1, rows] - cums[:, j : j + 1]
                decay = jnp.exp2(jnp.minimum(spread, 0.0))
                decays.append(decay)
                weights.append((decay * st).astype(bf16))
            dyp = dy_low[:, cols]
            stack = jnp.concatenate([dyp * m_low, dyp * m_high], axis=0)
            inside.append(dot(jnp.concatenate(weights, axis=1), stack))
            cross = dot_nt(vd_low[:, cols], stack)
            dst = dst + cross[:, :128] * decays[0] + cross[:, 128:] * decays[1]
        dst_ref[rows, :] += dst
        dvd = jnp.concatenate(inside, axis=1)
        through = ex[BLOCK - 1 :]
        if more:
            dvd = dvd + dvd_end
            ends = rows8(vd * dvd_end)
            if k > 0:
                ends = ends + through * rows8(dstate * h_low.astype(f32))
        p = dy * (y_ref[rows, :] - skip * v) - vd * dvd
        if more:
            p = jnp.concatenate([p[: BLOCK - 8], p[BLOCK - 8 :] + jnp.where(iota((8, 1), 0) == 7, jnp.sum(ends, axis=0, keepdims=True), 0.0)], axis=0)
        dcum_ref[rows, :] += to_heads(p)
        ddt_ref[rows, :] += dot((dvd * v).astype(bf16), et_scr[...])
        if k > 0:
            dstate = dstate * through + dot(ct_ref[:, rows], dye)
        dconv = (dvd * dtx + skip * dy) * (sig * (1.0 + conv * (1.0 - sig)))
        window = jnp.concatenate([dconv, behind], axis=0)
        behind = dconv[:8]
        for i, term in enumerate([*[dconv * shifted[3 - i] for i in range(4)], dconv, dy * v]):
            totals[i] = totals[i] + rows8(term)
        dcin_ref[rows, :] = conv_back(
            window, mask_ref[pl.ds(t0, BLOCK + 8), :], taps, 4
        ).astype(bf16)
    rows = [jnp.sum(t, axis=0, keepdims=True) for t in totals]
    grad_ref[...] = jnp.concatenate([*rows, jnp.zeros((2, GROUP), f32)], axis=0)


def bwd(base, count, cin, y, dy, taps, pre, h):
    tokens = cin.shape[0]
    full = lambda a: whole(a.shape)
    ea, eb, cum, cumt, b, c, ct, st, mask = pre
    local = lambda rows: pl.BlockSpec((rows, GROUP), lambda g: (0, g))
    global_ = lambda rows: pl.BlockSpec((rows, GROUP), lambda g: (0, base + g))
    wide = struct((tokens, 128))
    return call(
        functools.partial(bwd_kernel, base),
        [struct((tokens, count * GROUP), bf16), struct((8, count * GROUP))] + [wide] * 5,
        grid=(count,),
        in_specs=[
            local(tokens), local(tokens), global_(tokens), global_(8),
            full(ea), full(eb), full(cum),
            pl.BlockSpec((1, 4, tokens), lambda g: (base + g, 0, 0)),
            full(b), full(c), full(ct), full(st), full(mask), local(tokens),
        ],
        out_specs=[local(tokens), local(8)] + [whole(wide.shape)] * 5,
        scratch=[
            pltpu.VMEM((tokens + 8, GROUP), f32), pltpu.VMEM((128, 3 * GROUP), bf16), pltpu.VMEM((GROUP, 128), bf16),
        ],
        name=f"bwd{base}",
        us=count * 8.4,
    )(cin, y, dy, taps, ea, eb, cum, cumt, b, c, ct, st, mask, h)


def tail_kernel(sm, cin_ref, taps_ref, head_ref, b_ref, c_ref, step_ref, mask_ref, *refs):
    dp_ref, grad_ref, stat_ref, cs_scr, ds_scr = refs[-5:]
    sums = refs[:-5]
    tokens = cin_ref.shape[0]
    cs_scr[0:8, :] = jnp.zeros((8, 256), f32)
    cs_scr[pl.ds(8, tokens), :] = cin_ref[...].astype(f32)
    ds_scr[...] = jnp.zeros(ds_scr.shape, f32)
    taps = taps_ref[...]
    grad_ref[...] = jnp.zeros(grad_ref.shape, f32)
    stat_ref[...] = jnp.zeros(stat_ref.shape, f32)
    blocks = tokens // BLOCK

    def block(step, _):
        k = blocks - 1 - step
        t0 = pl.multiple_of(k * BLOCK, BLOCK)
        rows = pl.ds(t0, BLOCK)
        row, lane = iota((BLOCK, 128), 0), iota((BLOCK, 128), 1)
        dst_sum, db_sum, dc_sum, dcum_sum, ddt_sum = [
            functools.reduce(jnp.add, [ref[rows, :] for ref in sums[i::5]]) for i in range(5)
        ]
        keep = (lane >= row) & (scene_of(lane + t0, sm) == scene_of(row + t0, sm))
        dst = jnp.where(keep, dst_sum, 0.0).astype(bf16)
        db = db_sum + dot(dst, c_ref[rows, :])
        dc = dc_sum + dot_tn(dst, b_ref[rows, :])
        conv, shifted = conv_block(cs_scr[pl.ds(t0, BLOCK + 8), :], mask_ref[rows, :], taps, 4)
        sig = sigmoid(conv)
        dconv = jnp.concatenate([db, dc], axis=1) * (sig * (1.0 + conv * (1.0 - sig)))
        window = jnp.concatenate([dconv, ds_scr[...]], axis=0)
        ds_scr[...] = dconv[:8]
        grads = [jnp.sum(rows8(dconv * shifted[3 - i]), axis=0, keepdims=True) for i in range(4)]
        grads.append(jnp.sum(rows8(dconv), axis=0, keepdims=True))
        grads.append(jnp.zeros((3, 256), f32))
        grad_ref[...] += jnp.concatenate(grads, axis=0)
        dcin = conv_back(window, mask_ref[pl.ds(t0, BLOCK + 8), :], taps, 4)
        upper = jnp.where(lane >= row, 1.0, 0.0)
        dlog = jnp.dot(upper, dcum_sum, precision=highest, preferred_element_type=f32)
        step_in = step_ref[rows, :]
        dt = jnp.maximum(step_in, 0.0) + jnp.log1p(jnp.exp(-jnp.abs(step_in)))
        rate = head_ref[1:2, :]
        dstep = (ddt_sum - dlog * rate) * sigmoid(step_in)
        dalog = -dlog * dt * rate
        stat_ref[...] += jnp.concatenate(
            [
                jnp.sum(rows8(dstep), axis=0, keepdims=True),
                jnp.sum(rows8(dalog), axis=0, keepdims=True),
                jnp.zeros((6, 128), f32),
            ],
            axis=0,
        )
        dp_ref[rows, :] = jnp.concatenate([dcin, dstep], axis=1).astype(bf16)
        return 0

    lax.fori_loop(0, blocks, block, 0, unroll=True)


def tail(sm, cin, taps, inner, head, b, c, step, mask, sums):
    tokens = cin.shape[0]
    args = (cin, taps, head, b, c, step, mask, *sums)
    outs = [struct((tokens, 384), bf16), struct((8, 256)), struct((8, 128))]
    return call(
        tail_kernel,
        outs,
        in_specs=[SMEM] + [whole(a.shape) if a is not taps else bc_taps(inner) for a in args],
        out_specs=[whole(o.shape) for o in outs],
        scratch=[pltpu.VMEM((tokens + 8, 256), f32), pltpu.VMEM((8, 256), f32)],
        name="tail",
        us=8.0,
    )(sm, *args)


def term_kernel(tiles, add, into, sm, left_ref, *refs):
    out_ref = refs[-1]
    parts = refs[: len(tiles)]

    def product(part):
        value = dot(left_ref[...], part[...])
        if add:
            value = value + refs[len(tiles)][:, : part.shape[1]].astype(f32)
        out_ref[:, : part.shape[1]] = value.astype(bf16)

    first = 0
    for part, count in zip(parts, tiles):
        step = pl.program_id(0)
        pl.when((step >= first) & (step < first + count))(functools.partial(product, part))
        first += count


def in_term(half, left, parts, name, add=None, into=None, columns=None):
    halves, width, tokens = left.shape
    n = sum(p.shape[1] for p in parts)
    wide = min(512, n)
    tiles = [pl.cdiv(p.shape[1], wide) for p in parts]
    first = [sum(tiles[:i]) for i in range(len(parts))]
    total = n if columns is None else columns
    at = 0 if into is None else (total - n) // wide
    args = [left, *parts]
    specs = [pl.BlockSpec((None, width, tokens), lambda g, sm: (sm[0], 0, 0))] + [
        pl.BlockSpec(
            (tokens, min(wide, p.shape[1])),
            functools.partial(lambda f, c, g, sm: (0, jnp.clip(g - f, 0, c - 1)), f, c),
        )
        for p, f, c in zip(parts, first, tiles)
    ]
    if add is not None:
        args.append(add)
        specs.append(pl.BlockSpec((width, wide), lambda g, sm: (0, g)))
    aliases = {}
    if into is not None:
        aliases = {len(args) + 1: 0}
        args.append(into)
        specs.append(pl.BlockSpec(memory_space=pl.ANY))
    spec = pltpu.PrefetchScalarGridSpec(
        num_scalar_prefetch=1,
        grid=(sum(tiles),),
        in_specs=specs,
        out_specs=pl.BlockSpec((width, wide), lambda g, sm: (0, at + g)),
    )
    return pl.pallas_call(
        functools.partial(term_kernel, tiles, add is not None, into is not None),
        out_shape=struct((width, total), bf16),
        grid_spec=spec,
        name=name,
        input_output_aliases=aliases,
        compiler_params=pltpu.CompilerParams(vmem_limit_bytes=VMEM_LIMIT, dimension_semantics=("arbitrary",)),
        cost_estimate=cost(width * tokens * n * 5e-9),
    )(half, *args)


def out_kernel(add, sm, left_ref, right_ref, *refs):
    value = dot(left_ref[...], right_ref[...])
    if add:
        value = value + refs[0][...].astype(f32)
    refs[-1][...] = value.astype(bf16)


def out_term(ring, half, flip, cot_low, name, add=None, columns=None):
    inner, tokens = flip.shape
    width = cot_low.shape[1]
    rows = inner // 4
    left = flip.reshape(4, rows, tokens)
    steps = 2 if ring else 4
    out = pl.BlockSpec((rows, width), (lambda g, sm: (0, g)) if ring else (lambda g, sm: (g, 0)))
    args, specs = [left, cot_low], [
        pl.BlockSpec((None, rows, tokens), lambda g, sm: (sm[0] * 2 + g, 0, 0)),
        pl.BlockSpec(cot_low.shape, lambda g, sm: (0, 0)),
    ]
    if add is not None:
        args.append(add)
        specs.append(out)
    spec = pltpu.PrefetchScalarGridSpec(num_scalar_prefetch=1, grid=(steps,), in_specs=specs, out_specs=out)
    return pl.pallas_call(
        functools.partial(out_kernel, add is not None),
        out_shape=struct((rows, columns or 2 * width) if ring else (inner, width), bf16),
        grid_spec=spec,
        name=name,
        compiler_params=pltpu.CompilerParams(vmem_limit_bytes=VMEM_LIMIT, dimension_semantics=("arbitrary",)),
        cost_estimate=cost(5.0),
    )(half, *args)


def last_kernel(count, x_ref, cot_ref, gain_ref, *refs):
    ds, ws, dx_ref = refs[:count], refs[count : 2 * count], refs[-1]
    x = x_ref[...]
    width = x.shape[1]
    dn = functools.reduce(jnp.add, [dot_nt(d[...], w[...]) for d, w in zip(ds, ws)])
    r = lax.rsqrt(jnp.mean(x * x, axis=-1, keepdims=True) + EPS)
    u = dn * gain_ref[0:1, :]
    xr = x * r
    mu = jnp.sum(u * xr, axis=-1, keepdims=True) * (1.0 / width)
    dx_ref[...] = cot_ref[...] + r * (u - xr * mu)


def last(x, cot, gain, pairs):
    tokens, width = x.shape
    row = lambda n: pl.BlockSpec((MID, n), lambda g: (g, 0))
    ds, ws = zip(*pairs)
    n = sum(k for _, k, _ in ds)
    return call(
        functools.partial(last_kernel, len(pairs)),
        struct(x.shape),
        grid=(tokens // MID,),
        in_specs=[row(width), row(width), whole(gain.shape)]
        + [pl.BlockSpec((MID, k), functools.partial(lambda i, g: (g, i), i)) for _, k, i in ds]
        + [pl.BlockSpec((width, k), functools.partial(lambda i, g: (0, i), i)) for _, k, i in ws],
        out_specs=row(width),
        name="last",
        us=18.0,
        vmem=VMEM_LARGE,
    )(x, cot, gain, *[d[0] for d in ds], *[w[0] for w in ws])


Y, CORE, X, Z1, Z2 = 1, 2, 4, 8, 16


def exchange(a, bit):
    return lax.ppermute(a, AXES, [(i, i ^ bit) for i in range(SHARDS)])


def after(a, *others):
    return lax.optimization_barrier((a, *others))[0] if others else a


def together(arrays, *others):
    return list(lax.optimization_barrier((*arrays, *others))[: len(arrays)])


def join(a, got):
    return jnp.concatenate([a, got], axis=0)


def gather_z(own):
    two = join(own, exchange(own, Z1))
    return join(two, exchange(two, Z2))


def take(a, bit, axis):
    return lax.dynamic_index_in_dim(a, bit, axis, keepdims=False)


def scatter_start(keep):
    return [Z2, Z1, X, Y], keep.reshape(2, 2, 2, 2, keep.shape[0] // 16, keep.shape[1])


def scatter_send(place, state, bit):
    names, left = state
    axis = names.index(bit)
    mine = jnp.where((place & bit) > 0, 1, 0)
    names = names[:axis] + names[axis + 1 :]
    return names, take(left, mine, axis), exchange(take(left, 1 - mine, axis), bit)


def scatter_add(sent, got=None):
    names, left, flight = sent
    left = left.astype(f32) + (flight if got is None else got).astype(f32)
    return names, left.astype(bf16) if names else left


def both(a, b):
    return (a.astype(f32) + b.astype(f32)).astype(bf16)


def pad_to(a, rows, columns):
    return jnp.pad(a, ((0, rows - a.shape[0]), (0, columns - a.shape[1])))


def local(
    ring, block_input, cotangent, scene_lengths, norm_gain, in_weight, conv_weight, conv_bias, dt_bias, a_log, skip_gain,
    gated_gain, out_weight,
):
    tokens, width = block_input.shape
    heads = a_log.shape[0]
    inner = out_weight.shape[0] * lax.axis_size(AXES)
    channels = conv_bias.shape[0] * lax.axis_size(AXES)
    proj = in_weight.shape[1]
    bc = proj - 2 * inner
    place = lax.axis_index(AXES).astype(jnp.int32)
    bounds = jnp.cumsum(scene_lengths[0]).astype(jnp.int32)
    sm = jnp.concatenate([bounds, place[None], jnp.zeros((4,), jnp.int32)])
    groups = inner // GROUP

    def pack(grads, gg, stat):
        d_skip = jnp.sum(grads[5, :inner].reshape(heads, -1), axis=1)
        side = jnp.concatenate([stat[0, :heads], stat[1, :heads], d_skip])[None]
        return jnp.concatenate([grads[:5], pad_to(jnp.sum(gg, axis=0)[None], 1, channels), pad_to(side, 2, channels)], axis=0)

    gather = lambda a: lax.all_gather(a.astype(bf16), AXES, axis=0, tiled=True)
    skip_row = jnp.repeat(skip_gain, inner // heads)[None]
    w_low = in_weight.astype(bf16)
    if ring:
        small = jnp.concatenate(
            [
                jnp.concatenate([norm_gain, gated_gain])[None],
                pad_to(conv_weight.T, 4, 96),
                pad_to(conv_bias[None], 27, 96),
            ],
            axis=0,
        )
        first = jnp.concatenate([w_low[:, 2 * inner :], small.astype(bf16)], axis=1)
        wide = inner // 2
        one, two = [
            jnp.concatenate([w_low[:, at : at + wide], w_low[:, inner + at : inner + at + wide]], axis=1)
            for at in (0, wide)
        ]
        halves = lambda a: [a[:, : a.shape[1] // 2], a[:, a.shape[1] // 2 :]]
        outward = lambda a, bits: [exchange(part, bit) for part, bit in zip(a, bits)]
        joined = lambda a, got: [join(part, came) for part, came in zip(a, got)]
        row = join(first, exchange(first, Z1))
        row, one = joined([row, one], together([exchange(row, Z2), exchange(one, Z1)]))
        two = after(two, row)
        row, one, two = joined([row, one, two], together([exchange(row, X), exchange(one, Z2), exchange(two, Z1)]))
        two_flight = exchange(two, Z2)
        one = halves(one)
        row, *one = joined([row, *one], together([exchange(row, Y), *outward(one, (X, Y))]))
        one_flights = outward(one, (Y, X))
        w_bc, taps, gain = unpack(sm, [row, exchange(row, CORE)], skip_row, channels, width)
        two = halves(join(two, together([two_flight], w_bc)[0]))
        two_flights = outward(two, (X, Y))
        x_first = after(block_input, *two)
    else:
        in_full, outside, x_first = gather(in_weight), [gather(out_weight)], block_input
        norm_full, conv_full, bias_full, gated_full = map(gather, (norm_gain, conv_weight, conv_bias, gated_gain))
        gain = jnp.broadcast_to(norm_full.astype(f32)[None], (8, width))
        w_bc = pad_to(in_full[:, 2 * inner :], width, 384)
        taps = jnp.concatenate(
            [
                conv_full.astype(f32).T,
                bias_full.astype(f32)[None],
                pad_to(jnp.concatenate([skip_row, gated_full.astype(f32)[None]], axis=0), 3, channels),
            ],
            axis=0,
        )
    head = jnp.pad(jnp.stack([dt_bias, jnp.exp(a_log)]), ((0, 6), (0, 128 - heads)))
    (normed, normt, cin_bc, b, c, bt, ct, s, st, cum, cumt, ea, eb, step, mask) = prep(
        ring, sm, x_first, gain, w_bc, taps, inner, head, heads
    )
    pre = (ea, eb, cum, cumt, c, bt, s, mask)
    def scan(base, count, offset, *w, first=(), **more):
        return fwd(base, count, offset, ring, sm, after(normed, *first), *w, inner, taps, pre, **more)

    if ring:
        half, quarter = groups // 2, groups // 4
        pairs = lambda a, got: list(zip(a, got))
        one = joined(one, together(one_flights, normed))
        out = after(out_weight, one[0]).astype(bf16)
        got = together([*outward(one, (CORE, CORE)), *two_flights, exchange(out, Z1)])
        two, out = joined(two, got[2:4]), join(out, got[4])
        got = got[:2]
        two_flights = outward(two, (Y, X))
        front = pairs(one, got)
        out_flight = exchange(out, Z2)
        near = scan(0, quarter, 0, *front, first=[out, *two])
        *got, came = together([*two_flights, out_flight], near[2])
        two, out = joined(two, got), halves(join(out, came))
        flights = outward(two, (CORE, CORE)) + outward(out, (X, Y))
        next_ = scan(quarter, quarter, quarter, *front, first=[*two, *out])
        got = together(flights, next_[2])
        back, out = pairs(two, got[:2]), joined(out, got[2:])
        flights = outward(out, (Y, X))
        far = scan(half, quarter, 0, *back, first=out, total=half)
        out = joined(out, together(flights, far[2]))
        flights = outward(out, (CORE, CORE))
        far = scan(half + quarter, quarter, quarter, *back, first=out, total=half, into=far)
        got = together(flights, far[2])
        outside = [out[0], got[0], out[1], got[1]]
        runs = [(0, quarter, near), (quarter, quarter, next_), (half, half, far)]
    else:
        runs = [(0, groups, scan(0, groups, 0, [in_full], [in_full]))]
    mixed, dz, dy, gg, flip, cot_low, *w_out = mid(
        ring, sm, cotangent, outside, inner, taps, mask, [r[0] for *_, r in runs], [r[2] for *_, r in runs]
    )
    out_full = w_out[0] if ring else outside[0]
    normt = normt.reshape(2 if ring else 1, -1, tokens)
    core = sm[3:4] >> 1 & 1
    if ring:
        sent = out_term(ring, 1 - core, flip, cot_low, "out_away")
        out_away = exchange(sent, CORE)
        sent = in_term(1 - core, normt, [after(dz, sent)], "gate_away")
        gate_away = exchange(sent, CORE)
        out_here = out_term(ring, core, flip, cot_low, "out_here", after(out_away, sent))
        gate_here = in_term(core, normt, [dz], "gate_here", after(gate_away, out_here))
        outs, gates = scatter_start(out_here), scatter_start(gate_here)
        dy = after(dy, gate_here)
    pre = (ea, eb, cum, cumt, b, c, ct, st, mask)
    scan = lambda dy, base, count, run: bwd(base, count, run[1], run[2], dy, taps, pre, run[3])
    finish = lambda sums: tail(sm, cin_bc, taps, inner, head, b, c, step, mask, sums)
    if ring:

        def term(parts, name):
            away = exchange(in_term(1 - core, normt, parts, name + "_away"), CORE)
            return scatter_start(both(in_term(core, normt, parts, name + "_here"), away))

        send = functools.partial(scatter_send, place)
        gates, outs = send(gates, X), send(outs, Y)
        back = scan(dy, *runs[2])
        one, two = together([gates[2], outs[2]], back[0])
        gates, outs = send(scatter_add(gates, one), Y), send(scatter_add(outs, two), X)
        near = scan(after(dy, gates[1], outs[1], back[0]), *runs[0])
        one, two = together([gates[2], outs[2]], near[0])
        gates, outs = scatter_add(gates, one), scatter_add(outs, two)
        early = send((gates[0], jnp.concatenate([gates[1], outs[1]], axis=-1)), Z2)
        parts = [near[0], after(back[0], early[1])]
        away = in_term(1 - core, normt, parts, "late_away")
        here = in_term(core, normt, parts, "late_here")
        late = send(scatter_start(both(here, exchange(away, CORE))), X)
        mid_out = scan(after(dy, late[1], near[0]), *runs[1])
        sums = [a for out in (back, near, mid_out) for a in out[2:]]
        (one,) = together([late[2]], mid_out[0])
        late = send(scatter_add(late, one), Y)
        sums[0] = after(sums[0], late[1])
        dbc, grad_bc, stat = finish(sums)
        grads = jnp.concatenate([near[1], mid_out[1], back[1], grad_bc], axis=1)
        one, two = together([early[2], late[2]], dbc)
        early, late = send(scatter_add(early, one), Z1), send(scatter_add(late, two), Z2)
        small = pack(grads, gg, stat)
        flight = exchange(small, CORE)
        parts = [mid_out[0], after(dbc, early[1], late[1], small)]
        away = in_term(1 - core, normt, parts, "last_away")
        here = in_term(core, normt, parts, "last_here")
        one, two, flight = together([early[2], late[2], flight], here)
        early, late, small = scatter_add(early, one), send(scatter_add(late, two), Z1), small + flight
        flight = exchange(small, X)
        final = send(scatter_start(both(here, exchange(away, CORE))), X)
        x_last = after(block_input, final[1], small, late[1])
        pairs = []
        for (base, count, run), (dv, *_) in zip(runs, (near, mid_out, back)):
            wide = count * GROUP
            pairs.append(((dz, wide, base // count), (run[4], wide, 0)))
            pairs.append(((dv, wide, 0), (run[5], wide, 0)))
        x_last = after(block_input, final[1], small, late[1])
    else:
        scatter = lambda a: lax.psum_scatter(a.astype(f32), AXES, scatter_dimension=0, tiled=True)
        dv, grad, *sums = scan(dy, *runs[0])
        dbc, grad_bc, stat = finish(sums)
        grads = jnp.concatenate([grad, grad_bc], axis=1)
        in_grad = scatter(in_term(core * 0, normt, [dz, dv, dbc], "all")[:, :proj])
        out_grad = scatter(out_term(ring, core * 0, flip, cot_low, "out"))
        pairs = [((dz, inner, 0), (in_full, inner, 0)), ((dv, inner, 0), (in_full, inner, 1))]
        x_last = block_input
    pairs.append(((dbc, 384, 0), (w_bc, 384, 0)))
    input_grad = last(x_last, cotangent, gain, pairs)
    if ring:
        one, two, flight = together([late[2], final[2], flight], input_grad)
        late, final, small = scatter_add(late, one), send(scatter_add(final, two), Y), small + flight
        flight = exchange(small, Y)
        mixed = after(mixed, final[1], small)
    block_output = branch(block_input, mixed, out_full)
    if ring:
        one, flight = together([final[2], flight], block_output)
        final, small = send(scatter_add(final, one), Z2), small + flight
        small = small + exchange(small, Z1)
        final = scatter_add(send(scatter_add(final), Z1))
        small = small + exchange(small, Z2)
        gate_grad, out_grad = early[1][:, :inner], early[1][:, inner:]
        out_grad = jnp.concatenate([out_grad[:, :width], out_grad[:, width:]], axis=0)
        near, half = inner // 4, inner // 2
        in_grad = jnp.concatenate(
            [gate_grad, late[1][:, :near], final[1][:, :near], late[1][:, near:], final[1][:, near : near + bc]], axis=1
        )
    else:
        small = lax.psum(pack(grads, gg, stat), AXES)
    d_gain = jnp.sum(in_grad * w_low.astype(f32), axis=1) / norm_gain.astype(bf16).astype(f32)
    part = lambda row, n: lax.dynamic_slice_in_dim(row, place * n, n, axis=-1)
    side = small[6]
    return (
        block_output,
        input_grad,
        d_gain,
        in_grad,
        part(small[:4], conv_bias.shape[0]).T,
        part(small[4], conv_bias.shape[0]),
        side[:heads],
        side[heads : 2 * heads],
        side[2 * heads : 3 * heads],
        part(small[5], gated_gain.shape[0]),
        out_grad,
    )


def solution(mesh):
    dp, fsdp = mesh.devices.shape
    split = jax.sharding.Mesh(mesh.devices.reshape(dp // 2, 2, fsdp), AXES)
    row = P(AXES, None)
    flat = P(AXES)
    return jax.shard_map(
        functools.partial(local, (dp, fsdp) == (16, 2)),
        mesh=split,
        in_specs=(row, row, row, flat, row, row, flat, P(), P(), P(), flat, row),
        out_specs=(row, row, flat, row, row, flat, P(), P(), P(), flat, row),
        check_vma=False,
    )
```

```python
import functools

import jax
import jax.numpy as jnp
from jax import lax
from jax.experimental import pallas as pl
from jax.experimental.pallas import tpu as pltpu
from jax.sharding import PartitionSpec as P

AXES = ("chip", "core", "fsdp")
CHIPS = ("chip", "fsdp")
SHARDS = 32
PIECES = 2
BLOCK = 128
GROUP = 256
EPS = 1e-05
LOG2E = 1.4426950408889634
VMEM_LIMIT = 50 * 1024 * 1024
VMEM_LARGE = 56 * 1024 * 1024
f32 = jnp.float32
bf16 = jnp.bfloat16
highest = lax.Precision.HIGHEST


def dot(a, b):
    return jnp.dot(a, b, preferred_element_type=f32)


def dot_nt(a, b):
    return lax.dot_general(a, b, (((1,), (1,)), ((), ())), preferred_element_type=f32)


def dot_tn(a, b):
    return lax.dot_general(a, b, (((0,), (0,)), ((), ())), preferred_element_type=f32)


def sigmoid(v):
    return 0.5 * jnp.tanh(0.5 * v) + 0.5


def iota(shape, axis):
    return lax.broadcasted_iota(jnp.int32, shape, axis)


def rows8(v):
    return jnp.sum(v.reshape(v.shape[0] // 8, 8, v.shape[1]), axis=0)


def scene_of(place, sm):
    scene = jnp.zeros(place.shape, jnp.int32)
    for i in range(3):
        scene = scene + jnp.where(place >= sm[i], 1, 0)
    return scene


def cost(us):
    return pl.CostEstimate(flops=0, bytes_accessed=int(us * 3.69e6), transcendentals=0)


def call(kernel, out, grid=None, in_specs=None, out_specs=None, scratch=(), name=None, us=1.0, aliases=None, vmem=VMEM_LIMIT):
    return pl.pallas_call(
        kernel,
        out_shape=out,
        grid=grid or (1,),
        in_specs=in_specs,
        out_specs=out_specs,
        scratch_shapes=scratch,
        name=name,
        compiler_params=pltpu.CompilerParams(
            vmem_limit_bytes=vmem, dimension_semantics=("arbitrary",)
        ),
        cost_estimate=cost(us),
        input_output_aliases=aliases or {},
    )


def whole(shape):
    return pl.BlockSpec(shape, lambda g: (0,) * len(shape))


def bc_taps(inner):
    return pl.BlockSpec((8, 256), lambda g: (0, inner // 256))


SMEM = pl.BlockSpec(memory_space=pltpu.SMEM)


def struct(shape, dtype=f32):
    return jax.ShapeDtypeStruct(shape, dtype)


def conv_block(window, masks, taps, width):
    current = window[8:]
    total = taps[4:5] + current * taps[3:4]
    shifted = [current]
    for off in range(1, width):
        moved = window[8 - off : 8 - off + BLOCK] * masks[:, off - 1 : off]
        shifted.append(moved)
        total = total + moved * taps[width - 1 - off : width - off]
    return total, shifted


def conv_back(window, masks, taps, width):
    total = window[:BLOCK] * taps[width - 1 : width]
    for off in range(1, width):
        moved = pltpu.roll(window * masks[:, off - 1 : off], window.shape[0] - off, 0)[:BLOCK]
        total = total + moved * taps[width - 1 - off : width - off]
    return total


def unpack_kernel(sm, *refs):
    pieces, (skip_ref, w_ref, taps_ref, gain_ref) = refs[:PIECES], refs[PIECES:]
    assemble(sm, pieces, w_ref, 32, True)
    row, col = iota((8 * SHARDS, 32 * SHARDS), 0), iota((8 * SHARDS, 32 * SHARDS), 1)
    pick = jnp.where(col == (row & (SHARDS - 1)) * 32 + row // SHARDS, 1.0, 0.0).astype(bf16)
    packed = dot(pick, w_ref[:, 256:384]).astype(bf16)

    def spread(kind, lane, size):
        total = size * SHARDS
        place = iota((1, total), 1)
        owner, within = place // size, place % size
        copy = jnp.where(iota((128, total), 0) == within + lane, 1.0, 0.0).astype(bf16)
        values = dot(packed[kind * SHARDS : (kind + 1) * SHARDS, :], copy)
        return jnp.sum(jnp.where(iota((SHARDS, total), 0) == owner, values, 0.0), axis=0, keepdims=True)

    taps_ref[...] = jnp.zeros(taps_ref.shape, f32)
    gain_ref[...] = jnp.broadcast_to(spread(0, 32, 32), gain_ref.shape)
    inner = skip_ref.shape[1]
    taps_ref[6:7, :inner] = spread(0, 64, inner // SHARDS)
    channels = taps_ref.shape[1]
    for k in range(5):
        taps_ref[k : k + 1, :] = spread(k + 1, 32, channels // SHARDS)
    taps_ref[5:6, :inner] = skip_ref[0:1, :]


def unpack(sm, pieces, skip, channels, width):
    outs = [struct((width, 384), bf16), struct((8, channels)), struct((8, width))]
    return call(
        unpack_kernel,
        outs,
        in_specs=[SMEM] + [whole(a.shape) for a in (*pieces, skip)],
        out_specs=[whole(o.shape) for o in outs],
        name="unpack",
        us=3.0,
    )(sm, *pieces, skip)


def core_first(shard):
    return (shard >> 1 & 1) * 16 + (shard >> 2) * 2 + (shard & 1)


def prep_kernel(
    ring, sm, x_ref, gain_ref, w_ref, taps_ref, head_ref,
    normed_ref, normt_ref, cin_ref, b_ref, c_ref, bt_ref, ct_ref, s_ref, st_ref,
    cum_ref, cumt_ref, ea_ref, eb_ref, step_ref, mask_ref, cs_scr,
):
    tokens = x_ref.shape[0]
    x = x_ref[...]
    scale = lax.rsqrt(jnp.mean(x * x, axis=-1, keepdims=True) + EPS)
    normed_low = (x * scale * gain_ref[0:1, :]).astype(bf16)
    normed_ref[...] = normed_low
    flipped = normed_low.astype(f32).T.astype(bf16)
    if ring:
        for shard in range(SHARDS):
            at = core_first(shard) * 32
            normt_ref[at : at + 32, :] = flipped[shard * 32 : shard * 32 + 32, :]
    else:
        normt_ref[...] = flipped
    proj = dot(normed_low, w_ref[...])
    lanes = iota((1, 128), 1)
    heads = 4 * cumt_ref.shape[0]
    is_head = lanes < heads
    cin_low = proj[:, :256].astype(bf16)
    cin_ref[...] = cin_low
    cs_scr[0:8, :] = jnp.zeros((8, 256), f32)
    cs_scr[pl.ds(8, tokens), :] = cin_low.astype(f32)
    step_ref[...] = jnp.where(is_head, proj[:, 256:384] + head_ref[0:1, :], 0.0)
    taps = taps_ref[...]

    for k in range(tokens // BLOCK):
        t0 = k * BLOCK
        rows = pl.ds(t0, BLOCK)
        place = iota((BLOCK, 128), 0) + t0
        lane = iota((BLOCK, 128), 1)
        scene = scene_of(place, sm)
        before = place - lane - 1
        same = (before >= 0) & (scene_of(before, sm) == scene)
        mask = jnp.where(lane < 3, jnp.where(same, 1.0, 0.0), jnp.where(place < sm[2], 1.0, 0.0))
        mask_ref[rows, :] = mask
        conv, _ = conv_block(cs_scr[pl.ds(t0, BLOCK + 8), :], mask, taps, 4)
        act = conv * sigmoid(conv)
        b_low = act[:, :128].astype(bf16)
        c_low = act[:, 128:].astype(bf16)
        b_ref[rows, :] = b_low
        c_ref[rows, :] = c_low
        bt_ref[:, rows] = act[:, :128].T.astype(bf16)
        ct_ref[:, rows] = act[:, 128:].T.astype(bf16)
        other = scene_of(lane + t0, sm)
        low = (lane + t0 <= place) & (other == scene)
        s_ref[rows, :] = jnp.where(low, dot_nt(c_low, b_low), 0.0)
        high = (lane + t0 >= place) & (other == scene)
        st_ref[rows, :] = jnp.where(high, dot_nt(b_low, c_low), 0.0)
        step = step_ref[rows, :]
        dt = jnp.maximum(step, 0.0) + jnp.log1p(jnp.exp(-jnp.abs(step)))
        dt = jnp.where(is_head, dt, 0.0)
        log_decay = dt * (head_ref[1:2, :] * -LOG2E)
        lower = jnp.where(lane <= iota((BLOCK, 128), 0), 1.0, 0.0)
        cum = jnp.dot(lower, log_decay, precision=highest, preferred_element_type=f32)
        cum_ref[rows, :] = cum
        flat = cum.T
        for i in range(heads // 4):
            cumt_ref[i, :, rows] = flat[4 * i : 4 * i + 4, :]
        first = jnp.full((1, 128), t0 - 1, jnp.int32)
        last = jnp.full((1, 128), t0 + BLOCK - 1, jnp.int32)
        entering = (scene_of(first, sm) == scene) & (first >= 0) & is_head
        final = (scene_of(last, sm) == scene) & is_head
        grow = jnp.where(entering, jnp.exp2(cum), 0.0)
        end = jnp.where(final, jnp.exp2(cum[BLOCK - 1 :] - cum), 0.0)

        def packed(v):
            hi = v.astype(bf16).astype(f32)
            return hi + pltpu.roll((v - hi).astype(bf16).astype(f32), 32, 1)

        ea_ref[rows, :] = (packed(dt) + pltpu.roll(packed(grow), 64, 1)).astype(bf16)
        eb_ref[rows, :] = packed(end).astype(bf16)
    mask_ref[pl.ds(tokens, 8), :] = jnp.zeros((8, 128), f32)


def prep(ring, sm, x, gain, w_bc, taps, inner, head, heads):
    tokens, width = x.shape
    wide = (tokens, 128)
    outs = [
        struct(x.shape, bf16), struct((width, tokens), bf16), struct((tokens, 256), bf16),
        struct(wide, bf16), struct(wide, bf16), struct((128, tokens), bf16), struct((128, tokens), bf16),
        struct(wide), struct(wide), struct(wide), struct((heads // 4, 4, tokens)), struct(wide, bf16), struct(wide, bf16),
        struct(wide), struct((tokens + 8, 128)),
    ]
    args = (x, gain, w_bc, taps, head)
    return call(
        functools.partial(prep_kernel, ring),
        outs,
        in_specs=[SMEM] + [whole(a.shape) if a is not taps else bc_taps(inner) for a in args],
        out_specs=[whole(o.shape) for o in outs],
        scratch=[pltpu.VMEM((tokens + 8, 256), f32)],
        name="prep",
        us=13.0,
    )(sm, *args)


def fill_spread(e_scr, group):
    row = iota((128, 768), 0)
    col = iota((128, 768), 1)
    head = 4 * group + (col % GROUP) // 64
    part = jnp.where(col < GROUP, 0, jnp.where(col < 2 * GROUP, 64, 0))
    hit = (row == head + part) | (row == head + part + 32)
    e_scr[...] = jnp.where(hit, 1.0, 0.0).astype(bf16)


def pair_masks():
    low = jnp.where(iota((1, 128), 1) < 64, 1.0, 0.0).astype(bf16)
    high = jnp.where(iota((1, 128), 1) < 64, 0.0, 1.0).astype(bf16)
    return low, high


def assemble(sm, pieces, out_ref, block, x_first, columns=slice(None)):
    low, high = (4, 1) if x_first else (1, 4)
    for core, piece in enumerate(pieces):
        for j in range(SHARDS // 2):
            shard = sm[3] ^ (core << 1 | (j & 3) << 3 | (j >> 2 & 1) * low | (j >> 3) * high)
            out_ref[pl.ds(pl.multiple_of(shard * block, block), block), columns] = piece[j * block : (j + 1) * block, :]


def fwd_kernel(*refs):
    base, ring, into, sm = refs[:4]
    refs = refs[1:]
    if ring:
        n = PIECES
        gates, values = refs[3 : 3 + n], refs[3 + n : 3 + 2 * n]
        rest = list(refs[3 + 2 * n :])
        if into:
            del rest[10:16]
        wv_ref, wg_ref = rest.pop(15), rest.pop(14)
        assemble(sm, gates, wg_ref, 32, True)
        assemble(sm, values, wv_ref, 32, False)
        rest[1:1] = [wg_ref, wv_ref]
    else:
        rest = list(refs[5:])
        rest[1:1] = refs[3:5]
    fwd_body(base, *rest)


def fwd_body(
    base, normed_ref, wg_ref, wv_ref, taps_ref, ea_ref, eb_ref, cum_ref, cumt_ref, c_ref, bt_ref, s_ref, mask_ref,
    z_ref, cin_ref, y_ref, h_ref, cs_scr, e_scr, x_scr,
):
    group = pl.program_id(0) + base
    tokens = normed_ref.shape[0]
    normed = normed_ref[...]
    z_ref[...] = dot(normed, wg_ref[...]).astype(bf16)
    cin_low = dot(normed, wv_ref[...]).astype(bf16)
    cin_ref[...] = cin_low
    cs_scr[0:8, :] = jnp.zeros((8, GROUP), f32)
    cs_scr[pl.ds(8, tokens), :] = cin_low.astype(f32)
    fill_spread(e_scr, group)
    x_scr[:, : 2 * GROUP] = dot(ea_ref[...], e_scr[:, : 2 * GROUP])
    x_scr[:, 2 * GROUP :] = dot(eb_ref[...], e_scr[:, 2 * GROUP :])
    taps = taps_ref[...]
    m_low, m_high = pair_masks()

    state = jnp.zeros((128, GROUP), f32)
    blocks = tokens // BLOCK
    for k in range(blocks):
        t0 = k * BLOCK
        rows = pl.ds(t0, BLOCK)
        mask = mask_ref[rows, :]
        conv, _ = conv_block(cs_scr[pl.ds(t0, BLOCK + 8), :], mask, taps, 4)
        v = conv * sigmoid(conv)
        dtx, ex, wx = [x_scr[rows, i * GROUP : (i + 1) * GROUP] for i in range(3)]
        vd_low = (v * dtx).astype(bf16)
        h_low = state.astype(bf16)
        h_ref[rows, :] = h_low
        cums = pltpu.roll(cum_ref[rows, :], 128 - 4 * group, 1)
        s = s_ref[rows, :]
        inside = []
        for pair in range(2):
            weights = []
            for j in (2 * pair, 2 * pair + 1):
                spread = cums[:, j : j + 1] - cumt_ref[0, j : j + 1, rows]
                weights.append((jnp.exp2(jnp.minimum(spread, 0.0)) * s).astype(bf16))
            vp = vd_low[:, pair * 128 : pair * 128 + 128]
            stack = jnp.concatenate([vp * m_low, vp * m_high], axis=0)
            inside.append(dot(jnp.concatenate(weights, axis=1), stack))
        y = jnp.concatenate(inside, axis=1) + taps[5:6] * v
        if k > 0:
            y = y + dot(c_ref[rows, :], h_low) * ex
        y_ref[rows, :] = y
        if k < blocks - 1:
            fresh = dot(bt_ref[:, rows], (vd_low.astype(f32) * wx).astype(bf16))
            state = state * ex[BLOCK - 1 :] + fresh


def fwd(base, count, offset, ring, sm, normed, gates, values, inner, taps, pre, total=None, into=()):
    tokens, width = normed.shape
    full = lambda a: whole(a.shape)
    ea, eb, cum, cumt, c, bt, s, mask = pre
    first = inner // GROUP
    at = (total or count) - count if into else 0
    col = lambda rows, dtype: struct((rows, (total or count) * GROUP), dtype)
    block = lambda rows: pl.BlockSpec((rows, GROUP), lambda g: (0, at + g))
    outs = [col(tokens, bf16), col(tokens, bf16), col(tokens, f32), col(tokens, bf16)]
    if ring:
        w_specs = [pl.BlockSpec((a.shape[0], GROUP), lambda g: (0, offset + g)) for a in (*gates, *values)]
        outs += [col(width, bf16)] * 2
    else:
        w_specs = [
            pl.BlockSpec((width, GROUP), lambda g: (0, base + g)),
            pl.BlockSpec((width, GROUP), lambda g: (0, first + base + g)),
        ]
    return call(
        functools.partial(fwd_kernel, base, ring, bool(into)),
        outs,
        grid=(count,),
        in_specs=[SMEM] + w_specs + [
            full(normed),
            pl.BlockSpec((8, GROUP), lambda g: (0, base + g)),
            full(ea), full(eb), full(cum),
            pl.BlockSpec((1, 4, tokens), lambda g: (base + g, 0, 0)),
            full(c), full(bt), full(s), full(mask),
        ] + [pl.BlockSpec(memory_space=pl.ANY)] * len(into),
        out_specs=[block(o.shape[0]) for o in outs],
        aliases={11 + 2 * len(gates) + i: i for i in range(len(into))},
        scratch=[pltpu.VMEM((tokens + 8, GROUP), f32), pltpu.VMEM((128, 3 * GROUP), bf16), pltpu.VMEM((tokens, 3 * GROUP), f32)],
        name=f"fwd{base}",
        us=count * 6.6,
    )(sm, *gates, *values, normed, taps, ea, eb, cum, cumt, c, bt, s, mask, *into)


MID = 256
WIDE = 256
MID_C = 512


def mid_kernel(ring, chunks, sm, cot_ref, taps_ref, mask_ref, *refs):
    zs, ys = refs[:chunks], refs[chunks : 2 * chunks]
    *pieces, mixed_ref, dz_ref, dy_ref, gg_ref, flip_ref, low_ref, w_ref, g_scr, u_scr = refs[2 * chunks :]
    if not ring:
        pieces, w_ref = [], pieces[0]
    half = w_ref.shape[1] // 2

    @pl.when(pl.program_id(0) == 0)
    def _():
        gg_ref[...] = jnp.zeros(gg_ref.shape, f32)
        if ring:
            assemble(sm, pieces[:PIECES], w_ref, 64, True, slice(0, half))
            assemble(sm, pieces[PIECES:], w_ref, 64, False, slice(half, 2 * half))

    inner = dz_ref.shape[1]
    alive = mask_ref[:, 3:4]
    cot_low = cot_ref[...].astype(bf16)
    low_ref[...] = cot_low
    square = jnp.zeros((MID, 128), f32)
    parts = [slice(i, i + MID_C) for i in range(0, inner, MID_C)]
    here = [(z, y, slice(i, i + MID_C)) for z, y in zip(zs, ys) for i in range(0, z.shape[1], MID_C)]
    for part, (z_ref, y_ref, cut) in zip(parts, here):
        z = z_ref[:, cut].astype(f32)
        g = y_ref[:, cut] * (z * sigmoid(z))
        g_scr[:, part] = g
        sq = g * g
        for i in range(0, MID_C, 128):
            square = square + sq[:, i : i + 128]
    r = lax.rsqrt(jnp.sum(square, axis=-1, keepdims=True) * (1.0 / inner) + EPS)
    r_alive = r * alive
    cross = jnp.zeros((MID, 128), f32)
    for part in parts:
        gain = taps_ref[6:7, part]
        dm = dot_nt(cot_low, w_ref[part, :])
        g = g_scr[:, part]
        u = dm * gain
        u_scr[:, part] = u
        ug = u * g
        for i in range(0, MID_C, 128):
            cross = cross + ug[:, i : i + 128]
        gr = g * r_alive
        mixed = gr * gain
        mixed_ref[:, part] = mixed.astype(bf16)
        gg_ref[:, part] += rows8(dm * gr)
        flipped = mixed.T.astype(bf16)
        for i in range(0, MID_C, 32):
            shard, half = (part.start + i) // 64, i // 32 % 2
            place = core_first(shard) // 16 * 32 + half * 16 + core_first(shard) % 16 if ring else (part.start + i) // 32
            flip_ref[place * 32 : place * 32 + 32, :] = flipped[i : i + 32, :]
    r3 = r_alive * r * r * (jnp.sum(cross, axis=-1, keepdims=True) * (1.0 / inner))
    for part, (z_ref, y_ref, cut) in zip(parts, here):
        z = z_ref[:, cut].astype(f32)
        sig = sigmoid(z)
        dg = u_scr[:, part] * r_alive - g_scr[:, part] * r3
        silu = z * sig
        dy_ref[:, part] = (dg * silu).astype(bf16)
        dz_ref[:, part] = (dg * y_ref[:, cut] * (sig + silu * (1.0 - sig))).astype(bf16)


def mid(ring, sm, cot, pieces, inner, taps, mask, zs, ys):
    tokens, width = cot.shape
    row = lambda n: pl.BlockSpec((MID, n), lambda g: (g, 0))
    wide = struct((tokens, inner), bf16)
    outs = [wide, wide, wide, struct((8, inner)), struct((inner, tokens), bf16), struct(cot.shape, bf16)]
    outs.append(struct((inner, width) if ring else (8, 128), bf16))
    return call(
        functools.partial(mid_kernel, ring, len(zs)),
        outs,
        grid=(tokens // MID,),
        in_specs=[SMEM, row(width), whole(taps.shape), row(128)]
        + [row(a.shape[1]) for a in (*zs, *ys)]
        + [whole(a.shape) for a in pieces],
        out_specs=[row(inner)] * 3 + [whole((8, inner)), pl.BlockSpec((inner, MID), lambda g: (0, g)), row(width), whole(outs[-1].shape)],
        scratch=[pltpu.VMEM((MID, inner), f32), pltpu.VMEM((MID, inner), f32)],
        name="mid",
        us=25.0,
        vmem=VMEM_LARGE,
    )(sm, cot, taps, mask, *zs, *ys, *pieces)


def branch_kernel(x_ref, m_ref, w_ref, out_ref):
    out_ref[...] = x_ref[...] + dot(m_ref[...], w_ref[...])


def branch(x, mixed, w_out):
    tokens, width = x.shape
    row = lambda n: pl.BlockSpec((WIDE, n), lambda g: (g, 0))
    return call(
        branch_kernel,
        struct(x.shape),
        grid=(tokens // WIDE,),
        in_specs=[row(width), row(mixed.shape[1]), whole(w_out.shape)],
        out_specs=row(width),
        name="branch",
        us=9.0,
    )(x, mixed, w_out)


def bwd_kernel(
    base, cin_ref, y_ref, dy_ref, taps_ref, ea_ref, eb_ref, cum_ref, cumt_ref, b_ref, c_ref, ct_ref, st_ref, mask_ref, h_ref,
    dcin_ref, grad_ref, dst_ref, db_ref, dc_ref, dcum_ref, ddt_ref, cs_scr, e_scr, et_scr,
):
    group = pl.program_id(0) + base
    tokens = cin_ref.shape[0]
    cs_scr[0:8, :] = jnp.zeros((8, GROUP), f32)
    cs_scr[pl.ds(8, tokens), :] = cin_ref[...].astype(f32)
    fill_spread(e_scr, group)
    row, col = iota((GROUP, 128), 0), iota((GROUP, 128), 1)
    et_scr[...] = jnp.where(col == 4 * group + row // 64, 1.0, 0.0).astype(bf16)
    taps = taps_ref[...]
    m_low, m_high = pair_masks()

    @pl.when(pl.program_id(0) == 0)
    def _():
        for ref in (dst_ref, db_ref, dc_ref, dcum_ref, ddt_ref):
            ref[...] = jnp.zeros(ref.shape, f32)

    def to_heads(v):
        hi = v.astype(bf16)
        lo = (v - hi.astype(f32)).astype(bf16)
        return dot(hi, et_scr[...]) + dot(lo, et_scr[...])

    blocks = tokens // BLOCK

    dstate = jnp.zeros((128, GROUP), f32)
    behind = jnp.zeros((8, GROUP), f32)
    totals = [jnp.zeros((8, GROUP), f32) for _ in range(6)]
    for k in reversed(range(blocks)):
        t0 = k * BLOCK
        more = k < blocks - 1
        rows = pl.ds(t0, BLOCK)
        mask = mask_ref[rows, :]
        conv, shifted = conv_block(cs_scr[pl.ds(t0, BLOCK + 8), :], mask, taps, 4)
        sig = sigmoid(conv)
        v = conv * sig
        ea = dot(ea_ref[rows, :], e_scr[:, : 2 * GROUP])
        wx = dot(eb_ref[rows, :], e_scr[:, 2 * GROUP :])
        dtx, ex = ea[:, :GROUP], ea[:, GROUP:]
        vd_low = (v * dtx).astype(bf16)
        vd = vd_low.astype(f32)
        dy_low = dy_ref[rows, :]
        dy = dy_low.astype(f32)
        skip = taps[5:6]
        h_low = h_ref[rows, :]
        if k > 0:
            dye = (dy * ex).astype(bf16)
            dc_ref[rows, :] += dot_nt(dye, h_low)
        if more:
            dh_low = dstate.astype(bf16)
            db_ref[rows, :] += dot_nt((vd * wx).astype(bf16), dh_low)
            dvd_end = dot(b_ref[rows, :], dh_low) * wx
        cums = pltpu.roll(cum_ref[rows, :], 128 - 4 * group, 1)
        st = st_ref[rows, :]
        inside = []
        dst = jnp.zeros((BLOCK, BLOCK), f32)
        for pair in range(2):
            cols = slice(pair * 128, pair * 128 + 128)
            decays, weights = [], []
            for j in (2 * pair, 2 * pair + 1):
                spread = cumt_ref[0, j : j + 1, rows] - cums[:, j : j + 1]
                decay = jnp.exp2(jnp.minimum(spread, 0.0))
                decays.append(decay)
                weights.append((decay * st).astype(bf16))
            dyp = dy_low[:, cols]
            stack = jnp.concatenate([dyp * m_low, dyp * m_high], axis=0)
            inside.append(dot(jnp.concatenate(weights, axis=1), stack))
            cross = dot_nt(vd_low[:, cols], stack)
            dst = dst + cross[:, :128] * decays[0] + cross[:, 128:] * decays[1]
        dst_ref[rows, :] += dst
        dvd = jnp.concatenate(inside, axis=1)
        through = ex[BLOCK - 1 :]
        if more:
            dvd = dvd + dvd_end
            ends = rows8(vd * dvd_end)
            if k > 0:
                ends = ends + through * rows8(dstate * h_low.astype(f32))
        p = dy * (y_ref[rows, :] - skip * v) - vd * dvd
        if more:
            p = jnp.concatenate([p[: BLOCK - 8], p[BLOCK - 8 :] + jnp.where(iota((8, 1), 0) == 7, jnp.sum(ends, axis=0, keepdims=True), 0.0)], axis=0)
        dcum_ref[rows, :] += to_heads(p)
        ddt_ref[rows, :] += dot((dvd * v).astype(bf16), et_scr[...])
        if k > 0:
            dstate = dstate * through + dot(ct_ref[:, rows], dye)
        dconv = (dvd * dtx + skip * dy) * (sig * (1.0 + conv * (1.0 - sig)))
        window = jnp.concatenate([dconv, behind], axis=0)
        behind = dconv[:8]
        for i, term in enumerate([*[dconv * shifted[3 - i] for i in range(4)], dconv, dy * v]):
            totals[i] = totals[i] + rows8(term)
        dcin_ref[rows, :] = conv_back(
            window, mask_ref[pl.ds(t0, BLOCK + 8), :], taps, 4
        ).astype(bf16)
    rows = [jnp.sum(t, axis=0, keepdims=True) for t in totals]
    grad_ref[...] = jnp.concatenate([*rows, jnp.zeros((2, GROUP), f32)], axis=0)


def bwd(base, count, cin, y, dy, taps, pre, h):
    tokens = cin.shape[0]
    full = lambda a: whole(a.shape)
    ea, eb, cum, cumt, b, c, ct, st, mask = pre
    local = lambda rows: pl.BlockSpec((rows, GROUP), lambda g: (0, g))
    global_ = lambda rows: pl.BlockSpec((rows, GROUP), lambda g: (0, base + g))
    wide = struct((tokens, 128))
    return call(
        functools.partial(bwd_kernel, base),
        [struct((tokens, count * GROUP), bf16), struct((8, count * GROUP))] + [wide] * 5,
        grid=(count,),
        in_specs=[
            local(tokens), local(tokens), global_(tokens), global_(8),
            full(ea), full(eb), full(cum),
            pl.BlockSpec((1, 4, tokens), lambda g: (base + g, 0, 0)),
            full(b), full(c), full(ct), full(st), full(mask), local(tokens),
        ],
        out_specs=[local(tokens), local(8)] + [whole(wide.shape)] * 5,
        scratch=[
            pltpu.VMEM((tokens + 8, GROUP), f32), pltpu.VMEM((128, 3 * GROUP), bf16), pltpu.VMEM((GROUP, 128), bf16),
        ],
        name=f"bwd{base}",
        us=count * 8.4,
    )(cin, y, dy, taps, ea, eb, cum, cumt, b, c, ct, st, mask, h)


def tail_kernel(sm, cin_ref, taps_ref, head_ref, b_ref, c_ref, step_ref, mask_ref, *refs):
    dp_ref, grad_ref, stat_ref, cs_scr, ds_scr = refs[-5:]
    sums = refs[:-5]
    tokens = cin_ref.shape[0]
    cs_scr[0:8, :] = jnp.zeros((8, 256), f32)
    cs_scr[pl.ds(8, tokens), :] = cin_ref[...].astype(f32)
    ds_scr[...] = jnp.zeros(ds_scr.shape, f32)
    taps = taps_ref[...]
    grad_ref[...] = jnp.zeros(grad_ref.shape, f32)
    stat_ref[...] = jnp.zeros(stat_ref.shape, f32)
    blocks = tokens // BLOCK

    def block(step, _):
        k = blocks - 1 - step
        t0 = pl.multiple_of(k * BLOCK, BLOCK)
        rows = pl.ds(t0, BLOCK)
        row, lane = iota((BLOCK, 128), 0), iota((BLOCK, 128), 1)
        dst_sum, db_sum, dc_sum, dcum_sum, ddt_sum = [
            functools.reduce(jnp.add, [ref[rows, :] for ref in sums[i::5]]) for i in range(5)
        ]
        keep = (lane >= row) & (scene_of(lane + t0, sm) == scene_of(row + t0, sm))
        dst = jnp.where(keep, dst_sum, 0.0).astype(bf16)
        db = db_sum + dot(dst, c_ref[rows, :])
        dc = dc_sum + dot_tn(dst, b_ref[rows, :])
        conv, shifted = conv_block(cs_scr[pl.ds(t0, BLOCK + 8), :], mask_ref[rows, :], taps, 4)
        sig = sigmoid(conv)
        dconv = jnp.concatenate([db, dc], axis=1) * (sig * (1.0 + conv * (1.0 - sig)))
        window = jnp.concatenate([dconv, ds_scr[...]], axis=0)
        ds_scr[...] = dconv[:8]
        grads = [jnp.sum(rows8(dconv * shifted[3 - i]), axis=0, keepdims=True) for i in range(4)]
        grads.append(jnp.sum(rows8(dconv), axis=0, keepdims=True))
        grads.append(jnp.zeros((3, 256), f32))
        grad_ref[...] += jnp.concatenate(grads, axis=0)
        dcin = conv_back(window, mask_ref[pl.ds(t0, BLOCK + 8), :], taps, 4)
        upper = jnp.where(lane >= row, 1.0, 0.0)
        dlog = jnp.dot(upper, dcum_sum, precision=highest, preferred_element_type=f32)
        step_in = step_ref[rows, :]
        dt = jnp.maximum(step_in, 0.0) + jnp.log1p(jnp.exp(-jnp.abs(step_in)))
        rate = head_ref[1:2, :]
        dstep = (ddt_sum - dlog * rate) * sigmoid(step_in)
        dalog = -dlog * dt * rate
        stat_ref[...] += jnp.concatenate(
            [
                jnp.sum(rows8(dstep), axis=0, keepdims=True),
                jnp.sum(rows8(dalog), axis=0, keepdims=True),
                jnp.zeros((6, 128), f32),
            ],
            axis=0,
        )
        dp_ref[rows, :] = jnp.concatenate([dcin, dstep], axis=1).astype(bf16)
        return 0

    lax.fori_loop(0, blocks, block, 0, unroll=True)


def tail(sm, cin, taps, inner, head, b, c, step, mask, sums):
    tokens = cin.shape[0]
    args = (cin, taps, head, b, c, step, mask, *sums)
    outs = [struct((tokens, 384), bf16), struct((8, 256)), struct((8, 128))]
    return call(
        tail_kernel,
        outs,
        in_specs=[SMEM] + [whole(a.shape) if a is not taps else bc_taps(inner) for a in args],
        out_specs=[whole(o.shape) for o in outs],
        scratch=[pltpu.VMEM((tokens + 8, 256), f32), pltpu.VMEM((8, 256), f32)],
        name="tail",
        us=8.0,
    )(sm, *args)


def term_kernel(tiles, add, into, sm, left_ref, *refs):
    out_ref = refs[-1]
    parts = refs[: len(tiles)]

    def product(part):
        value = dot(left_ref[...], part[...])
        if add:
            value = value + refs[len(tiles)][:, : part.shape[1]].astype(f32)
        out_ref[:, : part.shape[1]] = value.astype(bf16)

    first = 0
    for part, count in zip(parts, tiles):
        step = pl.program_id(0)
        pl.when((step >= first) & (step < first + count))(functools.partial(product, part))
        first += count


def in_term(half, left, parts, name, add=None, into=None, columns=None):
    halves, width, tokens = left.shape
    n = sum(p.shape[1] for p in parts)
    wide = min(512, n)
    tiles = [pl.cdiv(p.shape[1], wide) for p in parts]
    first = [sum(tiles[:i]) for i in range(len(parts))]
    total = n if columns is None else columns
    at = 0 if into is None else (total - n) // wide
    args = [left, *parts]
    specs = [pl.BlockSpec((None, width, tokens), lambda g, sm: (sm[0], 0, 0))] + [
        pl.BlockSpec(
            (tokens, min(wide, p.shape[1])),
            functools.partial(lambda f, c, g, sm: (0, jnp.clip(g - f, 0, c - 1)), f, c),
        )
        for p, f, c in zip(parts, first, tiles)
    ]
    if add is not None:
        args.append(add)
        specs.append(pl.BlockSpec((width, wide), lambda g, sm: (0, g)))
    aliases = {}
    if into is not None:
        aliases = {len(args) + 1: 0}
        args.append(into)
        specs.append(pl.BlockSpec(memory_space=pl.ANY))
    spec = pltpu.PrefetchScalarGridSpec(
        num_scalar_prefetch=1,
        grid=(sum(tiles),),
        in_specs=specs,
        out_specs=pl.BlockSpec((width, wide), lambda g, sm: (0, at + g)),
    )
    return pl.pallas_call(
        functools.partial(term_kernel, tiles, add is not None, into is not None),
        out_shape=struct((width, total), bf16),
        grid_spec=spec,
        name=name,
        input_output_aliases=aliases,
        compiler_params=pltpu.CompilerParams(vmem_limit_bytes=VMEM_LIMIT, dimension_semantics=("arbitrary",)),
        cost_estimate=cost(width * tokens * n * 5e-9),
    )(half, *args)


def out_kernel(add, sm, left_ref, right_ref, *refs):
    value = dot(left_ref[...], right_ref[...])
    if add:
        value = value + refs[0][...].astype(f32)
    refs[-1][...] = value.astype(bf16)


def out_term(ring, half, flip, cot_low, name, add=None, columns=None):
    inner, tokens = flip.shape
    width = cot_low.shape[1]
    rows = inner // 4
    left = flip.reshape(4, rows, tokens)
    steps = 2 if ring else 4
    out = pl.BlockSpec((rows, width), (lambda g, sm: (0, g)) if ring else (lambda g, sm: (g, 0)))
    args, specs = [left, cot_low], [
        pl.BlockSpec((None, rows, tokens), lambda g, sm: (sm[0] * 2 + g, 0, 0)),
        pl.BlockSpec(cot_low.shape, lambda g, sm: (0, 0)),
    ]
    if add is not None:
        args.append(add)
        specs.append(out)
    spec = pltpu.PrefetchScalarGridSpec(num_scalar_prefetch=1, grid=(steps,), in_specs=specs, out_specs=out)
    return pl.pallas_call(
        functools.partial(out_kernel, add is not None),
        out_shape=struct((rows, columns or 2 * width) if ring else (inner, width), bf16),
        grid_spec=spec,
        name=name,
        compiler_params=pltpu.CompilerParams(vmem_limit_bytes=VMEM_LIMIT, dimension_semantics=("arbitrary",)),
        cost_estimate=cost(5.0),
    )(half, *args)


def last_kernel(count, x_ref, cot_ref, gain_ref, *refs):
    ds, ws, dx_ref = refs[:count], refs[count : 2 * count], refs[-1]
    x = x_ref[...]
    width = x.shape[1]
    dn = functools.reduce(jnp.add, [dot_nt(d[...], w[...]) for d, w in zip(ds, ws)])
    r = lax.rsqrt(jnp.mean(x * x, axis=-1, keepdims=True) + EPS)
    u = dn * gain_ref[0:1, :]
    xr = x * r
    mu = jnp.sum(u * xr, axis=-1, keepdims=True) * (1.0 / width)
    dx_ref[...] = cot_ref[...] + r * (u - xr * mu)


def last(x, cot, gain, pairs):
    tokens, width = x.shape
    row = lambda n: pl.BlockSpec((MID, n), lambda g: (g, 0))
    ds, ws = zip(*pairs)
    n = sum(k for _, k, _ in ds)
    return call(
        functools.partial(last_kernel, len(pairs)),
        struct(x.shape),
        grid=(tokens // MID,),
        in_specs=[row(width), row(width), whole(gain.shape)]
        + [pl.BlockSpec((MID, k), functools.partial(lambda i, g: (g, i), i)) for _, k, i in ds]
        + [pl.BlockSpec((width, k), functools.partial(lambda i, g: (0, i), i)) for _, k, i in ws],
        out_specs=row(width),
        name="last",
        us=18.0,
        vmem=VMEM_LARGE,
    )(x, cot, gain, *[d[0] for d in ds], *[w[0] for w in ws])


Y, CORE, X, Z1, Z2 = 1, 2, 4, 8, 16


def exchange(a, bit):
    return lax.ppermute(a, AXES, [(i, i ^ bit) for i in range(SHARDS)])


def after(a, *others):
    return lax.optimization_barrier((a, *others))[0] if others else a


def together(arrays, *others):
    return list(lax.optimization_barrier((*arrays, *others))[: len(arrays)])


def join(a, got):
    return jnp.concatenate([a, got], axis=0)


def gather_z(own):
    two = join(own, exchange(own, Z1))
    return join(two, exchange(two, Z2))


def take(a, bit, axis):
    return lax.dynamic_index_in_dim(a, bit, axis, keepdims=False)


def scatter_start(keep):
    return [Z2, Z1, X, Y], keep.reshape(2, 2, 2, 2, keep.shape[0] // 16, keep.shape[1])


def scatter_send(place, state, bit):
    names, left = state
    axis = names.index(bit)
    mine = jnp.where((place & bit) > 0, 1, 0)
    names = names[:axis] + names[axis + 1 :]
    return names, take(left, mine, axis), exchange(take(left, 1 - mine, axis), bit)


def scatter_add(sent, got=None):
    names, left, flight = sent
    left = left.astype(f32) + (flight if got is None else got).astype(f32)
    return names, left.astype(bf16) if names else left


def both(a, b):
    return (a.astype(f32) + b.astype(f32)).astype(bf16)


def pad_to(a, rows, columns):
    return jnp.pad(a, ((0, rows - a.shape[0]), (0, columns - a.shape[1])))


def local(
    ring, block_input, cotangent, scene_lengths, norm_gain, in_weight, conv_weight, conv_bias, dt_bias, a_log, skip_gain,
    gated_gain, out_weight,
):
    tokens, width = block_input.shape
    heads = a_log.shape[0]
    inner = out_weight.shape[0] * lax.axis_size(AXES)
    channels = conv_bias.shape[0] * lax.axis_size(AXES)
    proj = in_weight.shape[1]
    bc = proj - 2 * inner
    place = lax.axis_index(AXES).astype(jnp.int32)
    bounds = jnp.cumsum(scene_lengths[0]).astype(jnp.int32)
    sm = jnp.concatenate([bounds, place[None], jnp.zeros((4,), jnp.int32)])
    groups = inner // GROUP

    def pack(grads, gg, stat):
        d_skip = jnp.sum(grads[5, :inner].reshape(heads, -1), axis=1)
        side = jnp.concatenate([stat[0, :heads], stat[1, :heads], d_skip])[None]
        return jnp.concatenate([grads[:5], pad_to(jnp.sum(gg, axis=0)[None], 1, channels), pad_to(side, 2, channels)], axis=0)

    gather = lambda a: lax.all_gather(a.astype(bf16), AXES, axis=0, tiled=True)
    skip_row = jnp.repeat(skip_gain, inner // heads)[None]
    w_low = in_weight.astype(bf16)
    if ring:
        small = jnp.concatenate(
            [
                jnp.concatenate([norm_gain, gated_gain])[None],
                pad_to(conv_weight.T, 4, 96),
                pad_to(conv_bias[None], 27, 96),
            ],
            axis=0,
        )
        first = jnp.concatenate([w_low[:, 2 * inner :], small.astype(bf16)], axis=1)
        wide = inner // 2
        one, two = [
            jnp.concatenate([w_low[:, at : at + wide], w_low[:, inner + at : inner + at + wide]], axis=1)
            for at in (0, wide)
        ]
        halves = lambda a: [a[:, : a.shape[1] // 2], a[:, a.shape[1] // 2 :]]
        outward = lambda a, bits: [exchange(part, bit) for part, bit in zip(a, bits)]
        joined = lambda a, got: [join(part, came) for part, came in zip(a, got)]
        row = join(first, exchange(first, Z1))
        row, one = joined([row, one], together([exchange(row, Z2), exchange(one, Z1)]))
        two = after(two, row)
        row, one, two = joined([row, one, two], together([exchange(row, X), exchange(one, Z2), exchange(two, Z1)]))
        two_flight = exchange(two, Z2)
        one = halves(one)
        row, *one = joined([row, *one], together([exchange(row, Y), *outward(one, (X, Y))]))
        one_flights = outward(one, (Y, X))
        w_bc, taps, gain = unpack(sm, [row, exchange(row, CORE)], skip_row, channels, width)
        two = halves(join(two, together([two_flight], w_bc)[0]))
        two_flights = outward(two, (X, Y))
        x_first = after(block_input, *two)
    else:
        in_full, outside, x_first = gather(in_weight), [gather(out_weight)], block_input
        norm_full, conv_full, bias_full, gated_full = map(gather, (norm_gain, conv_weight, conv_bias, gated_gain))
        gain = jnp.broadcast_to(norm_full.astype(f32)[None], (8, width))
        w_bc = pad_to(in_full[:, 2 * inner :], width, 384)
        taps = jnp.concatenate(
            [
                conv_full.astype(f32).T,
                bias_full.astype(f32)[None],
                pad_to(jnp.concatenate([skip_row, gated_full.astype(f32)[None]], axis=0), 3, channels),
            ],
            axis=0,
        )
    head = jnp.pad(jnp.stack([dt_bias, jnp.exp(a_log)]), ((0, 6), (0, 128 - heads)))
    (normed, normt, cin_bc, b, c, bt, ct, s, st, cum, cumt, ea, eb, step, mask) = prep(
        ring, sm, x_first, gain, w_bc, taps, inner, head, heads
    )
    pre = (ea, eb, cum, cumt, c, bt, s, mask)
    def scan(base, count, offset, *w, first=(), **more):
        return fwd(base, count, offset, ring, sm, after(normed, *first), *w, inner, taps, pre, **more)

    if ring:
        half, quarter = groups // 2, groups // 4
        pairs = lambda a, got: list(zip(a, got))
        one = joined(one, together(one_flights, normed))
        out = after(out_weight, one[0]).astype(bf16)
        got = together([*outward(one, (CORE, CORE)), *two_flights, exchange(out, Z1)])
        two, out = joined(two, got[2:4]), join(out, got[4])
        got = got[:2]
        two_flights = outward(two, (Y, X))
        front = pairs(one, got)
        out_flight = exchange(out, Z2)
        near = scan(0, quarter, 0, *front, first=[out, *two])
        *got, came = together([*two_flights, out_flight], near[2])
        two, out = joined(two, got), halves(join(out, came))
        flights = outward(two, (CORE, CORE)) + outward(out, (X, Y))
        next_ = scan(quarter, quarter, quarter, *front, first=[*two, *out])
        got = together(flights, next_[2])
        back, out = pairs(two, got[:2]), joined(out, got[2:])
        flights = outward(out, (Y, X))
        far = scan(half, quarter, 0, *back, first=out, total=half)
        out = joined(out, together(flights, far[2]))
        flights = outward(out, (CORE, CORE))
        far = scan(half + quarter, quarter, quarter, *back, first=out, total=half, into=far)
        got = together(flights, far[2])
        outside = [out[0], got[0], out[1], got[1]]
        runs = [(0, quarter, near), (quarter, quarter, next_), (half, half, far)]
    else:
        runs = [(0, groups, scan(0, groups, 0, [in_full], [in_full]))]
    mixed, dz, dy, gg, flip, cot_low, *w_out = mid(
        ring, sm, cotangent, outside, inner, taps, mask, [r[0] for *_, r in runs], [r[2] for *_, r in runs]
    )
    out_full = w_out[0] if ring else outside[0]
    normt = normt.reshape(2 if ring else 1, -1, tokens)
    core = sm[3:4] >> 1 & 1
    if ring:
        sent = out_term(ring, 1 - core, flip, cot_low, "out_away")
        out_away = exchange(sent, CORE)
        sent = in_term(1 - core, normt, [after(dz, sent)], "gate_away")
        gate_away = exchange(sent, CORE)
        out_here = out_term(ring, core, flip, cot_low, "out_here", after(out_away, sent))
        gate_here = in_term(core, normt, [dz], "gate_here", after(gate_away, out_here))
        outs, gates = scatter_start(out_here), scatter_start(gate_here)
        dy = after(dy, gate_here)
    pre = (ea, eb, cum, cumt, b, c, ct, st, mask)
    scan = lambda dy, base, count, run: bwd(base, count, run[1], run[2], dy, taps, pre, run[3])
    finish = lambda sums: tail(sm, cin_bc, taps, inner, head, b, c, step, mask, sums)
    if ring:

        def term(parts, name):
            away = exchange(in_term(1 - core, normt, parts, name + "_away"), CORE)
            return scatter_start(both(in_term(core, normt, parts, name + "_here"), away))

        send = functools.partial(scatter_send, place)
        gates, outs = send(gates, X), send(outs, Y)
        back = scan(dy, *runs[2])
        one, two = together([gates[2], outs[2]], back[0])
        gates, outs = send(scatter_add(gates, one), Y), send(scatter_add(outs, two), X)
        near = scan(after(dy, gates[1], outs[1], back[0]), *runs[0])
        one, two = together([gates[2], outs[2]], near[0])
        gates, outs = scatter_add(gates, one), scatter_add(outs, two)
        early = send((gates[0], jnp.concatenate([gates[1], outs[1]], axis=-1)), Z2)
        parts = [near[0], after(back[0], early[1])]
        away = in_term(1 - core, normt, parts, "late_away")
        here = in_term(core, normt, parts, "late_here")
        late = send(scatter_start(both(here, exchange(away, CORE))), X)
        mid_out = scan(after(dy, late[1], near[0]), *runs[1])
        sums = [a for out in (back, near, mid_out) for a in out[2:]]
        (one,) = together([late[2]], mid_out[0])
        late = send(scatter_add(late, one), Y)
        sums[0] = after(sums[0], late[1])
        dbc, grad_bc, stat = finish(sums)
        grads = jnp.concatenate([near[1], mid_out[1], back[1], grad_bc], axis=1)
        one, two = together([early[2], late[2]], dbc)
        early, late = send(scatter_add(early, one), Z1), send(scatter_add(late, two), Z2)
        small = pack(grads, gg, stat)
        flight = exchange(small, CORE)
        parts = [mid_out[0], after(dbc, early[1], late[1], small)]
        away = in_term(1 - core, normt, parts, "last_away")
        here = in_term(core, normt, parts, "last_here")
        one, two, flight = together([early[2], late[2], flight], here)
        early, late, small = scatter_add(early, one), send(scatter_add(late, two), Z1), small + flight
        flight = exchange(small, X)
        final = send(scatter_start(both(here, exchange(away, CORE))), X)
        x_last = after(block_input, final[1], small, late[1])
        pairs = []
        for (base, count, run), (dv, *_) in zip(runs, (near, mid_out, back)):
            wide = count * GROUP
            pairs.append(((dz, wide, base // count), (run[4], wide, 0)))
            pairs.append(((dv, wide, 0), (run[5], wide, 0)))
        x_last = after(block_input, final[1], small, late[1])
    else:
        scatter = lambda a: lax.psum_scatter(a.astype(f32), AXES, scatter_dimension=0, tiled=True)
        dv, grad, *sums = scan(dy, *runs[0])
        dbc, grad_bc, stat = finish(sums)
        grads = jnp.concatenate([grad, grad_bc], axis=1)
        in_grad = scatter(in_term(core * 0, normt, [dz, dv, dbc], "all")[:, :proj])
        out_grad = scatter(out_term(ring, core * 0, flip, cot_low, "out"))
        pairs = [((dz, inner, 0), (in_full, inner, 0)), ((dv, inner, 0), (in_full, inner, 1))]
        x_last = block_input
    pairs.append(((dbc, 384, 0), (w_bc, 384, 0)))
    input_grad = last(x_last, cotangent, gain, pairs)
    if ring:
        one, two, flight = together([late[2], final[2], flight], input_grad)
        late, final, small = scatter_add(late, one), send(scatter_add(final, two), Y), small + flight
        flight = exchange(small, Y)
        mixed = after(mixed, final[1], small)
    block_output = branch(block_input, mixed, out_full)
    if ring:
        one, flight = together([final[2], flight], block_output)
        final, small = send(scatter_add(final, one), Z2), small + flight
        small = small + exchange(small, Z1)
        final = scatter_add(send(scatter_add(final), Z1))
        small = small + exchange(small, Z2)
        gate_grad, out_grad = early[1][:, :inner], early[1][:, inner:]
        out_grad = jnp.concatenate([out_grad[:, :width], out_grad[:, width:]], axis=0)
        near, half = inner // 4, inner // 2
        in_grad = jnp.concatenate(
            [gate_grad, late[1][:, :near], final[1][:, :near], late[1][:, near:], final[1][:, near : near + bc]], axis=1
        )
    else:
        small = lax.psum(pack(grads, gg, stat), AXES)
    d_gain = jnp.sum(in_grad * w_low.astype(f32), axis=1) / norm_gain.astype(bf16).astype(f32)
    part = lambda row, n: lax.dynamic_slice_in_dim(row, place * n, n, axis=-1)
    side = small[6]
    return (
        block_output,
        input_grad,
        d_gain,
        in_grad,
        part(small[:4], conv_bias.shape[0]).T,
        part(small[4], conv_bias.shape[0]),
        side[:heads],
        side[heads : 2 * heads],
        side[2 * heads : 3 * heads],
        part(small[5], gated_gain.shape[0]),
        out_grad,
    )


def solution(mesh):
    dp, fsdp = mesh.devices.shape
    split = jax.sharding.Mesh(mesh.devices.reshape(dp // 2, 2, fsdp), AXES)
    row = P(AXES, None)
    flat = P(AXES)
    return jax.shard_map(
        functools.partial(local, (dp, fsdp) == (16, 2)),
        mesh=split,
        in_specs=(row, row, row, flat, row, row, flat, P(), P(), P(), flat, row),
        out_specs=(row, row, flat, row, row, flat, P(), P(), P(), flat, row),
        check_vma=False,
    )
```
